32 devices in a mesh: dp: 8 (over z, x), fsdp: 4 (over y, core).
Axes of the slice: x: 2, y: 2, z: 4, core: 2. Of those that a mesh axis runs over, the one named last changes fastest.
Arguments:
- tokens: bfloat16 [4096, 17, 192], P(('dp', 'fsdp')), may hold values from -6 to 6
- out_grad: bfloat16 [4096, 17, 192], P(('dp', 'fsdp')), may hold values from -6 to 6
- flat_params: bfloat16 [2, 296960], P(None, ('dp', 'fsdp')), may hold values from -1.5 to 1.5, as said below
- feat_count: int32 [4096], P(('dp', 'fsdp')), may hold values from 1 to 16
- table_ids: int32 [4096], P(('dp', 'fsdp')), may hold values from 0 to 51
- table_counts: int32 [52], replicated, may hold values from 64 to 1024
Outputs:
- out_tokens: float32 [4096, 17, 192], P(('dp', 'fsdp'))
- in_grad: float32 [4096, 17, 192], P(('dp', 'fsdp'))
- param_grad: float32 [2, 296960], P(None, ('dp', 'fsdp'))
The draws below stay inside these ranges and needn't reach their ends.
Inputs may be any that keep to these rules, and one draw needn't show every extreme that they name: `feat_count`: slot s of a row holds a feature for 1 <= s <= the row's count. `flat_params`: the norm gains lie between 0.5 and 1.5.
All inputs are finite; a program needn't handle non-finite values.
Results may differ from the reference program's by a relative error of at most 0.013.
The reference program's roundings to bfloat16 on the way count: a program that leaves them out, or rounds other values in their place, can miss the bound.
Values may be sent and summed in bfloat16 or wider, within the bound.
No kernel may reach another device: no remote copies, remote signals or barrier semaphores. Data moves between devices by JAX's collectives and lax.ppermute only.
A program may use at most 192 MiB of HBM per device.

```python
import math
import jax
import jax.numpy as jnp
import numpy as np
from jax import lax

D = 192
HEADS = 8
HEAD_DIM = 24
FF = 256
LAYERS = 2
FEATS = 16
TABLES = 52
ROWS_DEV = 128
SEQ = 17
ROWS = 4096
PSIZE = 296960


def param_layout_drawn(model_width, hidden_units):
    return (('norm1_gain', (model_width,)), ('norm1_bias', (model_width,)), ('w_qkv', (model_width, 3 * model_width)), ('b_query', (model_width,)), ('b_value', (model_width,)), ('w_out', (model_width, model_width)), ('b_out', (model_width,)), ('norm2_gain', (model_width,)), ('norm2_bias', (model_width,)), ('w_gate_up', (model_width, 2 * hidden_units)), ('b_gate_up', (2 * hidden_units,)), ('w_down', (hidden_units, model_width)), ('b_down', (model_width,)))


def param_tables(model_width, hidden_units, padded_size):
    scales = np.full((padded_size,), 0.1, np.float32)
    gain_flags = np.zeros((padded_size,), np.float32)
    entry_scales = {'norm1_gain': 0.0, 'norm1_bias': 0.3, 'w_qkv': 1.2 / math.sqrt(model_width), 'b_query': 0.3, 'b_value': 0.3, 'w_out': 3.0 / math.sqrt(model_width), 'b_out': 0.3, 'norm2_gain': 0.0, 'norm2_bias': 0.3, 'w_gate_up': 1.0 / math.sqrt(model_width), 'b_gate_up': 0.3, 'w_down': 1.5 / math.sqrt(hidden_units), 'b_down': 0.3}
    position = 0
    for entry_name, entry_shape in param_layout_drawn(model_width, hidden_units):
        entry_size = math.prod(entry_shape)
        scales[position:position + entry_size] = entry_scales[entry_name]
        if entry_name in ('norm1_gain', 'norm2_gain'):
            gain_flags[position:position + entry_size] = 1.0
        position = position + entry_size
    return (scales, gain_flags)


def draw_flat_params(key, part):
    key = jax.random.fold_in(key, 17)
    normal_key, gain_key = jax.random.split(key)
    scales, gain_flags = param_tables(D, FF, PSIZE)
    base_draw = jnp.clip(jax.random.normal(normal_key, (LAYERS, PSIZE), jnp.float32), -4.0, 4.0)
    spread = jax.random.uniform(gain_key, (LAYERS, PSIZE), jnp.float32, 0.5, 1.5)
    values = jnp.where(jnp.asarray(gain_flags) > 0.5, spread, base_draw * jnp.asarray(scales))
    values = jnp.clip(values, -1.5, 1.5)
    return values.astype(jnp.bfloat16)


def place_ends(array, stream_key, least, top_value):
    place = [jax.random.randint(jax.random.fold_in(stream_key, axis), (), 0, length) for axis, length in enumerate(array.shape)]
    main_axis = array.shape.index(max(array.shape))
    beside = place[:main_axis] + [(place[main_axis] + 1) % array.shape[main_axis]] + place[main_axis + 1:]
    return array.at[tuple(place)].set(least).at[tuple(beside)].set(top_value)


def shard_levels(key, shape, cuts, smallest, high):
    loudness = 1.0
    for dim, shards_of in cuts:
        heights = jax.random.uniform(jax.random.fold_in(jax.random.fold_in(key, 6), dim), (shards_of,), jnp.float32, smallest / len(cuts), high / len(cuts))
        loudness = loudness * jnp.repeat(jnp.exp(heights), shape[dim] // shards_of).reshape((-1,) + (1,) * (len(shape) - 1 - dim))
    return loudness


def rank_table(count, slope):
    portions = [(1 << 20) // math.isqrt(grade ** slope) + 1 for grade in range(1, count + 1)]
    width = 1 + sum(portions) // (1 << 30)
    return np.cumsum(np.array([max(1, weight // width) for weight in portions]))


def skewed_ids(key, shape, count, lean):
    grid = rank_table(count, lean)
    lot = jax.random.randint(jax.random.fold_in(key, 1), shape, 0, int(grid[count - 1]))
    rank = jnp.searchsorted(jnp.asarray(grid, jnp.int32), lot, side="right")
    return jax.random.permutation(jax.random.fold_in(key, 2), count)[rank].astype(jnp.int32)


def scatter_about(stream_key, dims, width, reach, pieces=(), kind=jnp.bfloat16):
    entries = width * jax.random.normal(stream_key, dims, jnp.float32)
    if pieces:
        entries = entries * shard_levels(stream_key, dims, pieces, -0.22, 0.18)
    return jnp.clip(entries, -reach, reach).astype(kind)


def setup_inputs(seed: int = 0) -> dict:
    streams_of = jax.random.split(jax.random.key(seed), 7)
    tokens = scatter_about(streams_of[0], (ROWS, SEQ, D), 1.0, 6.0, ((0, 32),))
    out_grad = scatter_about(streams_of[1], (ROWS, SEQ, D), 1.0, 6.0, ((0, 32),))
    flat_params = draw_flat_params(jax.random.fold_in(streams_of[6], 71), 0)
    feat_count = place_ends(jax.random.randint(streams_of[3], (ROWS,), 1, FEATS + 1), jax.random.fold_in(streams_of[3], 1), 1, FEATS).astype(jnp.int32)
    table_ids = place_ends(skewed_ids(streams_of[4], (ROWS,), TABLES, 2), jax.random.fold_in(streams_of[4], 3), 0, TABLES - 1).astype(jnp.int32)
    table_counts = place_ends(jax.random.randint(streams_of[5], (TABLES,), 64, 1025), jax.random.fold_in(streams_of[5], 1), 64, 1024).astype(jnp.int32)
    return {"tokens": tokens, "out_grad": out_grad, "flat_params": flat_params, "feat_count": feat_count, "table_ids": table_ids, "table_counts": table_counts}


precise_mode = lax.Precision.HIGHEST
norm_epsilon = 1e-05
masked_score = -1000000000.0

@jax.custom_vjp
def low(v):
    return lax.optimization_barrier(v.astype(jnp.bfloat16)).astype(jnp.float32)

@jax.custom_vjp
def low_back(v):
    return v

def low_keep(v):
    return (low(v), None)

def low_pass(kept, grad):
    return (grad,)

def back_keep(v):
    return (v, None)

def back_low(kept, grad):
    return (low(grad),)
low.defvjp(low_keep, low_pass)
low_back.defvjp(back_keep, back_low)

def param_layout(model_width, hidden_units):
    return (('norm1_gain', (model_width,)), ('norm1_bias', (model_width,)), ('w_qkv', (model_width, 3 * model_width)), ('b_query', (model_width,)), ('b_value', (model_width,)), ('w_out', (model_width, model_width)), ('b_out', (model_width,)), ('norm2_gain', (model_width,)), ('norm2_bias', (model_width,)), ('w_gate_up', (model_width, 2 * hidden_units)), ('b_gate_up', (2 * hidden_units,)), ('w_down', (hidden_units, model_width)), ('b_down', (model_width,)))

def unpack_params(layer_flat, model_width, hidden_units):
    params = {}
    position = 0
    for entry_name, entry_shape in param_layout(model_width, hidden_units):
        entry_size = math.prod(entry_shape)
        params[entry_name] = layer_flat[position:position + entry_size].reshape(entry_shape)
        position = position + entry_size
    return params

def layer_norm(values, norm_gain, norm_bias):
    centre = values - lax.optimization_barrier(jnp.mean(values, axis=-1, keepdims=True))
    variance = lax.optimization_barrier(jnp.mean(centre * centre, axis=-1, keepdims=True))
    return centre * lax.rsqrt(variance + norm_epsilon) * norm_gain + norm_bias

def layer_forward(inputs, params, valid_slots):
    batch_rows, slot_count, model_width = inputs.shape
    score_scale = 1.0 / math.sqrt(HEAD_DIM)
    head_shape = (batch_rows, slot_count, HEADS, HEAD_DIM)
    normed = low(layer_norm(inputs, params['norm1_gain'], params['norm1_bias']))
    projected = jnp.einsum('rsd,de->rse', normed, params['w_qkv'], precision=precise_mode)
    queries = low(low_back(projected[..., :model_width] + params['b_query']))
    key_part = low(low_back(projected[..., model_width:2 * model_width]))
    value_part = low(low_back(projected[..., 2 * model_width:] + params['b_value']))
    query_heads = queries.reshape(head_shape)
    key_heads = key_part.reshape(head_shape)
    value_heads = value_part.reshape(head_shape)
    scores = low_back(jnp.einsum('rqhd,rkhd->rhqk', query_heads, key_heads, precision=precise_mode) * score_scale)
    scores = jnp.where(valid_slots[:, None, None, :], scores, masked_score)
    largest = lax.optimization_barrier(jnp.max(scores, axis=-1, keepdims=True))
    weights_exp = jnp.exp(scores - largest)
    attention = low(weights_exp / lax.optimization_barrier(jnp.sum(weights_exp, axis=-1, keepdims=True)))
    mixed_heads = jnp.einsum('rhqk,rkhd->rqhd', attention, value_heads, precision=precise_mode)
    mixed_heads = low(low_back(mixed_heads.reshape(batch_rows, slot_count, model_width)))
    attended = low_back(jnp.einsum('rsd,de->rse', mixed_heads, params['w_out'], precision=precise_mode) + params['b_out'])
    middle = inputs + attended
    normed_two = low(layer_norm(middle, params['norm2_gain'], params['norm2_bias']))
    gate_up = low_back(jnp.einsum('rsd,de->rse', normed_two, params['w_gate_up'], precision=precise_mode) + params['b_gate_up'])
    hidden_act = low(jax.nn.gelu(gate_up[..., :FF], approximate=False) * gate_up[..., FF:])
    branch = low_back(jnp.einsum('rsf,fd->rsd', hidden_act, params['w_down'], precision=precise_mode) + params['b_down'])
    return middle + branch

def reference(tokens, out_grad, flat_params, feat_count, table_ids, table_counts):
    rows_total = tokens.shape[0]
    row_block = ROWS_DEV
    block_count = rows_total // row_block
    params_float = flat_params.astype(jnp.float32)
    counts_float = table_counts.astype(jnp.float32)
    mean_count = jnp.mean(counts_float)
    slot_index = jnp.arange(SEQ, dtype=jnp.int32)
    table_index = jnp.arange(TABLES, dtype=jnp.int32)

    def one_block(gradient_total, block_index):
        start = (block_index * row_block).astype(jnp.int32)
        block_tokens = lax.dynamic_slice_in_dim(tokens, start, row_block, 0).astype(jnp.float32)
        block_cot = lax.dynamic_slice_in_dim(out_grad, start, row_block, 0).astype(jnp.float32)
        block_counts = lax.dynamic_slice_in_dim(feat_count, start, row_block, 0)
        block_tables = lax.dynamic_slice_in_dim(table_ids, start, row_block, 0)
        valid_slots = slot_index[None, :] <= block_counts[:, None]
        table_match = (block_tables[:, None] == table_index[None, :]).astype(jnp.float32)
        row_count = lax.optimization_barrier(jnp.sum(table_match * counts_float[None, :], axis=1))
        row_scale = jnp.sqrt(mean_count / row_count)
        seed_grad = block_cot * row_scale[:, None, None] * valid_slots[:, :, None].astype(jnp.float32)

        def stack_forward(inputs, flat_all):
            current = inputs
            for layer_index in range(LAYERS):
                current = layer_forward(current, unpack_params(flat_all[layer_index], D, FF), valid_slots)
            return current
        result, pull_back = jax.vjp(stack_forward, block_tokens, params_float)
        input_grad, flat_grad = pull_back(seed_grad)
        return (gradient_total + flat_grad, (result, input_grad))
    start_total = jnp.zeros((LAYERS, PSIZE), jnp.float32)
    gradient_total, (results, input_grads) = lax.scan(one_block, start_total, jnp.arange(block_count, dtype=jnp.int32))
    return (results.reshape(tokens.shape), input_grads.reshape(tokens.shape), gradient_total)
```

```python
import math

import jax
import jax.numpy as jnp
from jax import lax
from jax.experimental import pallas as pl
from jax.experimental.pallas import tpu as pltpu
from jax.sharding import PartitionSpec as P

D = 192
FF = 256
HEADS = 8
HEAD_DIM = 24
SEQ = 17
LAYERS = 2
PSIZE = 296960
ROWS = 128
SLOTS = 18
LANES = 128
GROUP = 8
GROUPS = ROWS // GROUP
GT = SLOTS * GROUP
QL = HEADS * GT
TOKENS = SLOTS * ROWS
CHUNK = 2 * ROWS
CHUNKS = TOKENS // CHUNK
FLAT = PSIZE // LANES
PARTS = 32
BLOCK = 80
EPS = 1e-05
SCALE = 1.0 / math.sqrt(HEAD_DIM)
F32 = jnp.float32
BF16 = jnp.bfloat16


def dot(a, b, ca, cb):
    return lax.dot_general(a, b, (((ca,), (cb,)), ((), ())), preferred_element_type=F32)


def lane_half(shape):
    return lax.broadcasted_iota(jnp.int32, shape, len(shape) - 1) < 64


def swap(x):
    return pltpu.roll(x, 64, x.ndim - 1)


def low_half(x):
    return jnp.where(lane_half(x.shape), x, 0.0)


def splice(a, b):
    return jnp.where(lane_half(a.shape), swap(a), swap(b))


def after(a, b):
    return jnp.where(lane_half(a.shape), a, swap(b))


def wide(column):
    return jnp.concatenate([column, column], axis=1)


def gather_flat(blocks, layer, flat):
    for pair in range(blocks.shape[0] // 2):
        base = 145 * pair
        first = blocks[2 * pair, layer].astype(F32)
        second = blocks[2 * pair + 1, layer].astype(F32)
        flat[pl.ds(base, BLOCK), :] = first
        flat[pl.ds(base + 72, BLOCK), :] = second
        flat[pl.ds(base + 72, 1), :] = jnp.where(
            lane_half((1, LANES)), first[72:73], second[0:1]
        )


def column_of(row):
    return jnp.transpose(jnp.broadcast_to(row, (LANES, 2 * LANES)))[0:D]


def unpack(flat, w, tmp):
    def rows(start, count, stride):
        return flat[pl.ds(start, count, stride=stride), :]

    def row(index):
        return flat[pl.ds(index, 1), :]

    def pair_row(a, b):
        return jnp.concatenate([a, b], axis=1)

    w["cols"][0] = column_of(pair_row(row(0), low_half(row(1))))
    w["cols"][1] = column_of(pair_row(splice(row(1), row(2)), low_half(swap(row(2)))))
    w["cols"][2] = column_of(pair_row(row(1158), low_half(row(1159))))
    w["cols"][3] = column_of(pair_row(splice(row(1159), row(1160)), low_half(swap(row(1160)))))
    w["cols"][4] = column_of(pair_row(row(1161), low_half(row(1162))))
    w["cols"][5] = column_of(pair_row(splice(row(2318), row(2319)), low_half(swap(row(2319)))))

    e = [rows(3 + j, 96, 9) for j in range(9)]
    even = (e[0], low_half(e[1]), splice(e[1], e[2]), low_half(swap(e[2])), e[3], low_half(e[4]))
    odd = (
        splice(e[4], e[5]),
        low_half(swap(e[5])),
        e[6],
        low_half(e[7]),
        splice(e[7], e[8]),
        low_half(swap(e[8])),
    )
    zero_row = jnp.zeros((1, LANES), F32)
    bias = (
        row(867),
        low_half(row(868)),
        zero_row,
        zero_row,
        splice(row(868), row(869)),
        low_half(swap(row(869))),
    )
    first_row = lax.broadcasted_iota(jnp.int32, (16, LANES), 0) == 0
    for j in range(6):
        tmp[j, pl.ds(0, 96, stride=2), :] = even[j]
        tmp[j, pl.ds(1, 96, stride=2), :] = odd[j]
        w["qkv"][0:D, j * LANES : (j + 1) * LANES] = tmp[j, 0:D, :].astype(BF16)
        w["qkv"][D : D + 16, j * LANES : (j + 1) * LANES] = jnp.where(
            first_row, jnp.broadcast_to(bias[j], (16, LANES)), 0.0
        ).astype(BF16)

    e = [rows(870 + j, 96, 3) for j in range(3)]
    tmp[0, pl.ds(0, 96, stride=2), :] = e[0]
    tmp[1, pl.ds(0, 96, stride=2), :] = low_half(e[1])
    tmp[0, pl.ds(1, 96, stride=2), :] = splice(e[1], e[2])
    tmp[1, pl.ds(1, 96, stride=2), :] = low_half(swap(e[2]))
    w_out = jnp.concatenate([tmp[0, 0:D, :], tmp[1, 0:D, :]], axis=1)
    w["out_t"][...] = jnp.transpose(w_out)[0:D].astype(BF16)

    g = [rows(1162 + j, 192, 4) for j in range(5)]
    tiles = [splice(g[j], g[j + 1]) for j in range(4)]
    gate_up = jnp.concatenate(tiles, axis=1)
    w["gu"][...] = gate_up.astype(BF16)
    bias_row = jnp.concatenate(
        [splice(row(1930 + j), row(1931 + j)) for j in range(4)], axis=1
    )
    bias_rows = jnp.where(
        lax.broadcasted_iota(jnp.int32, (64, 2 * FF), 0) == 0,
        jnp.broadcast_to(bias_row, (64, 2 * FF)),
        0.0,
    )
    w["gu_t"][...] = jnp.transpose(jnp.concatenate([gate_up, bias_rows], axis=0))[
        :, 0 : D + 16
    ].astype(BF16)

    e = [rows(1934 + j, 128, 3) for j in range(4)]
    tmp[0, pl.ds(0, 128, stride=2), :] = splice(e[0], e[1])
    tmp[1, pl.ds(0, 128, stride=2), :] = low_half(swap(e[1]))
    tmp[0, pl.ds(1, 128, stride=2), :] = e[2]
    tmp[1, pl.ds(1, 128, stride=2), :] = low_half(e[3])
    w_down = jnp.concatenate([tmp[0, 0:FF, :], tmp[1, 0:FF, :]], axis=1)
    w["down"][...] = w_down[:, 0:D].astype(BF16)
    w["down_t"][...] = jnp.transpose(w_down)[0:D].astype(BF16)


def row_of(columns):
    turned = jnp.sum(jnp.transpose(columns), axis=0, keepdims=True)
    return turned[:, 0:LANES], jnp.concatenate(
        [turned[:, LANES:D], jnp.zeros((1, LANES - (D - LANES)), F32)], axis=1
    )


def pack(flat, acc, sums, tmp):
    def put(start, count, stride, value):
        flat[pl.ds(start, count, stride=stride), :] = value

    def put_row(index, value):
        flat[pl.ds(index, 1), :] = value

    def down(j, start, count, stride):
        return acc["down"][j, pl.ds(start, count, stride=stride), :]

    g1 = row_of(sums[0])
    b1 = row_of(sums[1])
    g2 = row_of(sums[2])
    b2 = row_of(sums[3])
    bo = row_of(sums[4])
    put_row(0, g1[0])
    put_row(1, after(g1[1], b1[0]))
    put_row(2, splice(b1[0], b1[1]))

    even = [acc["qkv"][j, pl.ds(0, 96, stride=2), :] for j in range(6)]
    odd = [acc["qkv"][j, pl.ds(1, 96, stride=2), :] for j in range(6)]
    put(3, 96, 9, even[0])
    put(4, 96, 9, after(even[1], even[2]))
    put(5, 96, 9, splice(even[2], even[3]))
    put(6, 96, 9, even[4])
    put(7, 96, 9, after(even[5], odd[0]))
    put(8, 96, 9, splice(odd[0], odd[1]))
    put(9, 96, 9, odd[2])
    put(10, 96, 9, after(odd[3], odd[4]))
    put(11, 96, 9, splice(odd[4], odd[5]))
    bias = [acc["qkv"][j, D : D + 1, :] for j in range(6)]
    put_row(867, bias[0])
    put_row(868, after(bias[1], bias[4]))
    put_row(869, splice(bias[4], bias[5]))

    w_out = jnp.transpose(
        jnp.concatenate([acc["out_t"][...], jnp.zeros((64, D), F32)], axis=0)
    )
    tmp[0, 0:D, :] = w_out[:, 0:LANES]
    tmp[1, 0:D, :] = w_out[:, LANES:]
    even = [tmp[j, pl.ds(0, 96, stride=2), :] for j in range(2)]
    odd = [tmp[j, pl.ds(1, 96, stride=2), :] for j in range(2)]
    put(870, 96, 3, even[0])
    put(871, 96, 3, after(even[1], odd[0]))
    put(872, 96, 3, splice(odd[0], odd[1]))
    put_row(1158, bo[0])
    put_row(1159, after(bo[1], g2[0]))
    put_row(1160, splice(g2[0], g2[1]))
    put_row(1161, b2[0])

    gu = [acc["gu"][j, 0 : D + 8, :] for j in range(4)]
    put_row(1162, after(b2[1], gu[0][0:1]))
    put(1166, 192, 4, splice(gu[3][0:192], acc["gu"][0, pl.ds(1, 192), :]))
    for j in range(1, 4):
        joined = splice(gu[j - 1], gu[j])
        put(1162 + j, 192, 4, joined[0:192])
        put_row(1930 + j, joined[192:193])
    put_row(1934, splice(gu[3][192:193], acc["down"][0, 0:1, :]))

    w0e, w1e = down(0, 0, 128, 2), down(1, 0, 128, 2)
    w0o, w1o = down(0, 1, 128, 2), down(1, 1, 128, 2)
    put(1935, 128, 3, splice(w0e, w1e))
    put(1936, 128, 3, w0o)
    put(1937, 128, 3, after(w1o, down(0, 2, 128, 2)))
    put_row(2319, splice(acc["down"][0, FF : FF + 1, :], acc["down"][1, FF : FF + 1, :]))


def scatter_blocks(flat, layer, blocks):
    for part in range(blocks.shape[0]):
        start = (145 * part) // 2
        blocks[part, layer] = flat[pl.ds(start, BLOCK), :].astype(BF16)


def norm(x, gain, bias):
    centre = x - jnp.sum(x, axis=0, keepdims=True) * (1.0 / D)
    variance = jnp.sum(centre * centre, axis=0, keepdims=True) * (1.0 / D)
    rstd = lax.rsqrt(variance + EPS)
    xhat = centre * rstd
    return xhat, rstd, (xhat * gain + bias).astype(BF16)


def norm_back(grad, xhat, rstd, gain):
    e = gain * grad
    mean_e = jnp.sum(e, axis=0, keepdims=True) * (1.0 / D)
    mean_ex = jnp.sum(e * xhat, axis=0, keepdims=True) * (1.0 / D)
    return rstd * (e - mean_e - xhat * mean_ex)


def fold(x):
    return x[:, 0:LANES] + x[:, LANES:]


def gelu_parts(gate):
    z = jnp.abs(gate) * (1.0 / math.sqrt(2.0))
    t = 1.0 / (1.0 + 0.3275911 * z)
    ex = jnp.exp(-z * z)
    poly = t * (
        0.254829592
        + t * (-0.284496736 + t * (1.421413741 + t * (-1.453152027 + t * 1.061405429)))
    )
    tail = 0.5 * poly * ex
    cdf = jnp.where(gate < 0.0, tail, 1.0 - tail)
    return cdf, cdf + gate * (ex * (1.0 / math.sqrt(2.0 * math.pi)))


def to_groups(x):
    n = x.shape[-1]
    x = x.reshape(2, GROUPS, GROUP, n)
    return jnp.concatenate([x[0][:, None], x[1][:, None]], axis=1).reshape(
        GROUPS, 2 * GROUP, n
    )


def from_groups(x):
    n = x.shape[-1]
    x = x.reshape(GROUPS, 2, GROUP, n)
    return jnp.concatenate([x[:, 0], x[:, 1]], axis=0).reshape(CHUNK, n)


def lanes_of(c):
    return pl.ds(pl.multiple_of(c * CHUNK, CHUNK), CHUNK)


def group_rows(c):
    return pl.ds(pl.multiple_of(c * 2 * GROUP, 2 * GROUP), 2 * GROUP)


def forward_qkv(s, w):
    gain, bias = wide(w["cols"][0]), wide(w["cols"][1])

    def step(c, carry):
        lanes = lanes_of(c)
        xhat, rstd, normed = norm(s["x"][:, lanes], gain, bias)
        s["xhat1"][:, lanes] = xhat
        s["rstd1"][:, lanes] = rstd
        s["h1"][0:D, lanes] = normed
        qkv = dot(s["h1"][:, lanes], w["qkv"][...], 0, 0)
        place = group_rows(c)
        s["q"][:, place, :] = to_groups(qkv[:, 0:D]).astype(BF16)
        for name, start in (("k", 256), ("v", 512)):
            part = qkv[:, start : start + D].reshape(2, GROUPS, GROUP, D)
            turned = jnp.concatenate(
                [
                    pltpu.roll(part[t], lax.rem(2 * c + t, GROUP), 1)[:, None]
                    for t in range(2)
                ],
                axis=1,
            )
            s[name][:, place, :] = turned.reshape(GROUPS, 2 * GROUP, D).astype(BF16)
        return carry

    lax.fori_loop(0, CHUNKS, step, 0)


def spread(values, masks):
    n = values.shape[1]
    doubled = [
        jnp.concatenate([values[8 * a : 8 * a + 8], values[8 * a : 8 * a + 8]], axis=0).astype(BF16)
        for a in range(3)
    ]
    parts = [doubled[a] * masks[m][:, 0:n] for a in range(2) for m in range(4)]
    parts.append(doubled[2] * masks[4][:, 0:n])
    return jnp.concatenate(parts, axis=0)


def collect(scores, diff):
    out = []
    for a in range(2):
        kept = scores[64 * a : 64 * a + 8]
        for j in range(1, 8):
            kept = jnp.where(diff == j, scores[64 * a + 8 * j : 64 * a + 8 * j + 8], kept)
        out.append(kept)
    out.append(scores[128:136])
    return out


def expand(rows, heads, out):
    for h in range(HEADS):
        out[h * LANES : (h + 1) * LANES, :] = rows[0:LANES] * heads[h, 0:1, :]
        out[HEADS * LANES + 16 * h : HEADS * LANES + 16 * h + 16, :] = (
            rows[LANES:GT] * heads[h, 0:1, :]
        )


def heads_joined(tiles):
    main = []
    for h in range(HEADS):
        tile = tiles[h // 2]
        start = (h % 2) * LANES
        main.append(tile[h * HEAD_DIM : (h + 1) * HEAD_DIM, start : start + LANES])
    main = jnp.concatenate(main, axis=0)
    last = tiles[4]
    head_of_row = lax.broadcasted_iota(jnp.int32, last.shape, 0) // HEAD_DIM
    head_of_lane = lax.broadcasted_iota(jnp.int32, last.shape, 1) // 16
    last = jnp.where(head_of_row == head_of_lane, last, 0.0)
    pad = jnp.zeros((64, LANES), F32)
    main = jnp.transpose(jnp.concatenate([main, pad], axis=0))[:, 0:D]
    last = jnp.transpose(jnp.concatenate([last, pad], axis=0))[:, 0:D]
    last = jnp.sum(last.reshape(HEADS, 16, D), axis=0)
    return main, last


TILES = ((0, 256), (256, 256), (512, 256), (768, 256), (1024, 128))


def forward_attention(s, env):
    diff = env["diff"][...]

    def step(g, carry):
        expand(s["q"][g], env["heads"], env["qx"])
        keys, values = s["k"][g], s["v"][g]
        count = env["count"][pl.ds(g, 1), :]
        tiles = []
        for start, n in TILES:
            scores = dot(keys, env["qx"][start : start + n, :], 1, 1)
            own = diff[:, 0:n]
            kept = collect(scores, own)
            limit = count[:, 0:n]
            slot = own.astype(F32)
            shown = [
                jnp.where(slot <= limit, kept[0] * SCALE, -1e9),
                jnp.where(slot + 8.0 <= limit, kept[1] * SCALE, -1e9),
                jnp.where(
                    own == 0, jnp.where(limit >= 16.0, kept[2] * SCALE, -1e9), -3e38
                ),
            ]
            top = jnp.max(
                jnp.maximum(jnp.maximum(shown[0], shown[1]), shown[2]), axis=0, keepdims=True
            )
            shown = [jnp.exp(part - top) for part in shown]
            total = jnp.sum(shown[0] + shown[1] + shown[2], axis=0, keepdims=True)
            inverse = 1.0 / total
            attention = jnp.concatenate([part * inverse for part in shown], axis=0)
            s["att"][g, :, start : start + n] = attention
            tiles.append(dot(values, spread(attention, env["masks"]), 0, 0))
        main, last = heads_joined(tiles)
        s["mixed"][g, 0:LANES, :] = main.astype(BF16)
        s["mixed"][g, LANES:GT, :] = last.astype(BF16)
        return carry

    lax.fori_loop(0, GROUPS, step, 0)


def forward_rest(s, w, done):
    gain, bias = wide(w["cols"][3]), wide(w["cols"][4])
    bias_out, bias_down = wide(w["cols"][2]), wide(w["cols"][5])

    def step(c, carry):
        lanes = lanes_of(c)
        mixed = from_groups(s["mixed"][:, group_rows(c), :].astype(F32)).astype(BF16)
        middle = s["x"][:, lanes] + (dot(w["out_t"][...], mixed, 1, 1) + bias_out)
        xhat, rstd, normed = norm(middle, gain, bias)
        s["xhat2"][:, lanes] = xhat
        s["rstd2"][:, lanes] = rstd
        s["h2"][0:D, lanes] = normed
        gate_up = dot(w["gu_t"][...], s["h2"][:, lanes], 1, 0)
        gate, up = gate_up[0:FF], gate_up[FF:]
        cdf, slope = gelu_parts(gate)
        gelu = gate * cdf
        act = (gelu * up).astype(BF16)
        s["act"][0:FF, lanes] = act
        s["gelu"][:, lanes] = gelu
        s["slope"][:, lanes] = slope * up
        result = middle + (dot(w["down_t"][...], act, 1, 0) + bias_down)
        done(c, lanes, result)
        return carry

    lax.fori_loop(0, CHUNKS, step, 0)


def add_tiles(ref, value):
    for j in range(ref.shape[0]):
        ref[j] += value[:, j * LANES : (j + 1) * LANES]


def add_narrow(ref, value):
    ref[0] += value[:, 0:LANES]
    ref[1, :, 0 : D - LANES] += value[:, LANES:D]


def backward_rest(s, w, acc, sums):
    gain = wide(w["cols"][3])

    def step(c, carry):
        lanes = lanes_of(c)
        grad = s["g"][:, lanes]
        branch = grad.astype(BF16)
        add_narrow(acc["down"], dot(s["act"][:, lanes], branch, 1, 1))
        d_act = dot(w["down"][...], branch, 1, 0)
        d_gate_up = jnp.concatenate(
            [d_act * s["slope"][:, lanes], d_act * s["gelu"][:, lanes]], axis=0
        ).astype(BF16)
        add_tiles(acc["gu"], dot(s["h2"][:, lanes], d_gate_up, 1, 1))
        d_normed = dot(w["gu"][...], d_gate_up, 1, 0)
        xhat = s["xhat2"][:, lanes]
        sums[2] += fold(d_normed * xhat)
        sums[3] += fold(d_normed)
        d_middle = grad + norm_back(d_normed, xhat, s["rstd2"][:, lanes], gain)
        s["g"][:, lanes] = d_middle
        d_attended = d_middle.astype(BF16)
        sums[4] += fold(d_attended.astype(F32))
        place = group_rows(c)
        s["dm"][:, place, :] = to_groups(dot(d_attended, w["out_t"][...], 0, 0)).astype(BF16)
        mixed = from_groups(s["mixed"][:, place, :].astype(F32)).astype(BF16)
        acc["out_t"][...] += dot(d_attended, mixed, 1, 0)
        return carry

    lax.fori_loop(0, CHUNKS, step, 0)


def backward_attention(s, env):
    diff = env["diff"][...]

    def step(g, carry):
        expand(s["q"][g], env["heads"], env["qx"])
        expand(s["dm"][g], env["heads"], env["dx"])
        keys, values = s["k"][g], s["v"][g]
        tiles = []
        d_values = jnp.zeros((GT, D), F32)
        d_keys = jnp.zeros((GT, D), F32)
        for start, n in TILES:
            d_mixed = env["dx"][start : start + n, :]
            kept = jnp.concatenate(collect(dot(values, d_mixed, 1, 1), diff[:, 0:n]), axis=0)
            attention = s["att"][g, :, start : start + n]
            weighted = attention * kept
            total = jnp.sum(weighted, axis=0, keepdims=True)
            d_score = spread(weighted - attention * total, env["masks"])
            d_values += dot(spread(attention, env["masks"]), d_mixed, 1, 0)
            d_keys += dot(d_score, env["qx"][start : start + n, :], 1, 0)
            tiles.append(dot(keys, d_score, 0, 0))
        main, last = heads_joined(tiles)
        s["dqkv"][g, 0:LANES, 0:D] = (main * SCALE).astype(BF16)
        s["dqkv"][g, LANES:GT, 0:D] = (last * SCALE).astype(BF16)
        for value, start, scale in ((d_keys, 256, SCALE), (d_values, 512, 1.0)):
            slots = value.reshape(SLOTS, GROUP, D)
            turned = [
                slots[k] if k % GROUP == 0 else pltpu.roll(slots[k], GROUP - k % GROUP, 0)
                for k in range(SLOTS)
            ]
            s["dqkv"][g, :, start : start + D] = (jnp.concatenate(turned, axis=0) * scale).astype(
                BF16
            )
        return carry

    lax.fori_loop(0, GROUPS, step, 0)


def backward_qkv(s, w, acc, sums, done):
    gain = wide(w["cols"][0])

    def step(c, carry):
        lanes = lanes_of(c)
        d_qkv = from_groups(s["dqkv"][:, group_rows(c), :].astype(F32)).astype(BF16)
        add_tiles(acc["qkv"], dot(s["h1"][:, lanes], d_qkv, 1, 0))
        d_normed = dot(w["qkv"][0:D, :], d_qkv, 1, 1)
        xhat = s["xhat1"][:, lanes]
        sums[0] += fold(d_normed * xhat)
        sums[1] += fold(d_normed)
        done(
            c, lanes, s["g"][:, lanes] + norm_back(d_normed, xhat, s["rstd1"][:, lanes], gain)
        )
        return carry

    lax.fori_loop(0, CHUNKS, step, 0)


def per_layer():
    return {
        "x": ((D, TOKENS), F32),
        "xhat1": ((D, TOKENS), F32),
        "rstd1": ((1, TOKENS), F32),
        "h1": ((D + 16, TOKENS), BF16),
        "q": ((GROUPS, GT, D), BF16),
        "k": ((GROUPS, GT, D), BF16),
        "v": ((GROUPS, GT, D), BF16),
        "att": ((GROUPS, 24, QL), F32),
        "mixed": ((GROUPS, GT, D), BF16),
        "xhat2": ((D, TOKENS), F32),
        "rstd2": ((1, TOKENS), F32),
        "h2": ((D + 16, TOKENS), BF16),
        "act": ((FF + 16, TOKENS), BF16),
        "gelu": ((FF, TOKENS), F32),
        "slope": ((FF, TOKENS), F32),
    }


def weights():
    return {
        "cols": ((6, D, LANES), F32),
        "qkv": ((D + 16, 6 * LANES), BF16),
        "out_t": ((D, D), BF16),
        "gu": ((D, 2 * FF), BF16),
        "gu_t": ((2 * FF, D + 16), BF16),
        "down": ((FF, D), BF16),
        "down_t": ((D, FF), BF16),
    }


def accumulators():
    return {
        "qkv": ((6, D + 16, LANES), F32),
        "out_t": ((D, D), F32),
        "gu": ((4, D + 16, LANES), F32),
        "down": ((2, FF + 16, LANES), F32),
    }


def common():
    return {
        "qx": ((QL, D), BF16),
        "dx": ((QL, D), BF16),
        "heads": ((HEADS, 16, D), BF16),
        "masks": ((5, 16, CHUNK), BF16),
        "diff": ((GROUP, CHUNK), jnp.int32),
        "count": ((GROUPS, CHUNK), F32),
        "dm": ((GROUPS, GT, D), BF16),
        "dqkv": ((GROUPS, GT, 6 * LANES), BF16),
        "g": ((D, TOKENS), F32),
        "sums": ((5, D, LANES), F32),
        "flat": ((FLAT + 8, LANES), F32),
        "tmp": ((6, FF, LANES), F32),
    }


def make_scratch():
    shapes, names = [], []
    for prefix, table in (
        ("common", common()),
        ("acc", accumulators()),
        ("s0", per_layer()),
        ("s1", per_layer()),
        ("w0", weights()),
        ("w1", weights()),
    ):
        for name, (shape, kind) in table.items():
            names.append((prefix, name))
            shapes.append(pltpu.VMEM(shape, kind))
    return names, shapes


def init_env(env, count):
    lane = lax.broadcasted_iota(jnp.int32, (GROUP, CHUNK), 1)
    sub = lax.broadcasted_iota(jnp.int32, (GROUP, CHUNK), 0)
    diff = (sub - lane) & (GROUP - 1)
    env["diff"][...] = diff
    for m in range(5):
        first = jnp.where(diff == (2 * m) % 8, 1.0, 0.0)
        second = jnp.where(diff == 2 * m + 1, 1.0, 0.0)
        env["masks"][m] = jnp.concatenate([first, second], axis=0).astype(BF16)
    feature = lax.broadcasted_iota(jnp.int32, (16, D), 1) // HEAD_DIM
    for h in range(HEADS):
        env["heads"][h] = jnp.where(feature == h, 1.0, 0.0).astype(BF16)
    row = lax.broadcasted_iota(jnp.int32, (GROUPS, LANES), 1)
    group = lax.broadcasted_iota(jnp.int32, (GROUPS, LANES), 0)
    mine = jnp.where(row // GROUP == group, jnp.broadcast_to(count, (GROUPS, LANES)), 0.0)
    here = lax.broadcasted_iota(jnp.int32, (LANES, CHUNK), 0)
    there = lax.broadcasted_iota(jnp.int32, (LANES, CHUNK), 1)
    pick = jnp.where(here % GROUP == there % GROUP, 1.0, 0.0).astype(BF16)
    env["count"][...] = dot(mine.astype(BF16), pick, 1, 0)


def ones_below(ref, rows):
    tail = ref.shape[0] - rows
    mark = lax.broadcasted_iota(jnp.int32, (tail, ref.shape[1]), 0) == 0
    ref[rows:, :] = jnp.where(mark, 1.0, 0.0).astype(BF16)


def kernel(names, tokens, out_grad, blocks, row_scale, count, out, in_grad, grads, *scratch):
    table = {}
    for (prefix, name), ref in zip(names, scratch):
        table.setdefault(prefix, {})[name] = ref
    env, acc = table["common"], table["acc"]
    s, w = [table["s0"], table["s1"]], [table["w0"], table["w1"]]
    sums = env["sums"]

    init_env(env, count[...])
    valid_slots = count[...]
    env["dqkv"][...] = jnp.zeros_like(env["dqkv"])
    for layer in range(LAYERS):
        ones_below(s[layer]["h1"], D)
        ones_below(s[layer]["h2"], D)
        ones_below(s[layer]["act"], FF)
        gather_flat(blocks, layer, env["flat"])
        unpack(env["flat"], w[layer], env["tmp"])
    for slot in range(SLOTS):
        lanes = slice(slot * ROWS, (slot + 1) * ROWS)
        if slot < SEQ:
            s[0]["x"][:, lanes] = tokens[slot].astype(F32)
            keep = jnp.where(valid_slots >= float(slot), row_scale[...], 0.0)
            env["g"][:, lanes] = out_grad[slot].astype(F32) * keep
        else:
            s[0]["x"][:, lanes] = jnp.zeros((D, ROWS), F32)
            env["g"][:, lanes] = jnp.zeros((D, ROWS), F32)

    def put(target):
        def done(c, lanes, value):
            target[2 * c] = value[:, 0:ROWS]

            @pl.when(c < CHUNKS - 1)
            def _():
                target[2 * c + 1] = value[:, ROWS:]

        return done

    def keep(target):
        def done(c, lanes, value):
            target[:, lanes] = value

        return done

    for layer in range(LAYERS):
        forward_qkv(s[layer], w[layer])
        forward_attention(s[layer], env)
        last = layer == LAYERS - 1
        forward_rest(s[layer], w[layer], put(out) if last else keep(s[layer + 1]["x"]))
    for layer in reversed(range(LAYERS)):
        sums[...] = jnp.zeros_like(sums)
        for ref in acc.values():
            ref[...] = jnp.zeros_like(ref)
        state = dict(s[layer], g=env["g"], dm=env["dm"], dqkv=env["dqkv"])
        backward_rest(state, w[layer], acc, sums)
        backward_attention(state, env)
        backward_qkv(
            state, w[layer], acc, sums, put(in_grad) if layer == 0 else keep(env["g"])
        )
        pack(env["flat"], acc, sums, env["tmp"])
        scatter_blocks(env["flat"], layer, grads)


def run_kernel(tokens, out_grad, blocks, row_scale, count):
    names, scratch = make_scratch()
    full = jax.ShapeDtypeStruct((SEQ, D, ROWS), F32)

    def body(*refs):
        kernel(names, *refs)

    return pl.pallas_call(
        body,
        out_shape=(full, full, jax.ShapeDtypeStruct(blocks.shape, BF16)),
        in_specs=[pl.BlockSpec(memory_space=pltpu.VMEM)] * 5,
        out_specs=[pl.BlockSpec(memory_space=pltpu.VMEM)] * 3,
        scratch_shapes=scratch,
        compiler_params=pltpu.CompilerParams(vmem_limit_bytes=64 * 1024 * 1024 - 256 * 1024),
    )(tokens, out_grad, blocks, row_scale, count)


AXES = ("dp", "fsdp")


def flat_to_blocks(flat):
    rows = jnp.pad(flat.reshape(LAYERS, FLAT, LANES), ((0, 0), (0, BLOCK), (0, 0)))
    starts = [(145 * part) // 2 for part in range(PARTS)]
    return jnp.stack([rows[:, start : start + BLOCK] for start in starts])


def blocks_to_flat(blocks):
    joined = []
    for pair in range(PARTS // 2):
        first, second = blocks[2 * pair], blocks[2 * pair + 1]
        seam = jnp.concatenate([first[:, 72:73, 0:64], second[:, 0:1, 64:]], axis=2)
        joined += [first[:, 0:72], seam, second[:, 1:73]]
    return jnp.concatenate(joined, axis=1).reshape(LAYERS, PSIZE)


def gather_params(flat_params):
    parts = lax.axis_size(AXES)
    if parts != PARTS:
        return flat_to_blocks(lax.all_gather(flat_params, AXES, axis=1, tiled=True))
    size = flat_params.shape[1]
    room = BLOCK * LANES - size
    padded = jnp.where(
        lax.axis_index("fsdp") % 2 == 0,
        jnp.pad(flat_params, ((0, 0), (0, room))),
        jnp.pad(flat_params, ((0, 0), (64, room - 64))),
    ).reshape(LAYERS, BLOCK, LANES)
    return lax.all_gather(padded, AXES, axis=0, tiled=False)


def reduce_grads(grads, size):
    parts = lax.axis_size(AXES)
    if parts != PARTS:
        return lax.psum_scatter(
            blocks_to_flat(grads.astype(F32)), AXES, scatter_dimension=1, tiled=True
        )
    got = lax.all_to_all(grads, AXES, 0, 0, tiled=True)
    total = jnp.sum(got.astype(F32), axis=0).reshape(LAYERS, BLOCK * LANES)
    return jnp.where(
        lax.axis_index("fsdp") % 2 == 0, total[:, 0:size], total[:, 64 : 64 + size]
    )


def body(tokens, out_grad, flat_params, feat_count, table_ids, table_counts):
    counts_float = table_counts.astype(F32)
    table_index = jnp.arange(table_counts.shape[0], dtype=jnp.int32)
    match = (table_ids[None, :] == table_index[:, None]).astype(F32)
    row_count = jnp.sum(match * counts_float[:, None], axis=0)
    row_scale = jnp.sqrt(jnp.mean(counts_float) / row_count)[None, :]
    count = feat_count.astype(F32)[None, :]
    blocks = gather_params(flat_params)
    turned = jnp.transpose(tokens, (1, 2, 0))
    turned_grad = jnp.transpose(out_grad, (1, 2, 0))
    results = [
        run_kernel(
            turned[:, :, at : at + ROWS],
            turned_grad[:, :, at : at + ROWS],
            blocks,
            row_scale[:, at : at + ROWS],
            count[:, at : at + ROWS],
        )
        for at in range(0, tokens.shape[0], ROWS)
    ]
    out, in_grad, grads = results[0]
    if len(results) > 1:
        out = jnp.concatenate([r[0] for r in results], axis=2)
        in_grad = jnp.concatenate([r[1] for r in results], axis=2)
        grads = sum(r[2].astype(F32) for r in results).astype(BF16)
    return (
        jnp.transpose(out, (2, 0, 1)),
        jnp.transpose(in_grad, (2, 0, 1)),
        reduce_grads(grads, flat_params.shape[1]),
    )


def solution(mesh):
    rows = P(AXES, None, None)
    placed = (rows, rows, P(None, AXES), P(AXES), P(AXES), P())
    return jax.shard_map(
        body,
        mesh=mesh,
        in_specs=placed,
        out_specs=(rows, rows, P(None, AXES)),
        check_vma=False,
    )
```

```python
import math

import jax
import jax.numpy as jnp
from jax import lax
from jax.experimental import pallas as pl
from jax.experimental.pallas import tpu as pltpu
from jax.sharding import PartitionSpec as P

D = 192
FF = 256
HEADS = 8
HEAD_DIM = 24
SEQ = 17
LAYERS = 2
PSIZE = 296960
ROWS = 128
SLOTS = 18
LANES = 128
UNROLL = 4
DEPTH = 6
STEPS = 3
GROUP = 8
GROUPS = ROWS // GROUP
GT = SLOTS * GROUP
QL = HEADS * GT
TOKENS = SLOTS * ROWS
CHUNK = 2 * ROWS
CHUNKS = TOKENS // CHUNK
FLAT = PSIZE // LANES
PARTS = 32
BLOCK = 80
EPS = 1e-05
SCALE = 1.0 / math.sqrt(HEAD_DIM)
F32 = jnp.float32
BF16 = jnp.bfloat16


def dot(a, b, ca, cb):
    return lax.dot_general(a, b, (((ca,), (cb,)), ((), ())), preferred_element_type=F32)


def lane_half(shape):
    return lax.broadcasted_iota(jnp.int32, shape, len(shape) - 1) < 64


def swap(x):
    return pltpu.roll(x, 64, x.ndim - 1)


def low_half(x):
    return jnp.where(lane_half(x.shape), x, 0.0)


def splice(a, b):
    return jnp.where(lane_half(a.shape), swap(a), swap(b))


def after(a, b):
    return jnp.where(lane_half(a.shape), a, swap(b))


def wide(column):
    return jnp.concatenate([column, column], axis=1)


def gather_flat(blocks, layer, flat):
    for pair in range(blocks.shape[0] // 2):
        base = 145 * pair
        first = blocks[2 * pair, layer].astype(F32)
        second = blocks[2 * pair + 1, layer].astype(F32)
        flat[pl.ds(base, BLOCK), :] = first
        flat[pl.ds(base + 72, BLOCK), :] = second
        flat[pl.ds(base + 72, 1), :] = jnp.where(
            lane_half((1, LANES)), first[72:73], second[0:1]
        )


def column_of(row):
    return jnp.transpose(jnp.broadcast_to(row, (LANES, 2 * LANES)))[0:D]


def unpack(flat, w, tmp):
    def rows(start, count, stride):
        return flat[pl.ds(start, count, stride=stride), :]

    def row(index):
        return flat[pl.ds(index, 1), :]

    def pair_row(a, b):
        return jnp.concatenate([a, b], axis=1)

    w["cols"][0] = column_of(pair_row(row(0), low_half(row(1))))
    w["cols"][1] = column_of(pair_row(splice(row(1), row(2)), low_half(swap(row(2)))))
    w["cols"][2] = column_of(pair_row(row(1158), low_half(row(1159))))
    w["cols"][3] = column_of(pair_row(splice(row(1159), row(1160)), low_half(swap(row(1160)))))
    w["cols"][4] = column_of(pair_row(row(1161), low_half(row(1162))))
    w["cols"][5] = column_of(pair_row(splice(row(2318), row(2319)), low_half(swap(row(2319)))))

    e = [rows(3 + j, 96, 9) for j in range(9)]
    even = (e[0], low_half(e[1]), splice(e[1], e[2]), low_half(swap(e[2])), e[3], low_half(e[4]))
    odd = (
        splice(e[4], e[5]),
        low_half(swap(e[5])),
        e[6],
        low_half(e[7]),
        splice(e[7], e[8]),
        low_half(swap(e[8])),
    )
    zero_row = jnp.zeros((1, LANES), F32)
    bias = (
        row(867),
        low_half(row(868)),
        zero_row,
        zero_row,
        splice(row(868), row(869)),
        low_half(swap(row(869))),
    )
    first_row = lax.broadcasted_iota(jnp.int32, (16, LANES), 0) == 0
    for j in range(6):
        tmp[j, pl.ds(0, 96, stride=2), :] = even[j]
        tmp[j, pl.ds(1, 96, stride=2), :] = odd[j]
        w["qkv"][0:D, j * LANES : (j + 1) * LANES] = tmp[j, 0:D, :].astype(BF16)
        w["qkv"][D : D + 16, j * LANES : (j + 1) * LANES] = jnp.where(
            first_row, jnp.broadcast_to(bias[j], (16, LANES)), 0.0
        ).astype(BF16)

    e = [rows(870 + j, 96, 3) for j in range(3)]
    tmp[0, pl.ds(0, 96, stride=2), :] = e[0]
    tmp[1, pl.ds(0, 96, stride=2), :] = low_half(e[1])
    tmp[0, pl.ds(1, 96, stride=2), :] = splice(e[1], e[2])
    tmp[1, pl.ds(1, 96, stride=2), :] = low_half(swap(e[2]))
    w_out = jnp.concatenate([tmp[0, 0:D, :], tmp[1, 0:D, :]], axis=1)
    w["out_t"][...] = jnp.transpose(w_out)[0:D].astype(BF16)

    g = [rows(1162 + j, 192, 4) for j in range(5)]
    tiles = [splice(g[j], g[j + 1]) for j in range(4)]
    gate_up = jnp.concatenate(tiles, axis=1)
    w["gu"][...] = gate_up.astype(BF16)
    bias_row = jnp.concatenate(
        [splice(row(1930 + j), row(1931 + j)) for j in range(4)], axis=1
    )
    bias_rows = jnp.where(
        lax.broadcasted_iota(jnp.int32, (64, 2 * FF), 0) == 0,
        jnp.broadcast_to(bias_row, (64, 2 * FF)),
        0.0,
    )
    w["gu_t"][...] = jnp.transpose(jnp.concatenate([gate_up, bias_rows], axis=0))[
        :, 0 : D + 16
    ].astype(BF16)

    e = [rows(1934 + j, 128, 3) for j in range(4)]
    tmp[0, pl.ds(0, 128, stride=2), :] = splice(e[0], e[1])
    tmp[1, pl.ds(0, 128, stride=2), :] = low_half(swap(e[1]))
    tmp[0, pl.ds(1, 128, stride=2), :] = e[2]
    tmp[1, pl.ds(1, 128, stride=2), :] = low_half(e[3])
    w_down = jnp.concatenate([tmp[0, 0:FF, :], tmp[1, 0:FF, :]], axis=1)
    w["down"][...] = w_down[:, 0:D].astype(BF16)
    w["down_t"][...] = jnp.transpose(w_down)[0:D].astype(BF16)


def row_of(columns):
    turned = jnp.sum(jnp.transpose(columns), axis=0, keepdims=True)
    return turned[:, 0:LANES], jnp.concatenate(
        [turned[:, LANES:D], jnp.zeros((1, LANES - (D - LANES)), F32)], axis=1
    )


def pack(flat, acc, sums, tmp):
    def put(start, count, stride, value):
        flat[pl.ds(start, count, stride=stride), :] = value

    def put_row(index, value):
        flat[pl.ds(index, 1), :] = value

    def down(j, start, count, stride):
        return acc["down"][j, pl.ds(start, count, stride=stride), :]

    g1 = row_of(sums[0])
    b1 = row_of(sums[1])
    g2 = row_of(sums[2])
    b2 = row_of(sums[3])
    bo = row_of(sums[4])
    put_row(0, g1[0])
    put_row(1, after(g1[1], b1[0]))
    put_row(2, splice(b1[0], b1[1]))

    even = [acc["qkv"][j, pl.ds(0, 96, stride=2), :] for j in range(6)]
    odd = [acc["qkv"][j, pl.ds(1, 96, stride=2), :] for j in range(6)]
    put(3, 96, 9, even[0])
    put(4, 96, 9, after(even[1], even[2]))
    put(5, 96, 9, splice(even[2], even[3]))
    put(6, 96, 9, even[4])
    put(7, 96, 9, after(even[5], odd[0]))
    put(8, 96, 9, splice(odd[0], odd[1]))
    put(9, 96, 9, odd[2])
    put(10, 96, 9, after(odd[3], odd[4]))
    put(11, 96, 9, splice(odd[4], odd[5]))
    bias = [acc["qkv"][j, D : D + 1, :] for j in range(6)]
    put_row(867, bias[0])
    put_row(868, after(bias[1], bias[4]))
    put_row(869, splice(bias[4], bias[5]))

    w_out = jnp.transpose(
        jnp.concatenate([acc["out_t"][...], jnp.zeros((64, D), F32)], axis=0)
    )
    tmp[0, 0:D, :] = w_out[:, 0:LANES]
    tmp[1, 0:D, :] = w_out[:, LANES:]
    even = [tmp[j, pl.ds(0, 96, stride=2), :] for j in range(2)]
    odd = [tmp[j, pl.ds(1, 96, stride=2), :] for j in range(2)]
    put(870, 96, 3, even[0])
    put(871, 96, 3, after(even[1], odd[0]))
    put(872, 96, 3, splice(odd[0], odd[1]))
    put_row(1158, bo[0])
    put_row(1159, after(bo[1], g2[0]))
    put_row(1160, splice(g2[0], g2[1]))
    put_row(1161, b2[0])

    gu = [acc["gu"][j, 0 : D + 8, :] for j in range(4)]
    put_row(1162, after(b2[1], gu[0][0:1]))
    put(1166, 192, 4, splice(gu[3][0:192], acc["gu"][0, pl.ds(1, 192), :]))
    for j in range(1, 4):
        joined = splice(gu[j - 1], gu[j])
        put(1162 + j, 192, 4, joined[0:192])
        put_row(1930 + j, joined[192:193])
    put_row(1934, splice(gu[3][192:193], acc["down"][0, 0:1, :]))

    w0e, w1e = down(0, 0, 128, 2), down(1, 0, 128, 2)
    w0o, w1o = down(0, 1, 128, 2), down(1, 1, 128, 2)
    put(1935, 128, 3, splice(w0e, w1e))
    put(1936, 128, 3, w0o)
    put(1937, 128, 3, after(w1o, down(0, 2, 128, 2)))
    put_row(2319, splice(acc["down"][0, FF : FF + 1, :], acc["down"][1, FF : FF + 1, :]))


def scatter_blocks(flat, layer, blocks):
    for part in range(blocks.shape[0]):
        start = (145 * part) // 2
        blocks[part, layer] = flat[pl.ds(start, BLOCK), :].astype(BF16)


def norm(x, gain, bias):
    centre = x - jnp.sum(x, axis=0, keepdims=True) * (1.0 / D)
    variance = jnp.sum(centre * centre, axis=0, keepdims=True) * (1.0 / D)
    rstd = lax.rsqrt(variance + EPS)
    xhat = centre * rstd
    return xhat, rstd, (xhat * gain + bias).astype(BF16)


def norm_back(grad, xhat, rstd, gain):
    e = gain * grad
    mean_e = jnp.sum(e, axis=0, keepdims=True) * (1.0 / D)
    mean_ex = jnp.sum(e * xhat, axis=0, keepdims=True) * (1.0 / D)
    return rstd * (e - mean_e - xhat * mean_ex)


def fold(x):
    return x[:, 0:LANES] + x[:, LANES:]


def gelu_parts(gate):
    z = gate * (1.0 / math.sqrt(2.0))
    cdf = 0.5 * lax.erf(z) + 0.5
    bell = jnp.exp2(z * z * (-1.0 / math.log(2.0)))
    return cdf, cdf + (z * bell) * (1.0 / math.sqrt(math.pi))


def to_groups(x):
    n = x.shape[-1]
    x = x.reshape(2, GROUPS, GROUP, n)
    return jnp.concatenate([x[0][:, None], x[1][:, None]], axis=1).reshape(
        GROUPS, 2 * GROUP, n
    )


def from_groups(x):
    n = x.shape[-1]
    x = x.reshape(GROUPS, 2, GROUP, n)
    return jnp.concatenate([x[:, 0], x[:, 1]], axis=0).reshape(CHUNK, n)


def lanes_of(c):
    return pl.ds(pl.multiple_of(c * CHUNK, CHUNK), CHUNK)


def group_rows(c):
    return pl.ds(pl.multiple_of(c * 2 * GROUP, 2 * GROUP), 2 * GROUP)


def skewed(stages):
    def steps(i, carry):
        held = {}
        for tick in range(STEPS + len(stages) - 1):
            for j, stage in enumerate(stages):
                u = tick - j
                if 0 <= u < STEPS:
                    held[u] = stage(i * STEPS + u, held.get(u))
        return carry

    lax.fori_loop(0, CHUNKS // STEPS, steps, 0)


def forward_qkv(s, w):
    gain, bias = wide(w["cols"][0]), wide(w["cols"][1])

    def project(c, _):
        lanes = lanes_of(c)
        xhat, rstd, normed = norm(s["x"][:, lanes], gain, bias)
        s["xhat1"][:, lanes] = xhat
        s["rstd1"][:, lanes] = rstd
        s["h1"][0:D, lanes] = normed
        return dot(s["h1"][:, lanes], w["qkv"][...], 0, 0)

    def keep(c, qkv):
        place = group_rows(c)
        s["q"][:, place, :] = to_groups(qkv[:, 0:D]).astype(BF16)
        for name, start in (("k", 256), ("v", 512)):
            part = qkv[:, start : start + D].reshape(2, GROUPS, GROUP, D)
            turned = jnp.concatenate(
                [
                    pltpu.roll(part[t], lax.rem(2 * c + t, GROUP), 1)[:, None]
                    for t in range(2)
                ],
                axis=1,
            )
            s[name][:, place, :] = turned.reshape(GROUPS, 2 * GROUP, D).astype(BF16)

    skewed((project, keep))


def spread(values, masks):
    n = values.shape[1]
    doubled = [
        jnp.concatenate([values[8 * a : 8 * a + 8], values[8 * a : 8 * a + 8]], axis=0).astype(BF16)
        for a in range(3)
    ]
    parts = [doubled[a] * masks[m][:, 0:n] for a in range(2) for m in range(4)]
    parts.append(doubled[2] * masks[4][:, 0:n])
    return jnp.concatenate(parts, axis=0)


def collect(scores, bits):
    n = scores.shape[1]
    bits = [bit[:, 0:n] for bit in bits]
    out = []
    for a in range(2):
        level = [scores[64 * a + 8 * j : 64 * a + 8 * j + 8] for j in range(8)]
        for bit in bits:
            level = [
                jnp.where(bit, level[2 * i + 1], level[2 * i]) for i in range(len(level) // 2)
            ]
        out.append(level[0])
    out.append(scores[128:136])
    return out


def blocks_of(turned, t, halves):
    first = turned[48 * t : 48 * t + 16]
    middle = turned[48 * t + 16 : 48 * t + 32]
    last = turned[48 * t + 32 : 48 * t + 48]
    none = jnp.zeros_like(first)
    return jnp.concatenate(
        [
            jnp.concatenate([first, none], axis=1),
            jnp.concatenate([middle * halves[0], middle * halves[1]], axis=1),
            jnp.concatenate([none, last], axis=1),
        ],
        axis=0,
    )


def padded(block, t):
    parts = [block]
    if t > 0:
        parts.insert(0, jnp.zeros((48 * t, block.shape[1]), BF16))
    if t < 3:
        parts.append(jnp.zeros((48 * (3 - t), block.shape[1]), BF16))
    return jnp.concatenate(parts, axis=0)


def tail_of(rows, heads):
    return jnp.transpose(
        jnp.concatenate([rows * heads[h, 0:1, :] for h in range(HEADS)], axis=0)
    )


def heads_joined(tiles, tail, heads, scale=None):
    main = []
    for tile in tiles:
        main += [tile[0:HEAD_DIM, 0:LANES], tile[HEAD_DIM:, LANES:]]
    main = jnp.concatenate(main, axis=0)
    if scale is not None:
        main, tail = main * scale, tail * scale
    main = jnp.transpose(main.astype(BF16))
    tail = jnp.transpose(tail.astype(BF16))
    last = tail[0:16] * heads[0, 0:1, :]
    for h in range(1, HEADS):
        last += tail[16 * h : 16 * h + 16] * heads[h, 0:1, :]
    return main, last


def softmax(kept, diff, limit):
    n = kept[0].shape[1]
    own = diff[:, 0:n]
    limit = limit[:, 0:n]
    slot = own.astype(F32)
    shown = [
        jnp.where(slot <= limit, kept[0] * SCALE, -1e9),
        jnp.where(slot + 8.0 <= limit, kept[1] * SCALE, -1e9),
        jnp.where(own == 0, jnp.where(limit >= 16.0, kept[2] * SCALE, -1e9), -3e38),
    ]
    top = jnp.max(jnp.maximum(jnp.maximum(shown[0], shown[1]), shown[2]), axis=0, keepdims=True)
    shown = [jnp.exp(part - top) for part in shown]
    inverse = 1.0 / jnp.sum(shown[0] + shown[1] + shown[2], axis=0, keepdims=True)
    return jnp.concatenate([part * inverse for part in shown], axis=0)


def staged(items, first, second):
    waiting = []
    for item in items:
        waiting.append((item, first(item)))
        if len(waiting) > DEPTH:
            second(*waiting.pop(0))
    for entry in waiting:
        second(*entry)


def forward_attention(s, env):
    diff = env["diff"][...]
    bits = [(diff & (1 << i)) != 0 for i in range(3)]
    halves = [env["halves"][i] for i in range(2)]

    def step(i, carry):
        state = {}

        def load(u):
            g = i * UNROLL + u
            queries, values = s["q"][g], s["v"][g]
            state[u] = {
                "g": g,
                "queries": queries,
                "keys": s["k"][g],
                "turned": jnp.transpose(queries)[:, 0:LANES],
                "values": jnp.transpose(values),
                "count": env["count"][pl.ds(g, 1), :],
                "tiles": [],
            }

        def scores(item):
            u, t = item
            if t == 0:
                load(u)
            at = state[u]
            if t < 4:
                right = padded(blocks_of(at["turned"], t, halves), t)
            else:
                right = tail_of(at["queries"][LANES:GT], env["heads"])
            return dot(at["keys"], right, 1, 0)

        def mix(item, products):
            u, t = item
            at = state[u]
            attention = softmax(collect(products, bits), diff, at["count"])
            s["att"][at["g"], :, t * CHUNK : min((t + 1) * CHUNK, QL)] = attention
            low = spread(attention, env["masks"])
            left = at["values"][48 * t : 48 * t + 48] if t < 4 else at["values"]
            at["tiles"].append(dot(left, low, 1, 0))
            if t == 4:
                main, last = heads_joined(at["tiles"][0:4], at["tiles"][4], env["heads"])
                s["mixed"][at["g"], 0:LANES, :] = main
                s["mixed"][at["g"], LANES:GT, :] = last

        staged([(u, t) for u in range(UNROLL) for t in range(5)], scores, mix)
        return carry

    lax.fori_loop(0, GROUPS // UNROLL, step, 0)


def forward_rest(s, w, done):
    gain, bias = wide(w["cols"][3]), wide(w["cols"][4])
    bias_out, bias_down = wide(w["cols"][2]), wide(w["cols"][5])

    def attended(c, _):
        mixed = from_groups(s["mixed"][:, group_rows(c), :].astype(F32)).astype(BF16)
        return dot(w["out_t"][...], mixed, 1, 1)

    def normed(c, product):
        lanes = lanes_of(c)
        middle = s["x"][:, lanes] + (product + bias_out)
        xhat, rstd, low = norm(middle, gain, bias)
        s["middle"][:, lanes] = middle
        s["xhat2"][:, lanes] = xhat
        s["rstd2"][:, lanes] = rstd
        s["h2"][0:D, lanes] = low
        return dot(w["gu_t"][...], s["h2"][:, lanes], 1, 0)

    def gated(c, gate_up):
        lanes = lanes_of(c)
        gate, up = gate_up[0:FF], gate_up[FF:]
        cdf, slope = gelu_parts(gate)
        gelu = gate * cdf
        act = (gelu * up).astype(BF16)
        s["act"][0:FF, lanes] = act
        s["gelu"][:, lanes] = gelu
        s["slope"][:, lanes] = slope * up
        return dot(w["down_t"][...], act, 1, 0)

    def finish(c, product):
        lanes = lanes_of(c)
        done(c, lanes, s["middle"][:, lanes] + (product + bias_down))

    skewed((attended, normed, gated, finish))


def add_tiles(ref, value):
    for j in range(ref.shape[0]):
        ref[j] += value[:, j * LANES : (j + 1) * LANES]


def add_narrow(ref, value):
    ref[0] += value[:, 0:LANES]
    ref[1, :, 0 : D - LANES] += value[:, LANES:D]


def backward_rest(s, w, acc, sums):
    gain = wide(w["cols"][3])

    def down(c, _):
        lanes = lanes_of(c)
        branch = s["g"][:, lanes].astype(BF16)
        return dot(s["act"][:, lanes], branch, 1, 1), dot(w["down"][...], branch, 1, 0)

    def gate_up(c, held):
        lanes = lanes_of(c)
        grad_down, d_act = held
        add_narrow(acc["down"], grad_down)
        d_gate_up = jnp.concatenate(
            [d_act * s["slope"][:, lanes], d_act * s["gelu"][:, lanes]], axis=0
        ).astype(BF16)
        return dot(s["h2"][:, lanes], d_gate_up, 1, 1), dot(w["gu"][...], d_gate_up, 1, 0)

    def normed(c, held):
        lanes = lanes_of(c)
        grad_gu, d_normed = held
        add_tiles(acc["gu"], grad_gu)
        xhat = s["xhat2"][:, lanes]
        sums[2] += fold(d_normed * xhat)
        sums[3] += fold(d_normed)
        d_middle = s["g"][:, lanes] + norm_back(d_normed, xhat, s["rstd2"][:, lanes], gain)
        s["g"][:, lanes] = d_middle
        d_attended = d_middle.astype(BF16)
        sums[4] += fold(d_attended.astype(F32))
        mixed = from_groups(s["mixed"][:, group_rows(c), :].astype(F32)).astype(BF16)
        return dot(d_attended, w["out_t"][...], 0, 0), dot(d_attended, mixed, 1, 0)

    def finish(c, held):
        d_mixed, grad_out = held
        s["dm"][:, group_rows(c), :] = to_groups(d_mixed).astype(BF16)
        acc["out_t"][...] += grad_out

    skewed((down, gate_up, normed, finish))


def backward_attention(s, env):
    diff = env["diff"][...]
    bits = [(diff & (1 << i)) != 0 for i in range(3)]
    halves = [env["halves"][i] for i in range(2)]

    def step(i, carry):
        state = {}

        def load(u):
            g = i * UNROLL + u
            queries, keys, grads = s["q"][g], s["k"][g], s["dm"][g]
            state[u] = {
                "g": g,
                "queries": queries,
                "grads": grads,
                "values": s["v"][g],
                "turned": jnp.transpose(queries)[:, 0:LANES],
                "turned_grads": jnp.transpose(grads)[:, 0:LANES],
                "turned_keys": jnp.transpose(keys),
                "dq": [],
                "dk": [],
                "dv": [],
            }

        def products(item):
            u, t = item
            if t == 0:
                load(u)
            at = state[u]
            if t < 4:
                block = blocks_of(at["turned_grads"], t, halves)
                right = padded(block, t)
            else:
                block = right = tail_of(at["grads"][LANES:GT], env["heads"])
            return block, dot(at["values"], right, 1, 0)

        def back(item, result):
            u, t = item
            at = state[u]
            grad_block, product = result
            attention = s["att"][at["g"], :, t * CHUNK : min((t + 1) * CHUNK, QL)]
            weighted = attention * jnp.concatenate(collect(product, bits), axis=0)
            total = jnp.sum(weighted, axis=0, keepdims=True)
            d_score = spread(weighted - attention * total, env["masks"])
            at["dv"].append(dot(grad_block, spread(attention, env["masks"]), 1, 1))
            if t < 4:
                block = blocks_of(at["turned"], t, halves)
                left = at["turned_keys"][48 * t : 48 * t + 48]
            else:
                block = tail_of(at["queries"][LANES:GT], env["heads"])
                left = at["turned_keys"]
            at["dk"].append(dot(block, d_score, 1, 1))
            at["dq"].append(dot(left, d_score, 1, 0))
            if t == 4:
                finish(at)

        def finish(at):
            g = at["g"]
            main, last = heads_joined(at["dq"][0:4], at["dq"][4], env["heads"], SCALE)
            s["dqkv"][g, 0:LANES, 0:D] = main
            s["dqkv"][g, LANES:GT, 0:D] = last
            d_keys = (jnp.concatenate(at["dk"][0:4], axis=0) + at["dk"][4]) * SCALE
            d_values = jnp.concatenate(at["dv"][0:4], axis=0) + at["dv"][4]
            for value, start in ((d_keys, 256), (d_values, 512)):
                slots = jnp.transpose(value.astype(BF16)).astype(F32).reshape(SLOTS, GROUP, D)
                turned = [
                    slots[k] if k % GROUP == 0 else pltpu.roll(slots[k], GROUP - k % GROUP, 0)
                    for k in range(SLOTS)
                ]
                s["dqkv"][g, :, start : start + D] = jnp.concatenate(turned, axis=0).astype(BF16)

        staged([(u, t) for u in range(UNROLL) for t in range(5)], products, back)
        return carry

    lax.fori_loop(0, GROUPS // UNROLL, step, 0)


def backward_qkv(s, w, acc, sums, done):
    gain = wide(w["cols"][0])

    def products(c, _):
        d_qkv = from_groups(s["dqkv"][:, group_rows(c), :].astype(F32)).astype(BF16)
        return dot(s["h1"][:, lanes_of(c)], d_qkv, 1, 0), dot(w["qkv"][0:D, :], d_qkv, 1, 1)

    def finish(c, held):
        lanes = lanes_of(c)
        grad_qkv, d_normed = held
        add_tiles(acc["qkv"], grad_qkv)
        xhat = s["xhat1"][:, lanes]
        sums[0] += fold(d_normed * xhat)
        sums[1] += fold(d_normed)
        done(
            c, lanes, s["g"][:, lanes] + norm_back(d_normed, xhat, s["rstd1"][:, lanes], gain)
        )

    skewed((products, finish))


def per_layer():
    return {
        "x": ((D, TOKENS), F32),
        "xhat1": ((D, TOKENS), F32),
        "rstd1": ((1, TOKENS), F32),
        "h1": ((D + 16, TOKENS), BF16),
        "q": ((GROUPS, GT, D), BF16),
        "k": ((GROUPS, GT, D), BF16),
        "v": ((GROUPS, GT, D), BF16),
        "att": ((GROUPS, 24, QL), F32),
        "mixed": ((GROUPS, GT, D), BF16),
        "xhat2": ((D, TOKENS), F32),
        "rstd2": ((1, TOKENS), F32),
        "h2": ((D + 16, TOKENS), BF16),
        "act": ((FF + 16, TOKENS), BF16),
        "gelu": ((FF, TOKENS), F32),
        "slope": ((FF, TOKENS), F32),
    }


def weights():
    return {
        "cols": ((6, D, LANES), F32),
        "qkv": ((D + 16, 6 * LANES), BF16),
        "out_t": ((D, D), BF16),
        "gu": ((D, 2 * FF), BF16),
        "gu_t": ((2 * FF, D + 16), BF16),
        "down": ((FF, D), BF16),
        "down_t": ((D, FF), BF16),
    }


def accumulators():
    return {
        "qkv": ((6, D + 16, LANES), F32),
        "out_t": ((D, D), F32),
        "gu": ((4, D + 16, LANES), F32),
        "down": ((2, FF + 16, LANES), F32),
    }


def common():
    return {
        "halves": ((2, 16, LANES), BF16),
        "heads": ((HEADS, 16, D), BF16),
        "masks": ((5, 16, CHUNK), BF16),
        "diff": ((GROUP, CHUNK), jnp.int32),
        "count": ((GROUPS, CHUNK), F32),
        "dm": ((GROUPS, GT, D), BF16),
        "middle": ((D, TOKENS), F32),
        "dqkv": ((GROUPS, GT, 6 * LANES), BF16),
        "g": ((D, TOKENS), F32),
        "sums": ((5, D, LANES), F32),
        "flat": ((FLAT + 8, LANES), F32),
        "tmp": ((6, FF, LANES), F32),
    }


def make_scratch():
    shapes, names = [], []
    for prefix, table in (
        ("common", common()),
        ("acc", accumulators()),
        ("s0", per_layer()),
        ("s1", per_layer()),
        ("w0", weights()),
        ("w1", weights()),
    ):
        for name, (shape, kind) in table.items():
            names.append((prefix, name))
            shapes.append(pltpu.VMEM(shape, kind))
    return names, shapes


def init_env(env, count):
    lane = lax.broadcasted_iota(jnp.int32, (GROUP, CHUNK), 1)
    sub = lax.broadcasted_iota(jnp.int32, (GROUP, CHUNK), 0)
    diff = (sub - lane) & (GROUP - 1)
    env["diff"][...] = diff
    for m in range(5):
        first = jnp.where(diff == (2 * m) % 8, 1.0, 0.0)
        second = jnp.where(diff == 2 * m + 1, 1.0, 0.0)
        env["masks"][m] = jnp.concatenate([first, second], axis=0).astype(BF16)
    sub = lax.broadcasted_iota(jnp.int32, (16, LANES), 0)
    env["halves"][0] = jnp.where(sub < 8, 1.0, 0.0).astype(BF16)
    env["halves"][1] = jnp.where(sub < 8, 0.0, 1.0).astype(BF16)
    feature = lax.broadcasted_iota(jnp.int32, (16, D), 1) // HEAD_DIM
    for h in range(HEADS):
        env["heads"][h] = jnp.where(feature == h, 1.0, 0.0).astype(BF16)
    row = lax.broadcasted_iota(jnp.int32, (GROUPS, LANES), 1)
    group = lax.broadcasted_iota(jnp.int32, (GROUPS, LANES), 0)
    mine = jnp.where(row // GROUP == group, jnp.broadcast_to(count, (GROUPS, LANES)), 0.0)
    here = lax.broadcasted_iota(jnp.int32, (LANES, CHUNK), 0)
    there = lax.broadcasted_iota(jnp.int32, (LANES, CHUNK), 1)
    pick = jnp.where(here % GROUP == there % GROUP, 1.0, 0.0).astype(BF16)
    env["count"][...] = dot(mine.astype(BF16), pick, 1, 0)


def ones_below(ref, rows):
    tail = ref.shape[0] - rows
    mark = lax.broadcasted_iota(jnp.int32, (tail, ref.shape[1]), 0) == 0
    ref[rows:, :] = jnp.where(mark, 1.0, 0.0).astype(BF16)


def kernel(names, tokens, out_grad, blocks, row_scale, count, out, in_grad, grads, *scratch):
    table = {}
    for (prefix, name), ref in zip(names, scratch):
        table.setdefault(prefix, {})[name] = ref
    env, acc = table["common"], table["acc"]
    s, w = [table["s0"], table["s1"]], [table["w0"], table["w1"]]
    sums = env["sums"]

    init_env(env, count[...])
    valid_slots = count[...]
    env["dqkv"][...] = jnp.zeros_like(env["dqkv"])
    for layer in range(LAYERS):
        ones_below(s[layer]["h1"], D)
        ones_below(s[layer]["h2"], D)
        ones_below(s[layer]["act"], FF)
        gather_flat(blocks, layer, env["flat"])
        unpack(env["flat"], w[layer], env["tmp"])
    for slot in range(SLOTS):
        lanes = slice(slot * ROWS, (slot + 1) * ROWS)
        if slot < SEQ:
            s[0]["x"][:, lanes] = tokens[slot].astype(F32)
            keep = jnp.where(valid_slots >= float(slot), row_scale[...], 0.0)
            env["g"][:, lanes] = out_grad[slot].astype(F32) * keep
        else:
            s[0]["x"][:, lanes] = jnp.zeros((D, ROWS), F32)
            env["g"][:, lanes] = jnp.zeros((D, ROWS), F32)

    def put(target):
        def done(c, lanes, value):
            target[2 * c] = value[:, 0:ROWS]

            @pl.when(c < CHUNKS - 1)
            def _():
                target[2 * c + 1] = value[:, ROWS:]

        return done

    def keep(target):
        def done(c, lanes, value):
            target[:, lanes] = value

        return done

    for layer in range(LAYERS):
        forward_qkv(s[layer], w[layer])
        forward_attention(s[layer], env)
        last = layer == LAYERS - 1
        forward_rest(dict(s[layer], middle=env["middle"]), w[layer], put(out) if last else keep(s[layer + 1]["x"]))
    for layer in reversed(range(LAYERS)):
        sums[...] = jnp.zeros_like(sums)
        for ref in acc.values():
            ref[...] = jnp.zeros_like(ref)
        state = dict(s[layer], g=env["g"], dm=env["dm"], dqkv=env["dqkv"])
        backward_rest(state, w[layer], acc, sums)
        backward_attention(state, env)
        backward_qkv(
            state, w[layer], acc, sums, put(in_grad) if layer == 0 else keep(env["g"])
        )
        pack(env["flat"], acc, sums, env["tmp"])
        scatter_blocks(env["flat"], layer, grads)


def run_kernel(tokens, out_grad, blocks, row_scale, count):
    names, scratch = make_scratch()
    full = jax.ShapeDtypeStruct((SEQ, D, ROWS), F32)

    def body(*refs):
        kernel(names, *refs)

    return pl.pallas_call(
        body,
        out_shape=(full, full, jax.ShapeDtypeStruct(blocks.shape, BF16)),
        in_specs=[pl.BlockSpec(memory_space=pltpu.VMEM)] * 5,
        out_specs=[pl.BlockSpec(memory_space=pltpu.VMEM)] * 3,
        scratch_shapes=scratch,
        compiler_params=pltpu.CompilerParams(vmem_limit_bytes=64 * 1024 * 1024 - 256 * 1024),
    )(tokens, out_grad, blocks, row_scale, count)


AXES = ("dp", "fsdp")


def flat_to_blocks(flat):
    rows = jnp.pad(flat.reshape(LAYERS, FLAT, LANES), ((0, 0), (0, BLOCK), (0, 0)))
    starts = [(145 * part) // 2 for part in range(PARTS)]
    return jnp.stack([rows[:, start : start + BLOCK] for start in starts])


def blocks_to_flat(blocks):
    joined = []
    for pair in range(PARTS // 2):
        first, second = blocks[2 * pair], blocks[2 * pair + 1]
        seam = jnp.concatenate([first[:, 72:73, 0:64], second[:, 0:1, 64:]], axis=2)
        joined += [first[:, 0:72], seam, second[:, 1:73]]
    return jnp.concatenate(joined, axis=1).reshape(LAYERS, PSIZE)


def gather_params(flat_params):
    parts = lax.axis_size(AXES)
    if parts != PARTS:
        return flat_to_blocks(lax.all_gather(flat_params, AXES, axis=1, tiled=True))
    size = flat_params.shape[1]
    room = BLOCK * LANES - size
    padded = jnp.where(
        lax.axis_index("fsdp") % 2 == 0,
        jnp.pad(flat_params, ((0, 0), (0, room))),
        jnp.pad(flat_params, ((0, 0), (64, room - 64))),
    ).reshape(LAYERS, BLOCK, LANES)
    return lax.all_gather(padded, AXES, axis=0, tiled=False)


def reduce_grads(grads, size):
    parts = lax.axis_size(AXES)
    if parts != PARTS:
        return lax.psum_scatter(
            blocks_to_flat(grads.astype(F32)), AXES, scatter_dimension=1, tiled=True
        )
    got = lax.all_to_all(grads, AXES, 0, 0, tiled=True)
    total = jnp.sum(got.astype(F32), axis=0).reshape(LAYERS, BLOCK * LANES)
    return jnp.where(
        lax.axis_index("fsdp") % 2 == 0, total[:, 0:size], total[:, 64 : 64 + size]
    )


def body(tokens, out_grad, flat_params, feat_count, table_ids, table_counts):
    counts_float = table_counts.astype(F32)
    table_index = jnp.arange(table_counts.shape[0], dtype=jnp.int32)
    match = (table_ids[None, :] == table_index[:, None]).astype(F32)
    row_count = jnp.sum(match * counts_float[:, None], axis=0)
    row_scale = jnp.sqrt(jnp.mean(counts_float) / row_count)[None, :]
    count = feat_count.astype(F32)[None, :]
    blocks = gather_params(flat_params)
    turned = jnp.transpose(tokens, (1, 2, 0))
    turned_grad = jnp.transpose(out_grad, (1, 2, 0))
    results = [
        run_kernel(
            turned[:, :, at : at + ROWS],
            turned_grad[:, :, at : at + ROWS],
            blocks,
            row_scale[:, at : at + ROWS],
            count[:, at : at + ROWS],
        )
        for at in range(0, tokens.shape[0], ROWS)
    ]
    out, in_grad, grads = results[0]
    if len(results) > 1:
        out = jnp.concatenate([r[0] for r in results], axis=2)
        in_grad = jnp.concatenate([r[1] for r in results], axis=2)
        grads = sum(r[2].astype(F32) for r in results).astype(BF16)
    return (
        jnp.transpose(out, (2, 0, 1)),
        jnp.transpose(in_grad, (2, 0, 1)),
        reduce_grads(grads, flat_params.shape[1]),
    )


def solution(mesh):
    rows = P(AXES, None, None)
    placed = (rows, rows, P(None, AXES), P(AXES), P(AXES), P())
    return jax.shard_map(
        body,
        mesh=mesh,
        in_specs=placed,
        out_specs=(rows, rows, P(None, AXES)),
        check_vma=False,
    )
```

```python
import functools
import math

import jax
import jax.numpy as jnp
from jax import lax
from jax.experimental import pallas as pl
from jax.experimental.pallas import tpu as pltpu
from jax.sharding import PartitionSpec as P

D = 192
FF = 256
HEADS = 8
HEAD_DIM = 24
SEQ = 17
LAYERS = 2
PSIZE = 296960
ROWS = 128
SLOTS = 18
LANES = 128
UNROLL = 4
DEPTH = 6
STEPS = 3
GROUP = 8
GROUPS = ROWS // GROUP
GT = SLOTS * GROUP
QL = HEADS * GT
TOKENS = SLOTS * ROWS
CHUNK = 2 * ROWS
CHUNKS = TOKENS // CHUNK
FLAT = PSIZE // LANES
BLOCK = 80
EPS = 1e-05
SCALE = 1.0 / math.sqrt(HEAD_DIM)
F32 = jnp.float32
BF16 = jnp.bfloat16


def dot(a, b, ca, cb):
    return lax.dot_general(a, b, (((ca,), (cb,)), ((), ())), preferred_element_type=F32)


def lane_half(shape):
    return lax.broadcasted_iota(jnp.int32, shape, len(shape) - 1) < 64


def swap(x):
    return pltpu.roll(x, 64, x.ndim - 1)


def low_half(x):
    return jnp.where(lane_half(x.shape), x, 0.0)


def splice(a, b):
    return jnp.where(lane_half(a.shape), swap(a), swap(b))


def after(a, b):
    return jnp.where(lane_half(a.shape), a, swap(b))


def wide(column):
    return jnp.concatenate([column, column], axis=1)


def gather_flat(own, other, place, layer, flat):
    z, core = place[0], place[1]
    for chip in range(FLAT // 145):
        turn = z ^ (chip // 4)
        at = (turn & 1) * 2 + turn // 2
        mine = own[chip % 4, at, layer].astype(F32)
        theirs = other[chip % 4, at, layer].astype(F32)
        first = jnp.where(core == 0, mine, theirs)
        second = jnp.where(core == 0, theirs, mine)
        base = 145 * chip
        flat[pl.ds(base, BLOCK), :] = first
        flat[pl.ds(base + 72, BLOCK), :] = second
        flat[pl.ds(base + 72, 1), :] = jnp.where(
            lane_half((1, LANES)), first[72:73], second[0:1]
        )


def column_of(row):
    return jnp.transpose(jnp.broadcast_to(row, (LANES, 2 * LANES)))[0:D]


def unpack(flat, w, tmp):
    def rows(start, count, stride):
        return flat[pl.ds(start, count, stride=stride), :]

    def row(index):
        return flat[pl.ds(index, 1), :]

    def pair_row(a, b):
        return jnp.concatenate([a, b], axis=1)

    w["cols"][0] = column_of(pair_row(row(0), low_half(row(1))))
    w["cols"][1] = column_of(pair_row(splice(row(1), row(2)), low_half(swap(row(2)))))
    w["cols"][2] = column_of(pair_row(row(1158), low_half(row(1159))))
    w["cols"][3] = column_of(pair_row(splice(row(1159), row(1160)), low_half(swap(row(1160)))))
    w["cols"][4] = column_of(pair_row(row(1161), low_half(row(1162))))
    w["cols"][5] = column_of(pair_row(splice(row(2318), row(2319)), low_half(swap(row(2319)))))

    e = [rows(3 + j, 96, 9) for j in range(9)]
    even = (e[0], low_half(e[1]), splice(e[1], e[2]), low_half(swap(e[2])), e[3], low_half(e[4]))
    odd = (
        splice(e[4], e[5]),
        low_half(swap(e[5])),
        e[6],
        low_half(e[7]),
        splice(e[7], e[8]),
        low_half(swap(e[8])),
    )
    zero_row = jnp.zeros((1, LANES), F32)
    bias = (
        row(867),
        low_half(row(868)),
        zero_row,
        zero_row,
        splice(row(868), row(869)),
        low_half(swap(row(869))),
    )
    first_row = lax.broadcasted_iota(jnp.int32, (16, LANES), 0) == 0
    for j in range(6):
        tmp[j, pl.ds(0, 96, stride=2), :] = even[j]
        tmp[j, pl.ds(1, 96, stride=2), :] = odd[j]
        w["qkv"][0:D, j * LANES : (j + 1) * LANES] = tmp[j, 0:D, :].astype(BF16)
        w["qkv"][D : D + 16, j * LANES : (j + 1) * LANES] = jnp.where(
            first_row, jnp.broadcast_to(bias[j], (16, LANES)), 0.0
        ).astype(BF16)

    e = [rows(870 + j, 96, 3) for j in range(3)]
    tmp[0, pl.ds(0, 96, stride=2), :] = e[0]
    tmp[1, pl.ds(0, 96, stride=2), :] = low_half(e[1])
    tmp[0, pl.ds(1, 96, stride=2), :] = splice(e[1], e[2])
    tmp[1, pl.ds(1, 96, stride=2), :] = low_half(swap(e[2]))
    w_out = jnp.concatenate([tmp[0, 0:D, :], tmp[1, 0:D, :]], axis=1)
    w["out_t"][...] = jnp.transpose(w_out)[0:D].astype(BF16)

    g = [rows(1162 + j, 192, 4) for j in range(5)]
    tiles = [splice(g[j], g[j + 1]) for j in range(4)]
    gate_up = jnp.concatenate(tiles, axis=1)
    w["gu"][...] = gate_up.astype(BF16)
    bias_row = jnp.concatenate(
        [splice(row(1930 + j), row(1931 + j)) for j in range(4)], axis=1
    )
    bias_rows = jnp.where(
        lax.broadcasted_iota(jnp.int32, (64, 2 * FF), 0) == 0,
        jnp.broadcast_to(bias_row, (64, 2 * FF)),
        0.0,
    )
    w["gu_t"][...] = jnp.transpose(jnp.concatenate([gate_up, bias_rows], axis=0))[
        :, 0 : D + 16
    ].astype(BF16)

    e = [rows(1934 + j, 128, 3) for j in range(4)]
    tmp[0, pl.ds(0, 128, stride=2), :] = splice(e[0], e[1])
    tmp[1, pl.ds(0, 128, stride=2), :] = low_half(swap(e[1]))
    tmp[0, pl.ds(1, 128, stride=2), :] = e[2]
    tmp[1, pl.ds(1, 128, stride=2), :] = low_half(e[3])
    w_down = jnp.concatenate([tmp[0, 0:FF, :], tmp[1, 0:FF, :]], axis=1)
    w["down"][...] = w_down[:, 0:D].astype(BF16)
    w["down_t"][...] = jnp.transpose(w_down)[0:D].astype(BF16)


def row_of(columns):
    turned = jnp.sum(jnp.transpose(columns), axis=0, keepdims=True)
    return turned[:, 0:LANES], jnp.concatenate(
        [turned[:, LANES:D], jnp.zeros((1, LANES - (D - LANES)), F32)], axis=1
    )


def pack(flat, acc, sums, tmp):
    def put(start, count, stride, value):
        flat[pl.ds(start, count, stride=stride), :] = value

    def put_row(index, value):
        flat[pl.ds(index, 1), :] = value

    def down(j, start, count, stride):
        return acc["down"][j, pl.ds(start, count, stride=stride), :]

    g1 = row_of(sums[0])
    b1 = row_of(sums[1])
    g2 = row_of(sums[2])
    b2 = row_of(sums[3])
    bo = row_of(sums[4])
    put_row(0, g1[0])
    put_row(1, after(g1[1], b1[0]))
    put_row(2, splice(b1[0], b1[1]))

    even = [acc["qkv"][j, pl.ds(0, 96, stride=2), :] for j in range(6)]
    odd = [acc["qkv"][j, pl.ds(1, 96, stride=2), :] for j in range(6)]
    put(3, 96, 9, even[0])
    put(4, 96, 9, after(even[1], even[2]))
    put(5, 96, 9, splice(even[2], even[3]))
    put(6, 96, 9, even[4])
    put(7, 96, 9, after(even[5], odd[0]))
    put(8, 96, 9, splice(odd[0], odd[1]))
    put(9, 96, 9, odd[2])
    put(10, 96, 9, after(odd[3], odd[4]))
    put(11, 96, 9, splice(odd[4], odd[5]))
    bias = [acc["qkv"][j, D : D + 1, :] for j in range(6)]
    put_row(867, bias[0])
    put_row(868, after(bias[1], bias[4]))
    put_row(869, splice(bias[4], bias[5]))

    w_out = jnp.transpose(
        jnp.concatenate([acc["out_t"][...], jnp.zeros((64, D), F32)], axis=0)
    )
    tmp[0, 0:D, :] = w_out[:, 0:LANES]
    tmp[1, 0:D, :] = w_out[:, LANES:]
    even = [tmp[j, pl.ds(0, 96, stride=2), :] for j in range(2)]
    odd = [tmp[j, pl.ds(1, 96, stride=2), :] for j in range(2)]
    put(870, 96, 3, even[0])
    put(871, 96, 3, after(even[1], odd[0]))
    put(872, 96, 3, splice(odd[0], odd[1]))
    put_row(1158, bo[0])
    put_row(1159, after(bo[1], g2[0]))
    put_row(1160, splice(g2[0], g2[1]))
    put_row(1161, b2[0])

    gu = [acc["gu"][j, 0 : D + 8, :] for j in range(4)]
    put_row(1162, after(b2[1], gu[0][0:1]))
    put(1166, 192, 4, splice(gu[3][0:192], acc["gu"][0, pl.ds(1, 192), :]))
    for j in range(1, 4):
        joined = splice(gu[j - 1], gu[j])
        put(1162 + j, 192, 4, joined[0:192])
        put_row(1930 + j, joined[192:193])
    put_row(1934, splice(gu[3][192:193], acc["down"][0, 0:1, :]))

    w0e, w1e = down(0, 0, 128, 2), down(1, 0, 128, 2)
    w0o, w1o = down(0, 1, 128, 2), down(1, 1, 128, 2)
    put(1935, 128, 3, splice(w0e, w1e))
    put(1936, 128, 3, w0o)
    put(1937, 128, 3, after(w1o, down(0, 2, 128, 2)))
    put_row(2319, splice(acc["down"][0, FF : FF + 1, :], acc["down"][1, FF : FF + 1, :]))


def scatter_blocks(flat, place, layer, keep, give):
    core = place[1]
    for chip in range(FLAT // 145):
        first = flat[pl.ds(145 * chip, BLOCK), :]
        second = flat[pl.ds(145 * chip + 72, BLOCK), :]
        keep[chip % 4, chip // 4, layer] = jnp.where(core == 0, first, second).astype(BF16)
        give[chip % 4, chip // 4, layer] = jnp.where(core == 0, second, first).astype(BF16)


def norm(x, gain, bias):
    centre = x - jnp.sum(x, axis=0, keepdims=True) * (1.0 / D)
    variance = jnp.sum(centre * centre, axis=0, keepdims=True) * (1.0 / D)
    rstd = lax.rsqrt(variance + EPS)
    xhat = centre * rstd
    return xhat, rstd, (xhat * gain + bias).astype(BF16)


def norm_back(grad, xhat, rstd, gain):
    e = gain * grad
    mean_e = jnp.sum(e, axis=0, keepdims=True) * (1.0 / D)
    mean_ex = jnp.sum(e * xhat, axis=0, keepdims=True) * (1.0 / D)
    return rstd * (e - mean_e - xhat * mean_ex)


def fold(x):
    return x[:, 0:LANES] + x[:, LANES:]


def gelu_parts(gate):
    z = gate * (1.0 / math.sqrt(2.0))
    cdf = 0.5 * lax.erf(z) + 0.5
    bell = jnp.exp2(z * z * (-1.0 / math.log(2.0)))
    return cdf, cdf + (z * bell) * (1.0 / math.sqrt(math.pi))


def to_groups(x):
    n = x.shape[-1]
    x = x.reshape(2, GROUPS, GROUP, n)
    return jnp.concatenate([x[0][:, None], x[1][:, None]], axis=1).reshape(
        GROUPS, 2 * GROUP, n
    )


def from_groups(x):
    n = x.shape[-1]
    x = x.reshape(GROUPS, 2, GROUP, n)
    return jnp.concatenate([x[:, 0], x[:, 1]], axis=0).reshape(CHUNK, n)


def lanes_of(c):
    return pl.ds(pl.multiple_of(c * CHUNK, CHUNK), CHUNK)


def group_rows(c):
    return pl.ds(pl.multiple_of(c * 2 * GROUP, 2 * GROUP), 2 * GROUP)


def skewed(stages):
    def steps(i, carry):
        held = {}
        for tick in range(STEPS + len(stages) - 1):
            for j, stage in enumerate(stages):
                u = tick - j
                if 0 <= u < STEPS:
                    held[u] = stage(i * STEPS + u, held.get(u))
        return carry

    lax.fori_loop(0, CHUNKS // STEPS, steps, 0)


def forward_qkv(s, w):
    gain, bias = wide(w["cols"][0]), wide(w["cols"][1])

    def project(c, _):
        lanes = lanes_of(c)
        xhat, rstd, normed = norm(s["x"][:, lanes], gain, bias)
        s["xhat1"][:, lanes] = xhat
        s["rstd1"][:, lanes] = rstd
        s["h1"][0:D, lanes] = normed
        return dot(s["h1"][:, lanes], w["qkv"][...], 0, 0)

    def keep(c, qkv):
        place = group_rows(c)
        s["q"][:, place, :] = to_groups(qkv[:, 0:D]).astype(BF16)
        for name, start in (("k", 256), ("v", 512)):
            part = qkv[:, start : start + D].reshape(2, GROUPS, GROUP, D)
            turned = jnp.concatenate(
                [
                    pltpu.roll(part[t], lax.rem(2 * c + t, GROUP), 1)[:, None]
                    for t in range(2)
                ],
                axis=1,
            )
            s[name][:, place, :] = turned.reshape(GROUPS, 2 * GROUP, D).astype(BF16)

    skewed((project, keep))


def spread(values, masks):
    n = values.shape[1]
    doubled = [
        jnp.concatenate([values[8 * a : 8 * a + 8], values[8 * a : 8 * a + 8]], axis=0).astype(BF16)
        for a in range(3)
    ]
    parts = [doubled[a] * masks[m][:, 0:n] for a in range(2) for m in range(4)]
    parts.append(doubled[2] * masks[4][:, 0:n])
    return jnp.concatenate(parts, axis=0)


def collect(scores, bits):
    n = scores.shape[1]
    bits = [bit[:, 0:n] for bit in bits]
    out = []
    for a in range(2):
        level = [scores[64 * a + 8 * j : 64 * a + 8 * j + 8] for j in range(8)]
        for bit in bits:
            level = [
                jnp.where(bit, level[2 * i + 1], level[2 * i]) for i in range(len(level) // 2)
            ]
        out.append(level[0])
    out.append(scores[128:136])
    return out


def blocks_of(turned, t, halves):
    first = turned[48 * t : 48 * t + 16]
    middle = turned[48 * t + 16 : 48 * t + 32]
    last = turned[48 * t + 32 : 48 * t + 48]
    none = jnp.zeros_like(first)
    return jnp.concatenate(
        [
            jnp.concatenate([first, none], axis=1),
            jnp.concatenate([middle * halves[0], middle * halves[1]], axis=1),
            jnp.concatenate([none, last], axis=1),
        ],
        axis=0,
    )


def padded(block, t):
    parts = [block]
    if t > 0:
        parts.insert(0, jnp.zeros((48 * t, block.shape[1]), BF16))
    if t < 3:
        parts.append(jnp.zeros((48 * (3 - t), block.shape[1]), BF16))
    return jnp.concatenate(parts, axis=0)


def tail_of(rows, heads):
    return jnp.transpose(
        jnp.concatenate([rows * heads[h, 0:1, :] for h in range(HEADS)], axis=0)
    )


def heads_joined(tiles, tail, heads, scale=None):
    main = []
    for tile in tiles:
        main += [tile[0:HEAD_DIM, 0:LANES], tile[HEAD_DIM:, LANES:]]
    main = jnp.concatenate(main, axis=0)
    if scale is not None:
        main, tail = main * scale, tail * scale
    main = jnp.transpose(main.astype(BF16))
    tail = jnp.transpose(tail.astype(BF16))
    last = tail[0:16] * heads[0, 0:1, :]
    for h in range(1, HEADS):
        last += tail[16 * h : 16 * h + 16] * heads[h, 0:1, :]
    return main, last


def softmax(kept, diff, limit):
    n = kept[0].shape[1]
    own = diff[:, 0:n]
    limit = limit[:, 0:n]
    slot = own.astype(F32)
    shown = [
        jnp.where(slot <= limit, kept[0] * SCALE, -1e9),
        jnp.where(slot + 8.0 <= limit, kept[1] * SCALE, -1e9),
        jnp.where(own == 0, jnp.where(limit >= 16.0, kept[2] * SCALE, -1e9), -3e38),
    ]
    top = jnp.max(jnp.maximum(jnp.maximum(shown[0], shown[1]), shown[2]), axis=0, keepdims=True)
    shown = [jnp.exp(part - top) for part in shown]
    inverse = 1.0 / jnp.sum(shown[0] + shown[1] + shown[2], axis=0, keepdims=True)
    return jnp.concatenate([part * inverse for part in shown], axis=0)


def staged(items, first, second):
    waiting = []
    for item in items:
        waiting.append((item, first(item)))
        if len(waiting) > DEPTH:
            second(*waiting.pop(0))
    for entry in waiting:
        second(*entry)


def forward_attention(s, env):
    diff = env["diff"][...]
    bits = [(diff & (1 << i)) != 0 for i in range(3)]
    halves = [env["halves"][i] for i in range(2)]

    def step(i, carry):
        state = {}

        def load(u):
            g = i * UNROLL + u
            queries, values = s["q"][g], s["v"][g]
            state[u] = {
                "g": g,
                "queries": queries,
                "keys": s["k"][g],
                "turned": jnp.transpose(queries)[:, 0:LANES],
                "values": jnp.transpose(values),
                "count": env["count"][pl.ds(g, 1), :],
                "tiles": [],
            }

        def scores(item):
            u, t = item
            if t == 0:
                load(u)
            at = state[u]
            if t < 4:
                right = padded(blocks_of(at["turned"], t, halves), t)
            else:
                right = tail_of(at["queries"][LANES:GT], env["heads"])
            return dot(at["keys"], right, 1, 0)

        def mix(item, products):
            u, t = item
            at = state[u]
            attention = softmax(collect(products, bits), diff, at["count"])
            s["att"][at["g"], :, t * CHUNK : min((t + 1) * CHUNK, QL)] = attention
            low = spread(attention, env["masks"])
            left = at["values"][48 * t : 48 * t + 48] if t < 4 else at["values"]
            at["tiles"].append(dot(left, low, 1, 0))
            if t == 4:
                main, last = heads_joined(at["tiles"][0:4], at["tiles"][4], env["heads"])
                s["mixed"][at["g"], 0:LANES, :] = main
                s["mixed"][at["g"], LANES:GT, :] = last

        staged([(u, t) for u in range(UNROLL) for t in range(5)], scores, mix)
        return carry

    lax.fori_loop(0, GROUPS // UNROLL, step, 0)


def forward_rest(s, w, done):
    gain, bias = wide(w["cols"][3]), wide(w["cols"][4])
    bias_out, bias_down = wide(w["cols"][2]), wide(w["cols"][5])

    def attended(c, _):
        mixed = from_groups(s["mixed"][:, group_rows(c), :].astype(F32)).astype(BF16)
        return dot(w["out_t"][...], mixed, 1, 1)

    def normed(c, product):
        lanes = lanes_of(c)
        middle = s["x"][:, lanes] + (product + bias_out)
        xhat, rstd, low = norm(middle, gain, bias)
        s["middle"][:, lanes] = middle
        s["xhat2"][:, lanes] = xhat
        s["rstd2"][:, lanes] = rstd
        s["h2"][0:D, lanes] = low
        return dot(w["gu_t"][...], s["h2"][:, lanes], 1, 0)

    def gated(c, gate_up):
        lanes = lanes_of(c)
        gate, up = gate_up[0:FF], gate_up[FF:]
        cdf, slope = gelu_parts(gate)
        gelu = gate * cdf
        act = (gelu * up).astype(BF16)
        s["act"][0:FF, lanes] = act
        s["gelu"][:, lanes] = gelu
        s["slope"][:, lanes] = slope * up
        return dot(w["down_t"][...], act, 1, 0)

    def finish(c, product):
        lanes = lanes_of(c)
        done(c, lanes, s["middle"][:, lanes] + (product + bias_down))

    skewed((attended, normed, gated, finish))


def add_tiles(ref, value):
    for j in range(ref.shape[0]):
        ref[j] += value[:, j * LANES : (j + 1) * LANES]


def add_narrow(ref, value):
    ref[0] += value[:, 0:LANES]
    ref[1, :, 0 : D - LANES] += value[:, LANES:D]


def backward_rest(s, w, acc, sums):
    gain = wide(w["cols"][3])

    def down(c, _):
        lanes = lanes_of(c)
        branch = s["g"][:, lanes].astype(BF16)
        return dot(s["act"][:, lanes], branch, 1, 1), dot(w["down"][...], branch, 1, 0)

    def gate_up(c, held):
        lanes = lanes_of(c)
        grad_down, d_act = held
        add_narrow(acc["down"], grad_down)
        d_gate_up = jnp.concatenate(
            [d_act * s["slope"][:, lanes], d_act * s["gelu"][:, lanes]], axis=0
        ).astype(BF16)
        return dot(s["h2"][:, lanes], d_gate_up, 1, 1), dot(w["gu"][...], d_gate_up, 1, 0)

    def normed(c, held):
        lanes = lanes_of(c)
        grad_gu, d_normed = held
        add_tiles(acc["gu"], grad_gu)
        xhat = s["xhat2"][:, lanes]
        sums[2] += fold(d_normed * xhat)
        sums[3] += fold(d_normed)
        d_middle = s["g"][:, lanes] + norm_back(d_normed, xhat, s["rstd2"][:, lanes], gain)
        s["g"][:, lanes] = d_middle
        d_attended = d_middle.astype(BF16)
        sums[4] += fold(d_attended.astype(F32))
        mixed = from_groups(s["mixed"][:, group_rows(c), :].astype(F32)).astype(BF16)
        return dot(d_attended, w["out_t"][...], 0, 0), dot(d_attended, mixed, 1, 0)

    def finish(c, held):
        d_mixed, grad_out = held
        s["dm"][:, group_rows(c), :] = to_groups(d_mixed).astype(BF16)
        acc["out_t"][...] += grad_out

    skewed((down, gate_up, normed, finish))


def backward_attention(s, env):
    diff = env["diff"][...]
    bits = [(diff & (1 << i)) != 0 for i in range(3)]
    halves = [env["halves"][i] for i in range(2)]

    def step(i, carry):
        state = {}

        def load(u):
            g = i * UNROLL + u
            queries, keys, grads = s["q"][g], s["k"][g], s["dm"][g]
            state[u] = {
                "g": g,
                "queries": queries,
                "grads": grads,
                "values": s["v"][g],
                "turned": jnp.transpose(queries)[:, 0:LANES],
                "turned_grads": jnp.transpose(grads)[:, 0:LANES],
                "turned_keys": jnp.transpose(keys),
                "dq": [],
                "dk": [],
                "dv": [],
            }

        def products(item):
            u, t = item
            if t == 0:
                load(u)
            at = state[u]
            if t < 4:
                block = blocks_of(at["turned_grads"], t, halves)
                right = padded(block, t)
            else:
                block = right = tail_of(at["grads"][LANES:GT], env["heads"])
            return block, dot(at["values"], right, 1, 0)

        def back(item, result):
            u, t = item
            at = state[u]
            grad_block, product = result
            attention = s["att"][at["g"], :, t * CHUNK : min((t + 1) * CHUNK, QL)]
            weighted = attention * jnp.concatenate(collect(product, bits), axis=0)
            total = jnp.sum(weighted, axis=0, keepdims=True)
            d_score = spread(weighted - attention * total, env["masks"])
            at["dv"].append(dot(grad_block, spread(attention, env["masks"]), 1, 1))
            if t < 4:
                block = blocks_of(at["turned"], t, halves)
                left = at["turned_keys"][48 * t : 48 * t + 48]
            else:
                block = tail_of(at["queries"][LANES:GT], env["heads"])
                left = at["turned_keys"]
            at["dk"].append(dot(block, d_score, 1, 1))
            at["dq"].append(dot(left, d_score, 1, 0))
            if t == 4:
                finish(at)

        def finish(at):
            g = at["g"]
            main, last = heads_joined(at["dq"][0:4], at["dq"][4], env["heads"], SCALE)
            s["dqkv"][g, 0:LANES, 0:D] = main
            s["dqkv"][g, LANES:GT, 0:D] = last
            d_keys = (jnp.concatenate(at["dk"][0:4], axis=0) + at["dk"][4]) * SCALE
            d_values = jnp.concatenate(at["dv"][0:4], axis=0) + at["dv"][4]
            for value, start in ((d_keys, 256), (d_values, 512)):
                slots = jnp.transpose(value.astype(BF16)).astype(F32).reshape(SLOTS, GROUP, D)
                turned = [
                    slots[k] if k % GROUP == 0 else pltpu.roll(slots[k], GROUP - k % GROUP, 0)
                    for k in range(SLOTS)
                ]
                s["dqkv"][g, :, start : start + D] = jnp.concatenate(turned, axis=0).astype(BF16)

        staged([(u, t) for u in range(UNROLL) for t in range(5)], products, back)
        return carry

    lax.fori_loop(0, GROUPS // UNROLL, step, 0)


def backward_qkv(s, w, acc, sums, done):
    gain = wide(w["cols"][0])

    def products(c, _):
        d_qkv = from_groups(s["dqkv"][:, group_rows(c), :].astype(F32)).astype(BF16)
        return dot(s["h1"][:, lanes_of(c)], d_qkv, 1, 0), dot(w["qkv"][0:D, :], d_qkv, 1, 1)

    def finish(c, held):
        lanes = lanes_of(c)
        grad_qkv, d_normed = held
        add_tiles(acc["qkv"], grad_qkv)
        xhat = s["xhat1"][:, lanes]
        sums[0] += fold(d_normed * xhat)
        sums[1] += fold(d_normed)
        done(
            c, lanes, s["g"][:, lanes] + norm_back(d_normed, xhat, s["rstd1"][:, lanes], gain)
        )

    skewed((products, finish))


def per_layer():
    return {
        "xhat1": ((D, TOKENS), F32),
        "rstd1": ((1, TOKENS), F32),
        "h1": ((D + 16, TOKENS), BF16),
        "q": ((GROUPS, GT, D), BF16),
        "k": ((GROUPS, GT, D), BF16),
        "v": ((GROUPS, GT, D), BF16),
        "att": ((GROUPS, 24, QL), F32),
        "mixed": ((GROUPS, GT, D), BF16),
        "xhat2": ((D, TOKENS), F32),
        "rstd2": ((1, TOKENS), F32),
        "h2": ((D + 16, TOKENS), BF16),
        "act": ((FF + 16, TOKENS), BF16),
        "gelu": ((FF, TOKENS), F32),
        "slope": ((FF, TOKENS), F32),
    }


def weights():
    return {
        "cols": ((6, D, LANES), F32),
        "qkv": ((D + 16, 6 * LANES), BF16),
        "out_t": ((D, D), BF16),
        "gu": ((D, 2 * FF), BF16),
        "gu_t": ((2 * FF, D + 16), BF16),
        "down": ((FF, D), BF16),
        "down_t": ((D, FF), BF16),
    }


def accumulators():
    return {
        "qkv": ((6, D + 16, LANES), F32),
        "out_t": ((D, D), F32),
        "gu": ((4, D + 16, LANES), F32),
        "down": ((2, FF + 16, LANES), F32),
    }


def common():
    return {
        "halves": ((2, 16, LANES), BF16),
        "heads": ((HEADS, 16, D), BF16),
        "masks": ((5, 16, CHUNK), BF16),
        "diff": ((GROUP, CHUNK), jnp.int32),
        "count": ((GROUPS, CHUNK), F32),
        "dm": ((GROUPS, GT, D), BF16),
        "x": ((D, TOKENS), F32),
        "middle": ((D, TOKENS), F32),
        "dqkv": ((GROUPS, GT, 6 * LANES), BF16),
        "g": ((D, TOKENS), F32),
        "sums": ((5, D, LANES), F32),
        "flat": ((FLAT + 8, LANES), F32),
        "tmp": ((6, FF, LANES), F32),
    }


def make_scratch():
    shapes, names = [], []
    for prefix, table in (
        ("common", common()),
        ("acc", accumulators()),
        ("s0", per_layer()),
        ("s1", per_layer()),
        ("w0", weights()),
        ("w1", weights()),
    ):
        for name, (shape, kind) in table.items():
            names.append((prefix, name))
            shapes.append(pltpu.VMEM(shape, kind))
    return names, shapes


def init_env(env, count):
    lane = lax.broadcasted_iota(jnp.int32, (GROUP, CHUNK), 1)
    sub = lax.broadcasted_iota(jnp.int32, (GROUP, CHUNK), 0)
    diff = (sub - lane) & (GROUP - 1)
    env["diff"][...] = diff
    for m in range(5):
        first = jnp.where(diff == (2 * m) % 8, 1.0, 0.0)
        second = jnp.where(diff == 2 * m + 1, 1.0, 0.0)
        env["masks"][m] = jnp.concatenate([first, second], axis=0).astype(BF16)
    sub = lax.broadcasted_iota(jnp.int32, (16, LANES), 0)
    env["halves"][0] = jnp.where(sub < 8, 1.0, 0.0).astype(BF16)
    env["halves"][1] = jnp.where(sub < 8, 0.0, 1.0).astype(BF16)
    feature = lax.broadcasted_iota(jnp.int32, (16, D), 1) // HEAD_DIM
    for h in range(HEADS):
        env["heads"][h] = jnp.where(feature == h, 1.0, 0.0).astype(BF16)
    row = lax.broadcasted_iota(jnp.int32, (GROUPS, LANES), 1)
    group = lax.broadcasted_iota(jnp.int32, (GROUPS, LANES), 0)
    mine = jnp.where(row // GROUP == group, jnp.broadcast_to(count, (GROUPS, LANES)), 0.0)
    here = lax.broadcasted_iota(jnp.int32, (LANES, CHUNK), 0)
    there = lax.broadcasted_iota(jnp.int32, (LANES, CHUNK), 1)
    pick = jnp.where(here % GROUP == there % GROUP, 1.0, 0.0).astype(BF16)
    env["count"][...] = dot(mine.astype(BF16), pick, 1, 0)


def ones_below(ref, rows):
    tail = ref.shape[0] - rows
    mark = lax.broadcasted_iota(jnp.int32, (tail, ref.shape[1]), 0) == 0
    ref[rows:, :] = jnp.where(mark, 1.0, 0.0).astype(BF16)


def kernel(
    names, place, tokens, out_grad, own, other, row_scale, count, out, in_grad, keep_out, give_out, *scratch
):
    table = {}
    for (prefix, name), ref in zip(names, scratch):
        table.setdefault(prefix, {})[name] = ref
    env, acc = table["common"], table["acc"]
    s, w = [table["s0"], table["s1"]], [table["w0"], table["w1"]]
    sums = env["sums"]

    init_env(env, count[...])
    valid_slots = count[...]
    env["dqkv"][...] = jnp.zeros_like(env["dqkv"])
    for layer in range(LAYERS):
        ones_below(s[layer]["h1"], D)
        ones_below(s[layer]["h2"], D)
        ones_below(s[layer]["act"], FF)
        gather_flat(own, other, place, layer, env["flat"])
        unpack(env["flat"], w[layer], env["tmp"])
    for slot in range(SLOTS):
        lanes = slice(slot * ROWS, (slot + 1) * ROWS)
        if slot < SEQ:
            env["x"][:, lanes] = tokens[slot].astype(F32)
            keep = jnp.where(valid_slots >= float(slot), row_scale[...], 0.0)
            env["g"][:, lanes] = out_grad[slot].astype(F32) * keep
        else:
            env["x"][:, lanes] = jnp.zeros((D, ROWS), F32)
            env["g"][:, lanes] = jnp.zeros((D, ROWS), F32)

    def put(target):
        def done(c, lanes, value):
            target[2 * c] = value[:, 0:ROWS]

            @pl.when(c < CHUNKS - 1)
            def _():
                target[2 * c + 1] = value[:, ROWS:]

        return done

    def keep(target):
        def done(c, lanes, value):
            target[:, lanes] = value

        return done

    for layer in range(LAYERS):
        state = dict(s[layer], x=env["x"], middle=env["middle"])
        forward_qkv(state, w[layer])
        forward_attention(state, env)
        last = layer == LAYERS - 1
        forward_rest(state, w[layer], put(out) if last else keep(env["x"]))
    for layer in reversed(range(LAYERS)):
        sums[...] = jnp.zeros_like(sums)
        for ref in acc.values():
            ref[...] = jnp.zeros_like(ref)
        state = dict(s[layer], g=env["g"], dm=env["dm"], dqkv=env["dqkv"])
        backward_rest(state, w[layer], acc, sums)
        backward_attention(state, env)
        backward_qkv(
            state, w[layer], acc, sums, put(in_grad) if layer == 0 else keep(env["g"])
        )
        pack(env["flat"], acc, sums, env["tmp"])
        scatter_blocks(env["flat"], place, layer, keep_out, give_out)


def run_kernel(place, tokens, out_grad, own, other, row_scale, count):
    names, scratch = make_scratch()
    full = jax.ShapeDtypeStruct((SEQ, D, ROWS), F32)
    blocks = jax.ShapeDtypeStruct(own.shape, BF16)

    def body(*refs):
        kernel(names, *refs)

    vmem = pl.BlockSpec(memory_space=pltpu.VMEM)
    return pl.pallas_call(
        body,
        out_shape=(full, full, blocks, blocks),
        in_specs=[pl.BlockSpec(memory_space=pltpu.SMEM)] + [vmem] * 6,
        out_specs=[vmem] * 4,
        scratch_shapes=scratch,
        compiler_params=pltpu.CompilerParams(vmem_limit_bytes=64 * 1024 * 1024 - 256 * 1024),
    )(place, tokens, out_grad, own, other, row_scale, count)


def halves_of_pairs(flat):
    rows = jnp.pad(flat.reshape(LAYERS, FLAT, LANES), ((0, 0), (0, BLOCK), (0, 0)))

    def blocks(skip):
        parts = [rows[:, 145 * chip + skip : 145 * chip + skip + BLOCK] for chip in range(16)]
        return jnp.stack([jnp.stack(parts[at::4]) for at in range(4)])

    return blocks(0), blocks(72)


def pairs_joined(even, odd):
    joined = []
    for chip in range(16):
        first, second = even[chip % 4, chip // 4], odd[chip % 4, chip // 4]
        seam = jnp.concatenate([first[:, 72:73, 0:64], second[:, 0:1, 64:]], axis=2)
        joined += [first[:, 0:72], seam, second[:, 1:73]]
    return jnp.concatenate(joined, axis=1).reshape(LAYERS, PSIZE)


def swap_along(x, axis, bit):
    pairs = [(i, i ^ bit) for i in range(lax.axis_size(axis))]
    return lax.ppermute(x, axis, pairs)


def gather_pairs(flat_params):
    size = flat_params.shape[1]
    room = BLOCK * LANES - size
    part = jnp.where(
        lax.axis_index("core") == 0,
        jnp.pad(flat_params, ((0, 0), (0, room))),
        jnp.pad(flat_params, ((0, 0), (64, room - 64))),
    ).reshape(1, LAYERS, BLOCK, LANES)
    for bit in (2, 1):
        part = jnp.concatenate([part, swap_along(part, "z", bit)], axis=0)
    own = lax.all_gather(part, ("x", "y"), axis=0, tiled=False)
    return own, swap_along(own, "core", 1)


def reduce_pairs(keep, give, size):
    got = swap_along(give, "core", 1)
    part = (keep.astype(F32) + got.astype(F32)).astype(BF16)
    part = lax.all_to_all(part, ("x", "y"), 0, 0, tiled=True)
    part = jnp.sum(part.astype(F32), axis=0)
    z = lax.axis_index("z")
    for bit in (2, 1):
        high = (z // bit) % 2
        stay = lax.dynamic_slice_in_dim(part, high * bit, bit, 0)
        go = lax.dynamic_slice_in_dim(part, (1 - high) * bit, bit, 0).astype(BF16)
        part = stay + swap_along(go, "z", bit).astype(F32)
    total = part.reshape(LAYERS, BLOCK * LANES)
    return jnp.where(
        lax.axis_index("core") == 0, total[:, 0:size], total[:, 64 : 64 + size]
    )


def body(axes, tokens, out_grad, flat_params, feat_count, table_ids, table_counts):
    four = "core" in axes
    counts_float = table_counts.astype(F32)
    table_index = jnp.arange(table_counts.shape[0], dtype=jnp.int32)
    match = (table_ids[None, :] == table_index[:, None]).astype(F32)
    row_count = jnp.sum(match * counts_float[:, None], axis=0)
    row_scale = jnp.sqrt(jnp.mean(counts_float) / row_count)[None, :]
    count = feat_count.astype(F32)[None, :]
    if four:
        place = jnp.stack([lax.axis_index("z"), lax.axis_index("core")]).astype(jnp.int32)
        own, other = gather_pairs(flat_params)
    else:
        place = jnp.zeros((2,), jnp.int32)
        own, other = halves_of_pairs(lax.all_gather(flat_params, axes, axis=1, tiled=True))
        turn = jnp.array([0, 2, 1, 3])
        own, other = own[:, turn], other[:, turn]
    turned = jnp.transpose(tokens, (1, 2, 0))
    turned_grad = jnp.transpose(out_grad, (1, 2, 0))
    results = [
        run_kernel(
            place,
            turned[:, :, at : at + ROWS],
            turned_grad[:, :, at : at + ROWS],
            own,
            other,
            row_scale[:, at : at + ROWS],
            count[:, at : at + ROWS],
        )
        for at in range(0, tokens.shape[0], ROWS)
    ]
    out, in_grad, keep, give = results[0]
    if len(results) > 1:
        out = jnp.concatenate([r[0] for r in results], axis=2)
        in_grad = jnp.concatenate([r[1] for r in results], axis=2)
        keep = sum(r[2].astype(F32) for r in results)
        give = sum(r[3].astype(F32) for r in results)
    if four:
        grads = reduce_pairs(keep, give, flat_params.shape[1])
    else:
        flat = pairs_joined(keep.astype(F32), give.astype(F32))
        grads = lax.psum_scatter(flat, axes, scatter_dimension=1, tiled=True)
    return jnp.transpose(out, (2, 0, 1)), jnp.transpose(in_grad, (2, 0, 1)), grads


def solution(mesh):
    axes = mesh.axis_names
    if tuple(mesh.devices.shape) == (8, 4):
        axes = ("z", "x", "y", "core")
        mesh = jax.sharding.Mesh(mesh.devices.reshape(4, 2, 2, 2), axes)
    rows = P(axes, None, None)
    placed = (rows, rows, P(None, axes), P(axes), P(axes), P())
    return jax.shard_map(
        functools.partial(body, axes),
        mesh=mesh,
        in_specs=placed,
        out_specs=(rows, rows, P(None, axes)),
        check_vma=False,
    )
```

```python
import functools
import math

import jax
import jax.numpy as jnp
from jax import lax
from jax.experimental import pallas as pl
from jax.experimental.pallas import tpu as pltpu
from jax.sharding import PartitionSpec as P

D = 192
FF = 256
HEADS = 8
HEAD_DIM = 24
SEQ = 17
LAYERS = 2
PSIZE = 296960
ROWS = 128
SLOTS = 18
LANES = 128
UNROLL = 4
DEPTH = 6
BAND = 32
STEPS = 3
GROUP = 8
GROUPS = ROWS // GROUP
GT = SLOTS * GROUP
QL = HEADS * GT
TOKENS = SLOTS * ROWS
CHUNK = 2 * ROWS
CHUNKS = TOKENS // CHUNK
HALVES = (slice(0, ROWS), slice(ROWS, CHUNK))
FLAT = PSIZE // LANES
BLOCK = 80
EPS = 1e-05
SCALE = 1.0 / math.sqrt(HEAD_DIM)
F32 = jnp.float32
BF16 = jnp.bfloat16


def dot(a, b, ca, cb):
    return lax.dot_general(a, b, (((ca,), (cb,)), ((), ())), preferred_element_type=F32)


def lane_half(shape):
    return lax.broadcasted_iota(jnp.int32, shape, len(shape) - 1) < 64


def swap(x):
    return pltpu.roll(x, 64, x.ndim - 1)


def low_half(x):
    return jnp.where(lane_half(x.shape), x, 0.0)


def splice(a, b):
    return swap(jnp.where(lane_half(a.shape), b, a))


def after(a, b):
    return jnp.where(lane_half(a.shape), a, swap(b))


def wide(column):
    return jnp.concatenate([column, column], axis=1)


def gather_flat(own, other, place, layer, flat):
    z, core = place[0], place[1]
    for chip in range(FLAT // 145):
        turn = z ^ (chip // 4)
        at = (turn & 1) * 2 + turn // 2
        mine = own[chip % 4, at, layer].astype(F32)
        theirs = other[chip % 4, at, layer].astype(F32)
        first = jnp.where(core == 0, mine, theirs)
        second = jnp.where(core == 0, theirs, mine)
        base = 145 * chip
        flat[pl.ds(base, BLOCK), :] = first
        flat[pl.ds(base + 72, BLOCK), :] = second
        flat[pl.ds(base + 72, 1), :] = jnp.where(
            lane_half((1, LANES)), first[72:73], second[0:1]
        )


def unpack(flat, w, tmp):
    def rows(start, count, stride):
        return flat[pl.ds(start, count, stride=stride), :]

    def row(index):
        return flat[pl.ds(index, 1), :]

    def pair_row(a, b):
        return jnp.concatenate([a, b], axis=1)

    vectors = [
        pair_row(row(0), low_half(row(1))),
        pair_row(splice(row(1), row(2)), low_half(swap(row(2)))),
        pair_row(row(1158), low_half(row(1159))),
        pair_row(splice(row(1159), row(1160)), low_half(swap(row(1160)))),
        pair_row(row(1161), low_half(row(1162))),
        pair_row(splice(row(2318), row(2319)), low_half(swap(row(2319)))),
    ]
    index = lax.broadcasted_iota(jnp.int32, (16, 2 * LANES), 0)
    stacked = jnp.zeros((16, 2 * LANES), F32)
    for i, vector in enumerate(vectors):
        stacked = jnp.where(index == i, vector, stacked)
    stacked = stacked.astype(BF16)
    for i in range(6):
        pick = jnp.where(index[:, 0:LANES] == i, 1.0, 0.0).astype(BF16)
        w["cols"][i] = dot(stacked, pick, 0, 0)[0:D]

    e = [rows(3 + j, 96, 9) for j in range(9)]
    even = (e[0], low_half(e[1]), splice(e[1], e[2]), low_half(swap(e[2])), e[3], low_half(e[4]))
    odd = (
        splice(e[4], e[5]),
        low_half(swap(e[5])),
        e[6],
        low_half(e[7]),
        splice(e[7], e[8]),
        low_half(swap(e[8])),
    )
    zero_row = jnp.zeros((1, LANES), F32)
    bias = (
        row(867),
        low_half(row(868)),
        zero_row,
        zero_row,
        splice(row(868), row(869)),
        low_half(swap(row(869))),
    )
    first_row = lax.broadcasted_iota(jnp.int32, (16, LANES), 0) == 0
    for j in range(6):
        tmp[j % 2, pl.ds(0, 96, stride=2), :] = even[j]
        tmp[j % 2, pl.ds(1, 96, stride=2), :] = odd[j]
        w["qkv"][0:D, j * LANES : (j + 1) * LANES] = tmp[j % 2, 0:D, :].astype(BF16)
        w["qkv"][D : D + 16, j * LANES : (j + 1) * LANES] = jnp.where(
            first_row, jnp.broadcast_to(bias[j], (16, LANES)), 0.0
        ).astype(BF16)

    e = [rows(870 + j, 96, 3) for j in range(3)]
    tmp[0, pl.ds(0, 96, stride=2), :] = e[0]
    tmp[1, pl.ds(0, 96, stride=2), :] = low_half(e[1])
    tmp[0, pl.ds(1, 96, stride=2), :] = splice(e[1], e[2])
    tmp[1, pl.ds(1, 96, stride=2), :] = low_half(swap(e[2]))
    w_out = jnp.concatenate([tmp[0, 0:D, :], tmp[1, 0:D, :]], axis=1)
    w["out_t"][...] = jnp.transpose(w_out.astype(BF16))[0:D]

    g = [rows(1162 + j, 192, 4) for j in range(5)]
    tiles = [splice(g[j], g[j + 1]) for j in range(4)]
    gate_up = jnp.concatenate(tiles, axis=1)
    w["gu"][...] = gate_up.astype(BF16)
    bias_row = jnp.concatenate(
        [splice(row(1930 + j), row(1931 + j)) for j in range(4)], axis=1
    )
    bias_rows = jnp.where(
        lax.broadcasted_iota(jnp.int32, (64, 2 * FF), 0) == 0,
        jnp.broadcast_to(bias_row, (64, 2 * FF)),
        0.0,
    )
    w["gu_t"][...] = jnp.transpose(jnp.concatenate([gate_up, bias_rows], axis=0).astype(BF16))[
        :, 0 : D + 16
    ]

    e = [rows(1934 + j, 128, 3) for j in range(4)]
    tmp[0, pl.ds(0, 128, stride=2), :] = splice(e[0], e[1])
    tmp[1, pl.ds(0, 128, stride=2), :] = low_half(swap(e[1]))
    tmp[0, pl.ds(1, 128, stride=2), :] = e[2]
    tmp[1, pl.ds(1, 128, stride=2), :] = low_half(e[3])
    w_down = jnp.concatenate([tmp[0, 0:FF, :], tmp[1, 0:FF, :]], axis=1)
    w["down"][...] = w_down[:, 0:D].astype(BF16)
    w["down_t"][...] = jnp.transpose(w_down.astype(BF16))[0:D]


def row_of(columns):
    turned = jnp.sum(jnp.transpose(columns), axis=0, keepdims=True)
    return turned[:, 0:LANES], jnp.concatenate(
        [turned[:, LANES:D], jnp.zeros((1, LANES - (D - LANES)), F32)], axis=1
    )


def pack(flat, acc, sums, tmp):
    def put(start, count, stride, value):
        flat[pl.ds(start, count, stride=stride), :] = value

    def put_row(index, value):
        flat[pl.ds(index, 1), :] = value

    def down(j, start, count, stride):
        return acc["down"][j, pl.ds(start, count, stride=stride), :]

    g1 = row_of(sums[0])
    b1 = row_of(sums[1])
    g2 = row_of(sums[2])
    b2 = row_of(sums[3])
    bo = row_of(sums[4])
    put_row(0, g1[0])
    put_row(1, after(g1[1], b1[0]))
    put_row(2, splice(b1[0], b1[1]))

    even = [acc["qkv"][j, pl.ds(0, 96, stride=2), :] for j in range(6)]
    odd = [acc["qkv"][j, pl.ds(1, 96, stride=2), :] for j in range(6)]
    put(3, 96, 9, even[0])
    put(4, 96, 9, after(even[1], even[2]))
    put(5, 96, 9, splice(even[2], even[3]))
    put(6, 96, 9, even[4])
    put(7, 96, 9, after(even[5], odd[0]))
    put(8, 96, 9, splice(odd[0], odd[1]))
    put(9, 96, 9, odd[2])
    put(10, 96, 9, after(odd[3], odd[4]))
    put(11, 96, 9, splice(odd[4], odd[5]))
    bias = [acc["qkv"][j, D : D + 1, :] for j in range(6)]
    put_row(867, bias[0])
    put_row(868, after(bias[1], bias[4]))
    put_row(869, splice(bias[4], bias[5]))

    w_out = jnp.transpose(
        jnp.concatenate([acc["out_t"][...], jnp.zeros((64, D), F32)], axis=0)
    )
    tmp[0, 0:D, :] = w_out[:, 0:LANES]
    tmp[1, 0:D, :] = w_out[:, LANES:]
    even = [tmp[j, pl.ds(0, 96, stride=2), :] for j in range(2)]
    odd = [tmp[j, pl.ds(1, 96, stride=2), :] for j in range(2)]
    put(870, 96, 3, even[0])
    put(871, 96, 3, after(even[1], odd[0]))
    put(872, 96, 3, splice(odd[0], odd[1]))
    put_row(1158, bo[0])
    put_row(1159, after(bo[1], g2[0]))
    put_row(1160, splice(g2[0], g2[1]))
    put_row(1161, b2[0])

    gu = [acc["gu"][j, 0 : D + 8, :] for j in range(4)]
    put_row(1162, after(b2[1], gu[0][0:1]))
    put(1166, 192, 4, splice(gu[3][0:192], acc["gu"][0, pl.ds(1, 192), :]))
    for j in range(1, 4):
        joined = splice(gu[j - 1], gu[j])
        put(1162 + j, 192, 4, joined[0:192])
        put_row(1930 + j, joined[192:193])
    put_row(1934, splice(gu[3][192:193], acc["down"][0, 0:1, :]))

    w0e, w1e = down(0, 0, 128, 2), down(1, 0, 128, 2)
    w0o, w1o = down(0, 1, 128, 2), down(1, 1, 128, 2)
    put(1935, 128, 3, splice(w0e, w1e))
    put(1936, 128, 3, w0o)
    put(1937, 128, 3, after(w1o, down(0, 2, 128, 2)))
    put_row(2319, splice(acc["down"][0, FF : FF + 1, :], acc["down"][1, FF : FF + 1, :]))


def scatter_blocks(flat, place, layer, keep, give):
    core = place[1]
    for chip in range(FLAT // 145):
        first = flat[pl.ds(145 * chip, BLOCK), :]
        second = flat[pl.ds(145 * chip + 72, BLOCK), :]
        keep[chip % 4, chip // 4, layer] = jnp.where(core == 0, first, second).astype(BF16)
        give[chip % 4, chip // 4, layer] = jnp.where(core == 0, second, first).astype(BF16)


def norm(x, gain, bias):
    centre = x - jnp.sum(x, axis=0, keepdims=True) * (1.0 / D)
    variance = jnp.sum(centre * centre, axis=0, keepdims=True) * (1.0 / D)
    rstd = lax.rsqrt(variance + EPS)
    xhat = centre * rstd
    return xhat, rstd, (xhat * gain + bias).astype(BF16)


def norm_back(grad, xhat, rstd, gain):
    e = gain * grad
    mean_e = jnp.sum(e, axis=0, keepdims=True) * (1.0 / D)
    mean_ex = jnp.sum(e * xhat, axis=0, keepdims=True) * (1.0 / D)
    return rstd * (e - mean_e - xhat * mean_ex)


def fold(x):
    return x[:, 0:LANES] + x[:, LANES:]


def gelu_parts(gate):
    z = gate * (1.0 / math.sqrt(2.0))
    cdf = 0.5 * lax.erf(z) + 0.5
    bell = jnp.exp2(z * z * (-1.0 / math.log(2.0)))
    return cdf, cdf + (z * bell) * (1.0 / math.sqrt(math.pi))


def to_groups(x):
    n = x.shape[-1]
    x = x.reshape(2, GROUPS, GROUP, n)
    return jnp.concatenate([x[0][:, None], x[1][:, None]], axis=1).reshape(
        GROUPS, 2 * GROUP, n
    )


def from_groups(x):
    n = x.shape[-1]
    x = x.reshape(GROUPS, 2, GROUP, n)
    return jnp.concatenate([x[:, 0], x[:, 1]], axis=0).reshape(CHUNK, n)


def lanes_of(c):
    return pl.ds(pl.multiple_of(c * CHUNK, CHUNK), CHUNK)


def group_rows(c):
    return pl.ds(pl.multiple_of(c * 2 * GROUP, 2 * GROUP), 2 * GROUP)


def skewed(stages):
    def steps(i, carry):
        held = {}
        for tick in range(STEPS + len(stages) - 1):
            for j, stage in enumerate(stages):
                u = tick - j
                if 0 <= u < STEPS:
                    held[u] = stage(i * STEPS + u, u, held.get(u))
        return carry

    lax.fori_loop(0, CHUNKS // STEPS, steps, 0)


def view(ref, c, u, rows=None):
    lanes = lanes_of(c) if ref.shape[1] == TOKENS else pl.ds(u * CHUNK, CHUNK)
    return ref.at[slice(0, ref.shape[0] if rows is None else rows), lanes]


def project_stages(s, w):
    def project(c, u, _):
        lows = []
        for half in HALVES:
            xhat, rstd, low = norm(
                view(s["x"], c, u).at[:, half][...], w["cols"][0], w["cols"][1]
            )
            view(s["xhat1"], c, u).at[:, half][...] = xhat
            view(s["rstd1"], c, u).at[:, half][...] = rstd
            lows.append(low)
        view(s["h1"], c, u, D)[...] = jnp.concatenate(lows, axis=1)
        return dot(view(s["h1"], c, u)[...], w["qkv"][...], 0, 0)

    def keep(c, u, qkv):
        place = group_rows(c)
        s["q"][:, place, :] = to_groups(qkv[:, 0:D]).astype(BF16)
        for name, start in (("k", 256), ("v", 512)):
            part = qkv[:, start : start + D].reshape(2, GROUPS, GROUP, D)
            turned = jnp.concatenate(
                [
                    pltpu.roll(part[t], lax.rem(2 * c + t, GROUP), 1)[:, None]
                    for t in range(2)
                ],
                axis=1,
            )
            s[name][:, place, :] = turned.reshape(GROUPS, 2 * GROUP, D).astype(BF16)

    return project, keep


def spread(values, masks):
    n = values.shape[1]
    doubled = [
        jnp.concatenate([values[8 * a : 8 * a + 8], values[8 * a : 8 * a + 8]], axis=0).astype(BF16)
        for a in range(3)
    ]
    parts = [doubled[a] * masks[m][:, 0:n] for a in range(2) for m in range(4)]
    parts.append(doubled[2] * masks[4][:, 0:n])
    return jnp.concatenate(parts, axis=0)


def collect(scores, bits):
    n = scores.shape[1]
    bits = [bit[:, 0:n] for bit in bits]
    out = []
    for a in range(2):
        level = [scores[64 * a + 8 * j : 64 * a + 8 * j + 8] for j in range(8)]
        for bit in bits:
            level = [
                jnp.where(bit, level[2 * i + 1], level[2 * i]) for i in range(len(level) // 2)
            ]
        out.append(level[0])
    out.append(scores[128:136])
    return out


def blocks_of(turned, t, halves):
    first = turned[48 * t : 48 * t + 16]
    middle = turned[48 * t + 16 : 48 * t + 32]
    last = turned[48 * t + 32 : 48 * t + 48]
    none = jnp.zeros_like(first)
    return jnp.concatenate(
        [
            jnp.concatenate([first, none], axis=1),
            jnp.concatenate([middle * halves[0], middle * halves[1]], axis=1),
            jnp.concatenate([none, last], axis=1),
        ],
        axis=0,
    )


def padded(block, t):
    parts = [block]
    if t > 0:
        parts.insert(0, jnp.zeros((48 * t, block.shape[1]), BF16))
    if t < 3:
        parts.append(jnp.zeros((48 * (3 - t), block.shape[1]), BF16))
    return jnp.concatenate(parts, axis=0)


def tail_of(rows, heads):
    return jnp.concatenate([rows * heads[h, 0:1, :] for h in range(HEADS)], axis=0)


def heads_joined(tiles, tail, heads, scale=None):
    main = []
    for tile in tiles:
        main += [tile[0:HEAD_DIM, 0:LANES], tile[HEAD_DIM:, LANES:]]
    main = jnp.concatenate(main, axis=0)
    if scale is not None:
        main, tail = main * scale, tail * scale
    main = jnp.transpose(main.astype(BF16))
    tail = tail.astype(BF16)
    last = tail[0:16] * heads[0, 0:1, :]
    for h in range(1, HEADS):
        last += tail[16 * h : 16 * h + 16] * heads[h, 0:1, :]
    return main, last


def softmax(kept, diff, limit):
    n = kept[0].shape[1]
    own = diff[:, 0:n]
    limit = limit[:, 0:n]
    slot = own.astype(F32)
    shown = [
        jnp.where(slot <= limit, kept[0] * SCALE, -1e9),
        jnp.where(slot + 8.0 <= limit, kept[1] * SCALE, -1e9),
        jnp.where(own == 0, jnp.where(limit >= 16.0, kept[2] * SCALE, -1e9), -3e38),
    ]
    top = jnp.max(jnp.maximum(jnp.maximum(shown[0], shown[1]), shown[2]), axis=0, keepdims=True)
    shown = [jnp.exp(part - top) for part in shown]
    inverse = 1.0 / jnp.sum(shown[0] + shown[1] + shown[2], axis=0, keepdims=True)
    return jnp.concatenate([part * inverse for part in shown], axis=0)


def staged(items, first, second):
    waiting = []
    for item in items:
        waiting.append((item, first(item)))
        if len(waiting) > DEPTH:
            second(*waiting.pop(0))
    for entry in waiting:
        second(*entry)


def forward_attention(s, env):
    diff = env["diff"][...]
    bits = [(diff & (1 << i)) != 0 for i in range(3)]
    halves = [env["halves"][i] for i in range(2)]

    def step(i, carry):
        state = {}

        def load(u):
            g = i * UNROLL + u
            queries, values = s["q"][g], s["v"][g]
            state[u] = {
                "g": g,
                "queries": queries,
                "keys": s["k"][g],
                "turned": jnp.transpose(queries)[:, 0:LANES],
                "values": values,
                "turned_values": jnp.transpose(values),
                "count": env["count"][pl.ds(g, 1), :],
                "tiles": [],
            }

        def scores(item):
            u, t = item
            if t == 0:
                load(u)
            at = state[u]
            if t < 4:
                return dot(at["keys"], padded(blocks_of(at["turned"], t, halves), t), 1, 0)
            return dot(at["keys"], tail_of(at["queries"][LANES:GT], env["heads"]), 1, 1)

        def mix(item, products):
            u, t = item
            at = state[u]
            attention = softmax(collect(products, bits), diff, at["count"])
            s["att"][at["g"], :, t * CHUNK : min((t + 1) * CHUNK, QL)] = attention
            low = spread(attention, env["masks"])
            if t < 4:
                at["tiles"].append(dot(at["turned_values"][48 * t : 48 * t + 48], low, 1, 0))
                return
            tail = dot(low, at["values"], 0, 0)
            main, last = heads_joined(at["tiles"], tail, env["heads"])
            s["mixed"][at["g"], 0:LANES, :] = main
            s["mixed"][at["g"], LANES:GT, :] = last

        staged([(u, t) for u in range(UNROLL) for t in range(5)], scores, mix)
        return carry

    lax.fori_loop(0, GROUPS // UNROLL, step, 0)


def rest_stages(s, w, done):
    def attended(c, u, _):
        mixed = from_groups(s["mixed"][:, group_rows(c), :].astype(F32)).astype(BF16)
        return dot(w["out_t"][...], mixed, 1, 1)

    def normed(c, u, product):
        lows = []
        for half in HALVES:
            middle = view(s["x"], c, u).at[:, half][...] + (product[:, half] + w["cols"][2])
            view(s["middle"], c, u).at[:, half][...] = middle
            xhat, rstd, low = norm(middle, w["cols"][3], w["cols"][4])
            view(s["xhat2"], c, u).at[:, half][...] = xhat
            view(s["rstd2"], c, u).at[:, half][...] = rstd
            lows.append(low)
        view(s["h2"], c, u, D)[...] = jnp.concatenate(lows, axis=1)
        return dot(w["gu_t"][...], view(s["h2"], c, u)[...], 1, 0)

    def gated(c, u, gate_up):
        acts = []
        for r in range(0, FF, BAND):
            band = pl.ds(r, BAND)
            gate, up = gate_up[r : r + BAND], gate_up[FF + r : FF + r + BAND]
            cdf, slope = gelu_parts(gate)
            gelu = gate * cdf
            view(s["gelu"], c, u).at[band][...] = gelu
            view(s["slope"], c, u).at[band][...] = slope * up
            acts.append((gelu * up).astype(BF16))
        act = jnp.concatenate(acts, axis=0)
        view(s["act"], c, u, FF)[...] = act
        return dot(w["down_t"][...], act, 1, 0)

    def finish(c, u, product):
        for i, half in enumerate(HALVES):
            value = view(s["middle"], c, u).at[:, half][...]
            done(c, u, i, value + (product[:, half] + w["cols"][5]))

    return attended, normed, gated, finish


def add_tiles(ref, value):
    for j in range(ref.shape[0]):
        ref[j] += value[:, j * LANES : (j + 1) * LANES]


def add_narrow(ref, value):
    ref[0] += value[:, 0:LANES]
    ref[1, :, 0 : D - LANES] += value[:, LANES:D]


def rest_back_stages(s, w, acc, sums):
    def down(c, u, _):
        branch = view(s["g"], c, u)[...].astype(BF16)
        return dot(view(s["act"], c, u)[...], branch, 1, 1), dot(w["down"][...], branch, 1, 0)

    def gate_up(c, u, held):
        grad_down, d_act = held
        add_narrow(acc["down"], grad_down)
        gates, ups = [], []
        for r in range(0, FF, BAND):
            band = pl.ds(r, BAND)
            part = d_act[r : r + BAND]
            gates.append((part * view(s["slope"], c, u).at[band][...]).astype(BF16))
            ups.append((part * view(s["gelu"], c, u).at[band][...]).astype(BF16))
        d_gate_up = jnp.concatenate(gates + ups, axis=0)
        return dot(view(s["h2"], c, u)[...], d_gate_up, 1, 1), dot(w["gu"][...], d_gate_up, 1, 0)

    def normed(c, u, held):
        grad_gu, d_normed = held
        add_tiles(acc["gu"], grad_gu)
        lows = []
        for half in HALVES:
            xhat = view(s["xhat2"], c, u).at[:, half][...]
            part = d_normed[:, half]
            sums[2] += part * xhat
            sums[3] += part
            g = view(s["g"], c, u).at[:, half]
            d_middle = g[...] + norm_back(
                part, xhat, view(s["rstd2"], c, u).at[:, half][...], w["cols"][3]
            )
            g[...] = d_middle
            low = d_middle.astype(BF16)
            sums[4] += low.astype(F32)
            lows.append(low)
        d_attended = jnp.concatenate(lows, axis=1)
        mixed = from_groups(s["mixed"][:, group_rows(c), :].astype(F32)).astype(BF16)
        return dot(d_attended, w["out_t"][...], 0, 0), dot(d_attended, mixed, 1, 0)

    def finish(c, u, held):
        d_mixed, grad_out = held
        s["dm"][:, group_rows(c), :] = to_groups(d_mixed).astype(BF16)
        acc["out_t"][...] += grad_out

    return down, gate_up, normed, finish


def backward_attention(s, env):
    diff = env["diff"][...]
    bits = [(diff & (1 << i)) != 0 for i in range(3)]
    halves = [env["halves"][i] for i in range(2)]

    def step(i, carry):
        state = {}

        def load(u):
            g = i * UNROLL + u
            queries, keys, grads = s["q"][g], s["k"][g], s["dm"][g]
            state[u] = {
                "g": g,
                "queries": queries,
                "grads": grads,
                "keys": keys,
                "values": s["v"][g],
                "turned": jnp.transpose(queries)[:, 0:LANES],
                "turned_grads": jnp.transpose(grads)[:, 0:LANES],
                "turned_keys": jnp.transpose(keys),
                "dq": [],
                "dk": [],
                "dv": [],
            }

        def products(item):
            u, t = item
            if t == 0:
                load(u)
            at = state[u]
            if t < 4:
                block = blocks_of(at["turned_grads"], t, halves)
                return block, dot(at["values"], padded(block, t), 1, 0)
            block = tail_of(at["grads"][LANES:GT], env["heads"])
            return block, dot(at["values"], block, 1, 1)

        def back(item, result):
            u, t = item
            at = state[u]
            grad_block, product = result
            attention = s["att"][at["g"], :, t * CHUNK : min((t + 1) * CHUNK, QL)]
            weighted = attention * jnp.concatenate(collect(product, bits), axis=0)
            total = jnp.sum(weighted, axis=0, keepdims=True)
            d_score = spread(weighted - attention * total, env["masks"])
            low = spread(attention, env["masks"])
            if t < 4:
                at["dv"].append(dot(grad_block, low, 1, 1))
                at["dk"].append(dot(blocks_of(at["turned"], t, halves), d_score, 1, 1))
                at["dq"].append(dot(at["turned_keys"][48 * t : 48 * t + 48], d_score, 1, 0))
                return
            d_values = dot(low, grad_block, 1, 0)
            d_keys = dot(d_score, tail_of(at["queries"][LANES:GT], env["heads"]), 1, 0)
            finish(at, d_values, d_keys, dot(d_score, at["keys"], 0, 0))

        def finish(at, d_values, d_keys, tail):
            g = at["g"]
            main, last = heads_joined(at["dq"], tail, env["heads"], SCALE)
            s["dqkv"][g, 0:LANES, 0:D] = main
            s["dqkv"][g, LANES:GT, 0:D] = last
            for parts, own, start, scale in (
                (at["dk"], d_keys, 256, SCALE),
                (at["dv"], d_values, 512, 1.0),
            ):
                value = jnp.transpose(jnp.concatenate(parts, axis=0)) + own
                slots = (value * scale).reshape(SLOTS, GROUP, D)
                turned = [
                    slots[k] if k % GROUP == 0 else pltpu.roll(slots[k], GROUP - k % GROUP, 0)
                    for k in range(SLOTS)
                ]
                s["dqkv"][g, :, start : start + D] = jnp.concatenate(turned, axis=0).astype(BF16)

        staged([(u, t) for u in range(UNROLL) for t in range(5)], products, back)
        return carry

    lax.fori_loop(0, GROUPS // UNROLL, step, 0)


def project_back_stages(s, w, acc, sums, done):
    def products(c, u, _):
        d_qkv = from_groups(s["dqkv"][:, group_rows(c), :].astype(F32)).astype(BF16)
        return dot(view(s["h1"], c, u)[...], d_qkv, 1, 0), dot(w["qkv"][0:D, :], d_qkv, 1, 1)

    def finish(c, u, held):
        grad_qkv, d_normed = held
        add_tiles(acc["qkv"], grad_qkv)
        for i, half in enumerate(HALVES):
            xhat = view(s["xhat1"], c, u).at[:, half][...]
            part = d_normed[:, half]
            sums[0] += part * xhat
            sums[1] += part
            back = norm_back(part, xhat, view(s["rstd1"], c, u).at[:, half][...], w["cols"][0])
            done(c, u, i, view(s["g"], c, u).at[:, half][...] + back)

    return products, finish


def per_layer(layer):
    room = TOKENS if layer < LAYERS - 1 else STEPS * CHUNK
    return {
        "xhat1": ((D, TOKENS), F32),
        "rstd1": ((1, TOKENS), F32),
        "h1": ((D + 16, TOKENS), BF16),
        "q": ((GROUPS, GT, D), BF16),
        "k": ((GROUPS, GT, D), BF16),
        "v": ((GROUPS, GT, D), BF16),
        "att": ((GROUPS, 24, QL), F32),
        "mixed": ((GROUPS, GT, D), BF16),
        "xhat2": ((D, room), F32),
        "rstd2": ((1, room), F32),
        "h2": ((D + 16, room), BF16),
        "act": ((FF + 16, room), BF16),
        "gelu": ((FF, room), F32),
        "slope": ((FF, room), F32),
    }


def weights():
    return {
        "cols": ((6, D, LANES), F32),
        "qkv": ((D + 16, 6 * LANES), BF16),
        "out_t": ((D, D), BF16),
        "gu": ((D, 2 * FF), BF16),
        "gu_t": ((2 * FF, D + 16), BF16),
        "down": ((FF, D), BF16),
        "down_t": ((D, FF), BF16),
    }


def accumulators():
    return {
        "qkv": ((6, D + 16, LANES), F32),
        "out_t": ((D, D), F32),
        "gu": ((4, D + 16, LANES), F32),
        "down": ((2, FF + 16, LANES), F32),
        "sums": ((5, D, LANES), F32),
    }


def common():
    full = (SEQ, D, ROWS)
    blocks = (4, 4, LAYERS, BLOCK, LANES)
    return {
        "halves": ((2, 16, LANES), BF16),
        "heads": ((HEADS, 16, D), BF16),
        "masks": ((5, 16, CHUNK), BF16),
        "diff": ((GROUP, CHUNK), jnp.int32),
        "count": ((GROUPS, CHUNK), F32),
        "dm": ((GROUPS, GT, D), BF16),
        "dqkv": ((GROUPS, GT, 6 * LANES), BF16),
        "x": ((D, TOKENS), F32),
        "middle": ((D, STEPS * CHUNK), F32),
        "g": ((D, TOKENS), F32),
        "flat": ((FLAT + 8, LANES), F32),
        "tmp": ((2, FF, LANES), F32),
        "tokens": (full, BF16),
        "out_grad": (full, BF16),
        "own": (blocks, BF16),
        "other": (blocks, BF16),
        "out": ((SLOTS, D, ROWS), F32),
        "in_grad": ((SLOTS, D, ROWS), F32),
        "keep": (blocks, BF16),
        "give": (blocks, BF16),
    }


def make_scratch():
    shapes, names = [], []
    for prefix, table in (
        ("common", common()),
        ("acc0", accumulators()),
        ("acc1", accumulators()),
        ("s0", per_layer(0)),
        ("s1", per_layer(1)),
        ("w0", weights()),
        ("w1", weights()),
    ):
        for name, (shape, kind) in table.items():
            names.append((prefix, name))
            shapes.append(pltpu.VMEM(shape, kind))
    return names, shapes + [pltpu.SemaphoreType.DMA((10,))]


def init_env(env, count):
    lane = lax.broadcasted_iota(jnp.int32, (GROUP, CHUNK), 1)
    sub = lax.broadcasted_iota(jnp.int32, (GROUP, CHUNK), 0)
    diff = (sub - lane) & (GROUP - 1)
    env["diff"][...] = diff
    for m in range(5):
        first = jnp.where(diff == (2 * m) % 8, 1.0, 0.0)
        second = jnp.where(diff == 2 * m + 1, 1.0, 0.0)
        env["masks"][m] = jnp.concatenate([first, second], axis=0).astype(BF16)
    sub = lax.broadcasted_iota(jnp.int32, (16, LANES), 0)
    env["halves"][0] = jnp.where(sub < 8, 1.0, 0.0).astype(BF16)
    env["halves"][1] = jnp.where(sub < 8, 0.0, 1.0).astype(BF16)
    feature = lax.broadcasted_iota(jnp.int32, (16, D), 1) // HEAD_DIM
    for h in range(HEADS):
        env["heads"][h] = jnp.where(feature == h, 1.0, 0.0).astype(BF16)
    row = lax.broadcasted_iota(jnp.int32, (GROUPS, LANES), 1)
    group = lax.broadcasted_iota(jnp.int32, (GROUPS, LANES), 0)
    mine = jnp.where(row // GROUP == group, jnp.broadcast_to(count, (GROUPS, LANES)), 0.0)
    here = lax.broadcasted_iota(jnp.int32, (LANES, CHUNK), 0)
    there = lax.broadcasted_iota(jnp.int32, (LANES, CHUNK), 1)
    pick = jnp.where(here % GROUP == there % GROUP, 1.0, 0.0).astype(BF16)
    env["count"][...] = dot(mine.astype(BF16), pick, 1, 0)


def ones_below(ref, rows):
    tail = ref.shape[0] - rows
    mark = lax.broadcasted_iota(jnp.int32, (tail, ref.shape[1]), 0) == 0
    ref[rows:, :] = jnp.where(mark, 1.0, 0.0).astype(BF16)


def scales(ids, table_counts):
    counts = table_counts.astype(F32)
    tables = counts.shape[1]
    high = jnp.floor(counts * (1.0 / 32.0))
    table = lax.broadcasted_iota(jnp.int32, (tables, ROWS), 0)
    match = jnp.where(table == ids, 1.0, 0.0).astype(BF16)

    def pick(values):
        return dot(jnp.broadcast_to(values, (8, tables)).astype(BF16), match, 1, 0)[0:1]

    mine = 32.0 * pick(high) + pick(counts - 32.0 * high)
    return jnp.sqrt(jnp.sum(counts, axis=1, keepdims=True) * (1.0 / tables) / mine)


def kernel(names, four, *refs):
    inputs, outputs, scratch, sems = refs[0:7], refs[7:11], refs[11:-1], refs[-1]
    tokens, out_grad, own, other, feat_count, table_ids, table_counts = inputs
    out, in_grad, keep_out, give_out = outputs
    table = {}
    for (prefix, name), ref in zip(names, scratch):
        table.setdefault(prefix, {})[name] = ref
    env = table["common"]
    acc = [table["acc0"], table["acc1"]]
    s, w = [table["s0"], table["s1"]], [table["w0"], table["w1"]]
    sums = [part["sums"] for part in acc]
    place = (lax.axis_index("z"), lax.axis_index("core")) if four else (0, 0)

    copies = [
        pltpu.make_async_copy(source, env[name], sems.at[i])
        for i, (source, name) in enumerate(
            ((own, "own"), (other, "other"), (tokens, "tokens"), (out_grad, "out_grad"))
        )
    ]
    for copy in copies:
        copy.start()

    count = feat_count[...].astype(F32)
    init_env(env, count)
    pad = jnp.zeros((GROUPS, GT, 2 * LANES - D), BF16)
    for part in range(3):
        env["dqkv"][:, :, 2 * LANES * part + D : 2 * LANES * (part + 1)] = pad
    for layer in range(LAYERS):
        ones_below(s[layer]["h1"], D)
        ones_below(s[layer]["h2"], D)
        ones_below(s[layer]["act"], FF)
        for ref in acc[layer].values():
            ref[...] = jnp.zeros_like(ref)
    env["x"][:, SEQ * ROWS :] = jnp.zeros((D, ROWS), F32)
    env["g"][:, SEQ * ROWS :] = jnp.zeros((D, ROWS), F32)
    row_scale = scales(table_ids[...], table_counts[...])
    copies[0].wait()
    copies[1].wait()
    for layer in range(LAYERS):
        gather_flat(env["own"], env["other"], place, layer, env["flat"])
        unpack(env["flat"], w[layer], env["tmp"])
    copies[2].wait()
    copies[3].wait()
    for slot in range(SEQ):
        lanes = slice(slot * ROWS, (slot + 1) * ROWS)
        env["x"][:, lanes] = env["tokens"][slot].astype(F32)
        keep = jnp.where(count >= float(slot), row_scale, 0.0)
        env["g"][:, lanes] = env["out_grad"][slot].astype(F32) * keep

    def put(target):
        def done(c, u, i, value):
            target[2 * c + i] = value

        return done

    def set_to(target):
        def done(c, u, i, value):
            view(target, c, u).at[:, HALVES[i]][...] = value

        return done

    shared = {name: env[name] for name in ("x", "middle", "g", "dm", "dqkv")}
    s = [dict(part, **shared) for part in s]

    skewed(project_stages(s[0], w[0]))
    forward_attention(s[0], env)
    attended, normed, gated, finish = rest_stages(s[0], w[0], set_to(env["x"]))
    project, hold = project_stages(s[1], w[1])

    def finish_project(c, u, held):
        finish(c, u, held)
        return project(c, u, None)

    skewed((attended, normed, gated, finish_project, hold))
    forward_attention(s[1], env)
    attended, normed, gated, finish_out = rest_stages(s[1], w[1], put(env["out"]))
    down, gate_up, normed_back, finish_back = rest_back_stages(s[1], w[1], acc[1], sums[1])

    def gated_down(c, u, held):
        return gated(c, u, held), down(c, u, None)

    def finish_gate_up(c, u, held):
        finish_out(c, u, held[0])
        return gate_up(c, u, held[1])

    skewed((attended, normed, gated_down, finish_gate_up, normed_back, finish_back))
    out_copy = pltpu.make_async_copy(env["out"].at[0:SEQ], out, sems.at[4])
    out_copy.start()
    backward_attention(s[1], env)
    products, finish_project_back = project_back_stages(
        s[1], w[1], acc[1], sums[1], set_to(env["g"])
    )
    down, gate_up, normed_back, finish_back = rest_back_stages(s[0], w[0], acc[0], sums[0])

    def finish_down(c, u, held):
        finish_project_back(c, u, held)
        return down(c, u, None)

    skewed((products, finish_down, gate_up, normed_back, finish_back))

    def send(layer):
        pack(env["flat"], acc[layer], sums[layer], env["tmp"])
        scatter_blocks(env["flat"], place, layer, env["keep"], env["give"])
        started = []
        for i, (name, target) in enumerate((("keep", keep_out), ("give", give_out))):
            started.append(
                pltpu.make_async_copy(
                    env[name].at[:, :, layer], target.at[:, :, layer], sems.at[5 + 2 * layer + i]
                )
            )
            started[-1].start()
        return started

    started = [out_copy] + send(1)
    backward_attention(s[0], env)
    skewed(project_back_stages(s[0], w[0], acc[0], sums[0], put(env["in_grad"])))
    last = pltpu.make_async_copy(env["in_grad"].at[0:SEQ], in_grad, sems.at[9])
    last.start()
    started += send(0) + [last]
    for copy in started:
        copy.wait()


def run_kernel(four, tokens, out_grad, own, other, count, ids, table_counts):
    names, scratch = make_scratch()
    full = jax.ShapeDtypeStruct((SEQ, D, ROWS), F32)
    blocks = jax.ShapeDtypeStruct(own.shape, BF16)

    def body(*refs):
        kernel(names, four, *refs)

    vmem = pl.BlockSpec(memory_space=pltpu.VMEM)
    anywhere = pl.BlockSpec(memory_space=pl.ANY)
    return pl.pallas_call(
        body,
        out_shape=(full, full, blocks, blocks),
        in_specs=[anywhere] * 4 + [vmem] * 3,
        out_specs=[anywhere] * 4,
        scratch_shapes=scratch,
        compiler_params=pltpu.CompilerParams(vmem_limit_bytes=64 * 1024 * 1024 - 256 * 1024),
    )(tokens, out_grad, own, other, count, ids, table_counts)


def halves_of_pairs(flat):
    rows = jnp.pad(flat.reshape(LAYERS, FLAT, LANES), ((0, 0), (0, BLOCK), (0, 0)))

    def blocks(skip):
        parts = [rows[:, 145 * chip + skip : 145 * chip + skip + BLOCK] for chip in range(16)]
        return jnp.stack([jnp.stack(parts[at::4]) for at in range(4)])

    return blocks(0), blocks(72)


def pairs_joined(even, odd):
    joined = []
    for chip in range(16):
        first, second = even[chip % 4, chip // 4], odd[chip % 4, chip // 4]
        seam = jnp.concatenate([first[:, 72:73, 0:64], second[:, 0:1, 64:]], axis=2)
        joined += [first[:, 0:72], seam, second[:, 1:73]]
    return jnp.concatenate(joined, axis=1).reshape(LAYERS, PSIZE)


def swap_along(x, axis, bit):
    pairs = [(i, i ^ bit) for i in range(lax.axis_size(axis))]
    return lax.ppermute(x, axis, pairs)


def gather_pairs(flat_params):
    size = flat_params.shape[1]
    room = BLOCK * LANES - size
    part = jnp.where(
        lax.axis_index("core") == 0,
        jnp.pad(flat_params, ((0, 0), (0, room))),
        jnp.pad(flat_params, ((0, 0), (64, room - 64))),
    ).reshape(1, LAYERS, BLOCK, LANES)
    for bit in (2, 1):
        part = jnp.concatenate([part, swap_along(part, "z", bit)], axis=0)
    own = lax.all_gather(part, ("x", "y"), axis=0, tiled=False)
    return own, swap_along(own, "core", 1)


def reduce_pairs(keep, give, size):
    got = swap_along(give, "core", 1)
    part = (keep.astype(F32) + got.astype(F32)).astype(BF16)
    part = lax.all_to_all(part, ("x", "y"), 0, 0, tiled=True)
    part = jnp.sum(part.astype(F32), axis=0)
    z = lax.axis_index("z")
    for bit in (2, 1):
        high = (z // bit) % 2
        stay = lax.dynamic_slice_in_dim(part, high * bit, bit, 0)
        go = lax.dynamic_slice_in_dim(part, (1 - high) * bit, bit, 0).astype(BF16)
        part = stay + swap_along(go, "z", bit).astype(F32)
    total = part.reshape(LAYERS, BLOCK * LANES)
    return jnp.where(
        lax.axis_index("core") == 0, total[:, 0:size], total[:, 64 : 64 + size]
    )


def body(axes, tokens, out_grad, flat_params, feat_count, table_ids, table_counts):
    four = "core" in axes
    count, ids = feat_count[None, :], table_ids[None, :]
    if four:
        own, other = gather_pairs(flat_params)
    else:
        own, other = halves_of_pairs(lax.all_gather(flat_params, axes, axis=1, tiled=True))
        turn = jnp.array([0, 2, 1, 3])
        own, other = own[:, turn], other[:, turn]
    turned = jnp.transpose(tokens, (1, 2, 0))
    turned_grad = jnp.transpose(out_grad, (1, 2, 0))
    results = [
        run_kernel(
            four,
            turned[:, :, at : at + ROWS],
            turned_grad[:, :, at : at + ROWS],
            own,
            other,
            count[:, at : at + ROWS],
            ids[:, at : at + ROWS],
            table_counts[None, :],
        )
        for at in range(0, tokens.shape[0], ROWS)
    ]
    out, in_grad, keep, give = results[0]
    if len(results) > 1:
        out = jnp.concatenate([r[0] for r in results], axis=2)
        in_grad = jnp.concatenate([r[1] for r in results], axis=2)
        keep = sum(r[2].astype(F32) for r in results)
        give = sum(r[3].astype(F32) for r in results)
    if four:
        grads = reduce_pairs(keep, give, flat_params.shape[1])
    else:
        flat = pairs_joined(keep.astype(F32), give.astype(F32))
        grads = lax.psum_scatter(flat, axes, scatter_dimension=1, tiled=True)
    return jnp.transpose(out, (2, 0, 1)), jnp.transpose(in_grad, (2, 0, 1)), grads


def solution(mesh):
    axes = mesh.axis_names
    if tuple(mesh.devices.shape) == (8, 4):
        axes = ("z", "x", "y", "core")
        mesh = jax.sharding.Mesh(mesh.devices.reshape(4, 2, 2, 2), axes)
    rows = P(axes, None, None)
    placed = (rows, rows, P(None, axes), P(axes), P(axes), P())
    return jax.shard_map(
        functools.partial(body, axes),
        mesh=mesh,
        in_specs=placed,
        out_specs=(rows, rows, P(None, axes)),
        check_vma=False,
    )
```

```python
import functools
import math

import jax
import jax.numpy as jnp
from jax import lax
from jax.experimental import pallas as pl
from jax.experimental.pallas import tpu as pltpu
from jax.sharding import PartitionSpec as P

D = 192
FF = 256
HEADS = 8
HEAD_DIM = 24
SEQ = 17
LAYERS = 2
PSIZE = 296960
ROWS = 128
SLOTS = 18
LANES = 128
FORWARD_GROUPS = 8
BACKWARD_GROUPS = 16
DEPTH = 8
BAND = 32
GROUP = 8
GROUPS = ROWS // GROUP
GT = SLOTS * GROUP
QL = HEADS * GT
TOKENS = SLOTS * ROWS
CHUNK = 2 * ROWS
CHUNKS = TOKENS // CHUNK
HALVES = (slice(0, ROWS), slice(ROWS, CHUNK))
FLAT = PSIZE // LANES
BLOCK = 80
EPS = 1e-05
VMEM_BYTES = 60 * 1024 * 1024
SCALE = 1.0 / math.sqrt(HEAD_DIM)
F32 = jnp.float32
BF16 = jnp.bfloat16


def dot(a, b, ca, cb):
    return lax.dot_general(a, b, (((ca,), (cb,)), ((), ())), preferred_element_type=F32)


def lane_half(shape):
    return lax.broadcasted_iota(jnp.int32, shape, len(shape) - 1) < 64


def swap(x):
    return pltpu.roll(x, 64, x.ndim - 1)


def low_half(x):
    return jnp.where(lane_half(x.shape), x, 0.0)


def splice(a, b):
    return swap(jnp.where(lane_half(a.shape), b, a))


def after(a, b):
    return jnp.where(lane_half(a.shape), a, swap(b))


def wide(column):
    return jnp.concatenate([column, column], axis=1)


def gather_flat(own, other, place, layer, flat):
    z, core = place[0], place[1]
    for chip in range(FLAT // 145):
        turn = z ^ (chip // 4)
        at = (turn & 1) * 2 + turn // 2
        mine = own[chip % 4, at, layer].astype(F32)
        theirs = other[chip % 4, at, layer].astype(F32)
        first = jnp.where(core == 0, mine, theirs)
        second = jnp.where(core == 0, theirs, mine)
        base = 145 * chip
        flat[pl.ds(base, BLOCK), :] = first
        flat[pl.ds(base + 72, BLOCK), :] = second
        flat[pl.ds(base + 72, 1), :] = jnp.where(
            lane_half((1, LANES)), first[72:73], second[0:1]
        )


def unpack(flat, w, tmp):
    def rows(start, count, stride):
        return flat[pl.ds(start, count, stride=stride), :]

    def row(index):
        return flat[pl.ds(index, 1), :]

    def pair_row(a, b):
        return jnp.concatenate([a, b], axis=1)

    vectors = [
        pair_row(row(0), low_half(row(1))),
        pair_row(splice(row(1), row(2)), low_half(swap(row(2)))),
        pair_row(row(1158), low_half(row(1159))),
        pair_row(splice(row(1159), row(1160)), low_half(swap(row(1160)))),
        pair_row(row(1161), low_half(row(1162))),
        pair_row(splice(row(2318), row(2319)), low_half(swap(row(2319)))),
    ]
    index = lax.broadcasted_iota(jnp.int32, (16, 2 * LANES), 0)
    stacked = jnp.zeros((16, 2 * LANES), F32)
    for i, vector in enumerate(vectors):
        stacked = jnp.where(index == i, vector, stacked)
    stacked = stacked.astype(BF16)
    for i in range(6):
        pick = jnp.where(index[:, 0:LANES] == i, 1.0, 0.0).astype(BF16)
        w["cols"][i] = dot(stacked, pick, 0, 0)[0:D]

    e = [rows(3 + j, 96, 9) for j in range(9)]
    even = (e[0], low_half(e[1]), splice(e[1], e[2]), low_half(swap(e[2])), e[3], low_half(e[4]))
    odd = (
        splice(e[4], e[5]),
        low_half(swap(e[5])),
        e[6],
        low_half(e[7]),
        splice(e[7], e[8]),
        low_half(swap(e[8])),
    )
    zero_row = jnp.zeros((1, LANES), F32)
    bias = (
        row(867),
        low_half(row(868)),
        zero_row,
        zero_row,
        splice(row(868), row(869)),
        low_half(swap(row(869))),
    )
    first_row = lax.broadcasted_iota(jnp.int32, (16, LANES), 0) == 0
    for j in range(6):
        tmp[j % 2, pl.ds(0, 96, stride=2), :] = even[j]
        tmp[j % 2, pl.ds(1, 96, stride=2), :] = odd[j]
        w["qkv"][0:D, j * LANES : (j + 1) * LANES] = tmp[j % 2, 0:D, :].astype(BF16)
        w["qkv"][D : D + 16, j * LANES : (j + 1) * LANES] = jnp.where(
            first_row, jnp.broadcast_to(bias[j], (16, LANES)), 0.0
        ).astype(BF16)

    e = [rows(870 + j, 96, 3) for j in range(3)]
    tmp[0, pl.ds(0, 96, stride=2), :] = e[0]
    tmp[1, pl.ds(0, 96, stride=2), :] = low_half(e[1])
    tmp[0, pl.ds(1, 96, stride=2), :] = splice(e[1], e[2])
    tmp[1, pl.ds(1, 96, stride=2), :] = low_half(swap(e[2]))
    w_out = jnp.concatenate([tmp[0, 0:D, :], tmp[1, 0:D, :]], axis=1)
    w["out_t"][...] = jnp.transpose(w_out.astype(BF16))[0:D]

    g = [rows(1162 + j, 192, 4) for j in range(5)]
    tiles = [splice(g[j], g[j + 1]) for j in range(4)]
    gate_up = jnp.concatenate(tiles, axis=1)
    w["gu"][...] = gate_up.astype(BF16)
    bias_row = jnp.concatenate(
        [splice(row(1930 + j), row(1931 + j)) for j in range(4)], axis=1
    )
    bias_rows = jnp.where(
        lax.broadcasted_iota(jnp.int32, (64, 2 * FF), 0) == 0,
        jnp.broadcast_to(bias_row, (64, 2 * FF)),
        0.0,
    )
    w["gu_t"][...] = jnp.transpose(jnp.concatenate([gate_up, bias_rows], axis=0).astype(BF16))[
        :, 0 : D + 16
    ]

    e = [rows(1934 + j, 128, 3) for j in range(4)]
    tmp[0, pl.ds(0, 128, stride=2), :] = splice(e[0], e[1])
    tmp[1, pl.ds(0, 128, stride=2), :] = low_half(swap(e[1]))
    tmp[0, pl.ds(1, 128, stride=2), :] = e[2]
    tmp[1, pl.ds(1, 128, stride=2), :] = low_half(e[3])
    w_down = jnp.concatenate([tmp[0, 0:FF, :], tmp[1, 0:FF, :]], axis=1)
    w["down"][...] = w_down[:, 0:D].astype(BF16)
    w["down_t"][...] = jnp.transpose(w_down.astype(BF16))[0:D]


def row_of(columns):
    turned = jnp.sum(jnp.transpose(columns), axis=0, keepdims=True)
    return turned[:, 0:LANES], jnp.concatenate(
        [turned[:, LANES:D], jnp.zeros((1, LANES - (D - LANES)), F32)], axis=1
    )


def pack(flat, acc, sums, tmp):
    def put(start, count, stride, value):
        flat[pl.ds(start, count, stride=stride), :] = value

    def put_row(index, value):
        flat[pl.ds(index, 1), :] = value

    def down(j, start, count, stride):
        return acc["down"][j, pl.ds(start, count, stride=stride), :]

    g1 = row_of(sums[0])
    b1 = row_of(sums[1])
    g2 = row_of(sums[2])
    b2 = row_of(sums[3])
    bo = row_of(sums[4])
    put_row(0, g1[0])
    put_row(1, after(g1[1], b1[0]))
    put_row(2, splice(b1[0], b1[1]))

    even = [acc["qkv"][j, pl.ds(0, 96, stride=2), :] for j in range(6)]
    odd = [acc["qkv"][j, pl.ds(1, 96, stride=2), :] for j in range(6)]
    put(3, 96, 9, even[0])
    put(4, 96, 9, after(even[1], even[2]))
    put(5, 96, 9, splice(even[2], even[3]))
    put(6, 96, 9, even[4])
    put(7, 96, 9, after(even[5], odd[0]))
    put(8, 96, 9, splice(odd[0], odd[1]))
    put(9, 96, 9, odd[2])
    put(10, 96, 9, after(odd[3], odd[4]))
    put(11, 96, 9, splice(odd[4], odd[5]))
    bias = [acc["qkv"][j, D : D + 1, :] for j in range(6)]
    put_row(867, bias[0])
    put_row(868, after(bias[1], bias[4]))
    put_row(869, splice(bias[4], bias[5]))

    w_out = jnp.transpose(
        jnp.concatenate([acc["out_t"][...], jnp.zeros((64, D), F32)], axis=0)
    )
    tmp[0, 0:D, :] = w_out[:, 0:LANES]
    tmp[1, 0:D, :] = w_out[:, LANES:]
    even = [tmp[j, pl.ds(0, 96, stride=2), :] for j in range(2)]
    odd = [tmp[j, pl.ds(1, 96, stride=2), :] for j in range(2)]
    put(870, 96, 3, even[0])
    put(871, 96, 3, after(even[1], odd[0]))
    put(872, 96, 3, splice(odd[0], odd[1]))
    put_row(1158, bo[0])
    put_row(1159, after(bo[1], g2[0]))
    put_row(1160, splice(g2[0], g2[1]))
    put_row(1161, b2[0])

    gu = [acc["gu"][j, 0 : D + 8, :] for j in range(4)]
    put_row(1162, after(b2[1], gu[0][0:1]))
    put(1166, 192, 4, splice(gu[3][0:192], acc["gu"][0, pl.ds(1, 192), :]))
    for j in range(1, 4):
        joined = splice(gu[j - 1], gu[j])
        put(1162 + j, 192, 4, joined[0:192])
        put_row(1930 + j, joined[192:193])
    put_row(1934, splice(gu[3][192:193], acc["down"][0, 0:1, :]))

    w0e, w1e = down(0, 0, 128, 2), down(1, 0, 128, 2)
    w0o, w1o = down(0, 1, 128, 2), down(1, 1, 128, 2)
    put(1935, 128, 3, splice(w0e, w1e))
    put(1936, 128, 3, w0o)
    put(1937, 128, 3, after(w1o, down(0, 2, 128, 2)))
    put_row(2319, splice(acc["down"][0, FF : FF + 1, :], acc["down"][1, FF : FF + 1, :]))


def scatter_blocks(flat, place, layer, keep, give):
    core = place[1]
    for chip in range(FLAT // 145):
        first = flat[pl.ds(145 * chip, BLOCK), :]
        second = flat[pl.ds(145 * chip + 72, BLOCK), :]
        keep[chip % 4, chip // 4, layer] = jnp.where(core == 0, first, second).astype(BF16)
        give[chip % 4, chip // 4, layer] = jnp.where(core == 0, second, first).astype(BF16)


def norm(x, gain, bias):
    centre = x - jnp.sum(x, axis=0, keepdims=True) * (1.0 / D)
    variance = jnp.sum(centre * centre, axis=0, keepdims=True) * (1.0 / D)
    rstd = lax.rsqrt(variance + EPS)
    xhat = centre * rstd
    return xhat, rstd, (xhat * gain + bias).astype(BF16)


def norm_back(grad, xhat, rstd, gain):
    e = gain * grad
    mean_e = jnp.sum(e, axis=0, keepdims=True) * (1.0 / D)
    mean_ex = jnp.sum(e * xhat, axis=0, keepdims=True) * (1.0 / D)
    return rstd * (e - mean_e - xhat * mean_ex)


def fold(x):
    return x[:, 0:LANES] + x[:, LANES:]


def gelu_parts(gate):
    z = gate * (1.0 / math.sqrt(2.0))
    cdf = 0.5 * lax.erf(z) + 0.5
    bell = jnp.exp2(z * z * (-1.0 / math.log(2.0)))
    return cdf, cdf + (z * bell) * (1.0 / math.sqrt(math.pi))


def to_groups(x):
    n = x.shape[-1]
    x = x.reshape(2, GROUPS, GROUP, n)
    return jnp.concatenate([x[0][:, None], x[1][:, None]], axis=1).reshape(
        GROUPS, 2 * GROUP, n
    )


def from_groups(x):
    n = x.shape[-1]
    x = x.reshape(GROUPS, 2, GROUP, n)
    return jnp.concatenate([x[:, 0], x[:, 1]], axis=0).reshape(CHUNK, n)


def group_rows(c):
    return slice(2 * GROUP * c, 2 * GROUP * (c + 1))


def skewed(stages):
    held = {}
    for tick in range(CHUNKS + len(stages) - 1):
        for j, stage in enumerate(stages):
            c = tick - j
            if 0 <= c < CHUNKS:
                held[c] = stage(c, held.get(c))


def view(ref, c, rows=None):
    return ref.at[0 : ref.shape[0] if rows is None else rows, c * CHUNK : (c + 1) * CHUNK]


def project_stages(s, w):
    def project(c, _):
        lows = []
        for half in HALVES:
            xhat, rstd, low = norm(
                view(s["x"], c).at[:, half][...], w["cols"][0], w["cols"][1]
            )
            view(s["xhat1"], c).at[:, half][...] = xhat
            view(s["rstd1"], c).at[:, half][...] = rstd
            lows.append(low)
        view(s["h1"], c, D)[...] = jnp.concatenate(lows, axis=1)
        return dot(view(s["h1"], c)[...], w["qkv"][...], 0, 0)

    def keep(c, qkv):
        place = group_rows(c)
        s["q"][:, place, :] = to_groups(qkv[:, 0:D]).astype(BF16)
        for name, start in (("k", 256), ("v", 512)):
            part = qkv[:, start : start + D].reshape(2, GROUPS, GROUP, D)
            turned = jnp.concatenate(
                [
                    pltpu.roll(part[t], (2 * c + t) % GROUP, 1)[:, None]
                    for t in range(2)
                ],
                axis=1,
            )
            s[name][:, place, :] = turned.reshape(GROUPS, 2 * GROUP, D).astype(BF16)

    return project, keep


def spread(values, masks):
    n = values.shape[1]
    doubled = [
        jnp.concatenate([values[8 * a : 8 * a + 8], values[8 * a : 8 * a + 8]], axis=0).astype(BF16)
        for a in range(3)
    ]
    parts = [doubled[a] * masks[m][:, 0:n] for a in range(2) for m in range(4)]
    parts.append(doubled[2] * masks[4][:, 0:n])
    return jnp.concatenate(parts, axis=0)


def collect(scores, bits):
    n = scores.shape[1]
    bits = [bit[:, 0:n] for bit in bits]
    out = []
    for a in range(2):
        level = [scores[64 * a + 8 * j : 64 * a + 8 * j + 8] for j in range(8)]
        for bit in bits:
            level = [
                jnp.where(bit, level[2 * i + 1], level[2 * i]) for i in range(len(level) // 2)
            ]
        out.append(level[0])
    out.append(scores[128:136])
    return out


def blocks_of(turned, t, halves):
    first = turned[48 * t : 48 * t + 16]
    middle = turned[48 * t + 16 : 48 * t + 32]
    last = turned[48 * t + 32 : 48 * t + 48]
    none = jnp.zeros_like(first)
    return jnp.concatenate(
        [
            jnp.concatenate([first, none], axis=1),
            jnp.concatenate([middle * halves[0], middle * halves[1]], axis=1),
            jnp.concatenate([none, last], axis=1),
        ],
        axis=0,
    )


def padded(block, t):
    parts = [block]
    if t > 0:
        parts.insert(0, jnp.zeros((48 * t, block.shape[1]), BF16))
    if t < 3:
        parts.append(jnp.zeros((48 * (3 - t), block.shape[1]), BF16))
    return jnp.concatenate(parts, axis=0)


def tail_of(rows, heads):
    return jnp.concatenate([rows * heads[h, 0:1, :] for h in range(HEADS)], axis=0)


def heads_joined(tiles, tail, heads, scale=None):
    main = []
    for tile in tiles:
        main += [tile[0:HEAD_DIM, 0:LANES], tile[HEAD_DIM:, LANES:]]
    main = jnp.concatenate(main, axis=0)
    if scale is not None:
        main, tail = main * scale, tail * scale
    main = jnp.transpose(main.astype(BF16))
    tail = tail.astype(BF16)
    last = tail[0:16] * heads[0, 0:1, :]
    for h in range(1, HEADS):
        last += tail[16 * h : 16 * h + 16] * heads[h, 0:1, :]
    return main, last


def softmax(kept, diff, limit):
    n = kept[0].shape[1]
    own = diff[:, 0:n]
    limit = limit[:, 0:n]
    slot = own.astype(F32)
    shown = [
        jnp.where(slot <= limit, kept[0] * SCALE, -1e9),
        jnp.where(slot + 8.0 <= limit, kept[1] * SCALE, -1e9),
        jnp.where(own == 0, jnp.where(limit >= 16.0, kept[2] * SCALE, -1e9), -3e38),
    ]
    top = jnp.max(jnp.maximum(jnp.maximum(shown[0], shown[1]), shown[2]), axis=0, keepdims=True)
    shown = [jnp.exp(part - top) for part in shown]
    inverse = 1.0 / jnp.sum(shown[0] + shown[1] + shown[2], axis=0, keepdims=True)
    return jnp.concatenate([part * inverse for part in shown], axis=0)


def staged(items, first, second):
    waiting = []
    for item in items:
        waiting.append((item, first(item)))
        if len(waiting) > DEPTH:
            second(*waiting.pop(0))
    for entry in waiting:
        second(*entry)


def batches(size, run):
    if size == GROUPS:
        run(0)
        return

    def step(i, carry):
        run(i * size)
        return carry

    lax.fori_loop(0, GROUPS // size, step, 0)


def forward_attention(s, env):
    diff = env["diff"][...]
    bits = [(diff & (1 << i)) != 0 for i in range(3)]
    halves = [env["halves"][i] for i in range(2)]

    def run(base):
        state = {}

        def load(u):
            g = base + u
            queries, values = s["q"][g], s["v"][g]
            state[u] = {
                "g": g,
                "queries": queries,
                "keys": s["k"][g],
                "turned": jnp.transpose(queries)[:, 0:LANES],
                "values": values,
                "turned_values": jnp.transpose(values),
                "count": env["count"][pl.ds(g, 1), :],
                "tiles": [],
            }

        def scores(item):
            u, t = item
            if t == 0:
                load(u)
            at = state[u]
            if t < 4:
                return dot(at["keys"], padded(blocks_of(at["turned"], t, halves), t), 1, 0)
            return dot(at["keys"], tail_of(at["queries"][LANES:GT], env["heads"]), 1, 1)

        def mix(item, products):
            u, t = item
            at = state[u]
            attention = softmax(collect(products, bits), diff, at["count"])
            s["att"][at["g"], :, t * CHUNK : min((t + 1) * CHUNK, QL)] = attention
            low = spread(attention, env["masks"])
            if t < 4:
                at["tiles"].append(dot(at["turned_values"][48 * t : 48 * t + 48], low, 1, 0))
                return
            tail = dot(low, at["values"], 0, 0)
            main, last = heads_joined(at["tiles"], tail, env["heads"])
            s["mixed"][at["g"], 0:LANES, :] = main
            s["mixed"][at["g"], LANES:GT, :] = last

        staged([(u, t) for u in range(FORWARD_GROUPS) for t in range(5)], scores, mix)

    batches(FORWARD_GROUPS, run)


def rest_stages(s, w, done):
    def attended(c, _):
        mixed = from_groups(s["mixed"][:, group_rows(c), :].astype(F32)).astype(BF16)
        return dot(w["out_t"][...], mixed, 1, 1)

    def normed(c, product):
        lows = []
        for half in HALVES:
            middle = view(s["x"], c).at[:, half][...] + (product[:, half] + w["cols"][2])
            view(s["middle"], c).at[:, half][...] = middle
            xhat, rstd, low = norm(middle, w["cols"][3], w["cols"][4])
            view(s["xhat2"], c).at[:, half][...] = xhat
            view(s["rstd2"], c).at[:, half][...] = rstd
            lows.append(low)
        view(s["h2"], c, D)[...] = jnp.concatenate(lows, axis=1)
        return dot(w["gu_t"][...], view(s["h2"], c)[...], 1, 0)

    def gated(c, gate_up):
        acts = []
        for r in range(0, FF, BAND):
            band = pl.ds(r, BAND)
            gate, up = gate_up[r : r + BAND], gate_up[FF + r : FF + r + BAND]
            cdf, slope = gelu_parts(gate)
            gelu = gate * cdf
            view(s["gelu"], c).at[band][...] = gelu
            view(s["slope"], c).at[band][...] = slope * up
            acts.append((gelu * up).astype(BF16))
        act = jnp.concatenate(acts, axis=0)
        view(s["act"], c, FF)[...] = act
        return dot(w["down_t"][...], act, 1, 0)

    def finish(c, product):
        for i, half in enumerate(HALVES):
            value = view(s["middle"], c).at[:, half][...]
            done(c, i, value + (product[:, half] + w["cols"][5]))

    return attended, normed, gated, finish


def add_tiles(ref, value):
    for j in range(ref.shape[0]):
        ref[j] += value[:, j * LANES : (j + 1) * LANES]


def add_narrow(ref, value):
    ref[0] += value[:, 0:LANES]
    ref[1, :, 0 : D - LANES] += value[:, LANES:D]


def rest_back_stages(s, w, acc, sums):
    def down(c, _):
        branch = view(s["g"], c)[...].astype(BF16)
        return dot(view(s["act"], c)[...], branch, 1, 1), dot(w["down"][...], branch, 1, 0)

    def gate_up(c, held):
        grad_down, d_act = held
        add_narrow(acc["down"], grad_down)
        gates, ups = [], []
        for r in range(0, FF, BAND):
            band = pl.ds(r, BAND)
            part = d_act[r : r + BAND]
            gates.append((part * view(s["slope"], c).at[band][...]).astype(BF16))
            ups.append((part * view(s["gelu"], c).at[band][...]).astype(BF16))
        d_gate_up = jnp.concatenate(gates + ups, axis=0)
        return dot(view(s["h2"], c)[...], d_gate_up, 1, 1), dot(w["gu"][...], d_gate_up, 1, 0)

    def normed(c, held):
        grad_gu, d_normed = held
        add_tiles(acc["gu"], grad_gu)
        lows = []
        for half in HALVES:
            xhat = view(s["xhat2"], c).at[:, half][...]
            part = d_normed[:, half]
            sums[2] += part * xhat
            sums[3] += part
            g = view(s["g"], c).at[:, half]
            d_middle = g[...] + norm_back(
                part, xhat, view(s["rstd2"], c).at[:, half][...], w["cols"][3]
            )
            g[...] = d_middle
            low = d_middle.astype(BF16)
            sums[4] += low.astype(F32)
            lows.append(low)
        d_attended = jnp.concatenate(lows, axis=1)
        mixed = from_groups(s["mixed"][:, group_rows(c), :].astype(F32)).astype(BF16)
        return dot(d_attended, w["out_t"][...], 0, 0), dot(d_attended, mixed, 1, 0)

    def finish(c, held):
        d_mixed, grad_out = held
        s["dqkv"][:, group_rows(c), 0:D] = to_groups(d_mixed).astype(BF16)
        acc["out_t"][...] += grad_out

    return down, gate_up, normed, finish


def backward_attention(s, env):
    diff = env["diff"][...]
    bits = [(diff & (1 << i)) != 0 for i in range(3)]
    halves = [env["halves"][i] for i in range(2)]

    def run(base):
        state = {}

        def load(u):
            g = base + u
            queries, keys, grads = s["q"][g], s["k"][g], s["dqkv"][g, :, 0:D]
            state[u] = {
                "g": g,
                "queries": queries,
                "grads": grads,
                "keys": keys,
                "values": s["v"][g],
                "turned": jnp.transpose(queries)[:, 0:LANES],
                "turned_grads": jnp.transpose(grads)[:, 0:LANES],
                "turned_keys": jnp.transpose(keys),
                "dq": [],
                "dk": [],
                "dv": [],
            }

        def products(item):
            u, t = item
            if t == 0:
                load(u)
            at = state[u]
            if t < 4:
                block = blocks_of(at["turned_grads"], t, halves)
                return block, dot(at["values"], padded(block, t), 1, 0)
            block = tail_of(at["grads"][LANES:GT], env["heads"])
            return block, dot(at["values"], block, 1, 1)

        def back(item, result):
            u, t = item
            at = state[u]
            grad_block, product = result
            attention = s["att"][at["g"], :, t * CHUNK : min((t + 1) * CHUNK, QL)]
            weighted = attention * jnp.concatenate(collect(product, bits), axis=0)
            total = jnp.sum(weighted, axis=0, keepdims=True)
            d_score = spread(weighted - attention * total, env["masks"])
            low = spread(attention, env["masks"])
            if t < 4:
                at["dv"].append(dot(grad_block, low, 1, 1))
                at["dk"].append(dot(blocks_of(at["turned"], t, halves), d_score, 1, 1))
                at["dq"].append(dot(at["turned_keys"][48 * t : 48 * t + 48], d_score, 1, 0))
                return
            d_values = dot(low, grad_block, 1, 0)
            d_keys = dot(d_score, tail_of(at["queries"][LANES:GT], env["heads"]), 1, 0)
            finish(at, d_values, d_keys, dot(d_score, at["keys"], 0, 0))

        def finish(at, d_values, d_keys, tail):
            g = at["g"]
            main, last = heads_joined(at["dq"], tail, env["heads"], SCALE)
            s["dqkv"][g, 0:LANES, 0:D] = main
            s["dqkv"][g, LANES:GT, 0:D] = last
            for parts, own, start, scale in (
                (at["dk"], d_keys, 256, SCALE),
                (at["dv"], d_values, 512, 1.0),
            ):
                value = jnp.transpose(jnp.concatenate(parts, axis=0)) + own
                slots = (value * scale).reshape(SLOTS, GROUP, D)
                turned = [
                    slots[k] if k % GROUP == 0 else pltpu.roll(slots[k], GROUP - k % GROUP, 0)
                    for k in range(SLOTS)
                ]
                s["dqkv"][g, :, start : start + D] = jnp.concatenate(turned, axis=0).astype(BF16)

        staged([(u, t) for u in range(BACKWARD_GROUPS) for t in range(5)], products, back)

    batches(BACKWARD_GROUPS, run)


def project_back_stages(s, w, acc, sums, done):
    def products(c, _):
        d_qkv = from_groups(s["dqkv"][:, group_rows(c), :].astype(F32)).astype(BF16)
        return dot(view(s["h1"], c)[...], d_qkv, 1, 0), dot(w["qkv"][0:D, :], d_qkv, 1, 1)

    def finish(c, held):
        grad_qkv, d_normed = held
        add_tiles(acc["qkv"], grad_qkv)
        for i, half in enumerate(HALVES):
            xhat = view(s["xhat1"], c).at[:, half][...]
            part = d_normed[:, half]
            sums[0] += part * xhat
            sums[1] += part
            back = norm_back(part, xhat, view(s["rstd1"], c).at[:, half][...], w["cols"][0])
            done(c, i, view(s["g"], c).at[:, half][...] + back)

    return products, finish


def per_layer():
    return {
        "xhat1": ((D, TOKENS), F32),
        "rstd1": ((1, TOKENS), F32),
        "h1": ((D + 16, TOKENS), BF16),
        "q": ((GROUPS, GT, D), BF16),
        "k": ((GROUPS, GT, D), BF16),
        "v": ((GROUPS, GT, D), BF16),
        "att": ((GROUPS, 24, QL), F32),
        "mixed": ((GROUPS, GT, D), BF16),
        "xhat2": ((D, TOKENS), F32),
        "rstd2": ((1, TOKENS), F32),
        "h2": ((D + 16, TOKENS), BF16),
        "act": ((FF + 16, TOKENS), BF16),
        "gelu": ((FF, TOKENS), F32),
        "slope": ((FF, TOKENS), F32),
    }


def weights():
    return {
        "cols": ((6, D, LANES), F32),
        "qkv": ((D + 16, 6 * LANES), BF16),
        "out_t": ((D, D), BF16),
        "gu": ((D, 2 * FF), BF16),
        "gu_t": ((2 * FF, D + 16), BF16),
        "down": ((FF, D), BF16),
        "down_t": ((D, FF), BF16),
    }


def accumulators():
    return {
        "qkv": ((6, D + 16, LANES), F32),
        "out_t": ((D, D), F32),
        "gu": ((4, D + 16, LANES), F32),
        "down": ((2, FF + 16, LANES), F32),
        "sums": ((5, D, LANES), F32),
    }


def common():
    full = (SEQ, D, ROWS)
    return {
        "halves": ((2, 16, LANES), BF16),
        "heads": ((HEADS, 16, D), BF16),
        "masks": ((5, 16, CHUNK), BF16),
        "diff": ((GROUP, CHUNK), jnp.int32),
        "count": ((GROUPS, CHUNK), F32),
        "dqkv": ((GROUPS, GT, 6 * LANES), BF16),
        "x": ((D, TOKENS), F32),
        "middle": ((D, TOKENS), F32),
        "g": ((D, TOKENS), F32),
        "flat": ((FLAT + 8, LANES), F32),
        "tmp": ((2, FF, LANES), F32),
        "tokens": (full, BF16),
        "out_grad": (full, BF16),
        "out": ((SLOTS, D, ROWS), F32),
    }


def make_scratch():
    shapes, names = [], []
    for prefix, table in (
        ("common", common()),
        ("acc0", accumulators()),
        ("acc1", accumulators()),
        ("s0", per_layer()),
        ("s1", per_layer()),
        ("w0", weights()),
        ("w1", weights()),
    ):
        for name, (shape, kind) in table.items():
            names.append((prefix, name))
            shapes.append(pltpu.VMEM(shape, kind))
    return names, shapes + [pltpu.SemaphoreType.DMA((6,))]


def init_env(env, count):
    lane = lax.broadcasted_iota(jnp.int32, (GROUP, CHUNK), 1)
    sub = lax.broadcasted_iota(jnp.int32, (GROUP, CHUNK), 0)
    diff = (sub - lane) & (GROUP - 1)
    env["diff"][...] = diff
    for m in range(5):
        first = jnp.where(diff == (2 * m) % 8, 1.0, 0.0)
        second = jnp.where(diff == 2 * m + 1, 1.0, 0.0)
        env["masks"][m] = jnp.concatenate([first, second], axis=0).astype(BF16)
    sub = lax.broadcasted_iota(jnp.int32, (16, LANES), 0)
    env["halves"][0] = jnp.where(sub < 8, 1.0, 0.0).astype(BF16)
    env["halves"][1] = jnp.where(sub < 8, 0.0, 1.0).astype(BF16)
    feature = lax.broadcasted_iota(jnp.int32, (16, D), 1) // HEAD_DIM
    for h in range(HEADS):
        env["heads"][h] = jnp.where(feature == h, 1.0, 0.0).astype(BF16)
    row = lax.broadcasted_iota(jnp.int32, (GROUPS, LANES), 1)
    group = lax.broadcasted_iota(jnp.int32, (GROUPS, LANES), 0)
    mine = jnp.where(row // GROUP == group, jnp.broadcast_to(count, (GROUPS, LANES)), 0.0)
    here = lax.broadcasted_iota(jnp.int32, (LANES, CHUNK), 0)
    there = lax.broadcasted_iota(jnp.int32, (LANES, CHUNK), 1)
    pick = jnp.where(here % GROUP == there % GROUP, 1.0, 0.0).astype(BF16)
    env["count"][...] = dot(mine.astype(BF16), pick, 1, 0)


def ones_below(ref, rows):
    tail = ref.shape[0] - rows
    mark = lax.broadcasted_iota(jnp.int32, (tail, ref.shape[1]), 0) == 0
    ref[rows:, :] = jnp.where(mark, 1.0, 0.0).astype(BF16)


def scales(ids, table_counts):
    counts = table_counts.astype(F32)
    tables = counts.shape[1]
    high = jnp.floor(counts * (1.0 / 32.0))
    table = lax.broadcasted_iota(jnp.int32, (tables, ROWS), 0)
    match = jnp.where(table == ids, 1.0, 0.0).astype(BF16)

    def pick(values):
        return dot(jnp.broadcast_to(values, (8, tables)).astype(BF16), match, 1, 0)[0:1]

    mine = 32.0 * pick(high) + pick(counts - 32.0 * high)
    return jnp.sqrt(jnp.sum(counts, axis=1, keepdims=True) * (1.0 / tables) / mine)


def kernel(names, four, *refs):
    inputs, outputs, scratch, sems = refs[0:7], refs[7:11], refs[11:-1], refs[-1]
    tokens, out_grad, own, other, feat_count, table_ids, table_counts = inputs
    out, in_grad, keep_out, give_out = outputs
    table = {}
    for (prefix, name), ref in zip(names, scratch):
        table.setdefault(prefix, {})[name] = ref
    env = table["common"]
    acc = [table["acc0"], table["acc1"]]
    s, w = [table["s0"], table["s1"]], [table["w0"], table["w1"]]
    sums = [part["sums"] for part in acc]
    place = (lax.axis_index("z"), lax.axis_index("core")) if four else (0, 0)

    copies = [
        pltpu.make_async_copy(source, env[name], sems.at[i])
        for i, (source, name) in enumerate(
            ((tokens, "tokens"), (out_grad, "out_grad"))
        )
    ]
    for copy in copies:
        copy.start()

    count = feat_count[...].astype(F32)
    init_env(env, count)
    pad = jnp.zeros((GROUPS, GT, 2 * LANES - D), BF16)
    for part in range(3):
        env["dqkv"][:, :, 2 * LANES * part + D : 2 * LANES * (part + 1)] = pad
    for layer in range(LAYERS):
        ones_below(s[layer]["h1"], D)
        ones_below(s[layer]["h2"], D)
        ones_below(s[layer]["act"], FF)
        for ref in acc[layer].values():
            ref[...] = jnp.zeros_like(ref)
    env["x"][:, SEQ * ROWS :] = jnp.zeros((D, ROWS), F32)
    env["g"][:, SEQ * ROWS :] = jnp.zeros((D, ROWS), F32)
    row_scale = scales(table_ids[...], table_counts[...])
    for layer in range(LAYERS):
        gather_flat(own, other, place, layer, env["flat"])
        unpack(env["flat"], w[layer], env["tmp"])
    copies[0].wait()
    copies[1].wait()
    for slot in range(SEQ):
        lanes = slice(slot * ROWS, (slot + 1) * ROWS)
        env["x"][:, lanes] = env["tokens"][slot].astype(F32)
        keep = jnp.where(count >= float(slot), row_scale, 0.0)
        env["g"][:, lanes] = env["out_grad"][slot].astype(F32) * keep

    def put(target):
        def done(c, i, value):
            target[2 * c + i] = value

        return done

    def set_to(target):
        def done(c, i, value):
            view(target, c).at[:, HALVES[i]][...] = value

        return done

    shared = {name: env[name] for name in ("x", "middle", "g", "dqkv")}
    s = [dict(part, **shared) for part in s]

    skewed(project_stages(s[0], w[0]))
    forward_attention(s[0], env)
    attended, normed, gated, finish = rest_stages(s[0], w[0], set_to(env["x"]))
    project, hold = project_stages(s[1], w[1])

    def finish_project(c, held):
        finish(c, held)
        return project(c, None)

    skewed((attended, normed, gated, finish_project, hold))
    forward_attention(s[1], env)
    attended, normed, gated, finish_out = rest_stages(s[1], w[1], put(env["out"]))
    down, gate_up, normed_back, finish_back = rest_back_stages(s[1], w[1], acc[1], sums[1])

    def gated_down(c, held):
        return gated(c, held), down(c, None)

    def finish_gate_up(c, held):
        finish_out(c, held[0])
        return gate_up(c, held[1])

    skewed((attended, normed, gated_down, finish_gate_up, normed_back, finish_back))
    out_copy = pltpu.make_async_copy(env["out"].at[0:SEQ], out, sems.at[4])
    out_copy.start()
    backward_attention(s[1], env)
    products, finish_project_back = project_back_stages(
        s[1], w[1], acc[1], sums[1], set_to(env["g"])
    )
    down, gate_up, normed_back, finish_back = rest_back_stages(s[0], w[0], acc[0], sums[0])

    def finish_down(c, held):
        finish_project_back(c, held)
        return down(c, None)

    skewed((products, finish_down, gate_up, normed_back, finish_back))

    def send(layer):
        pack(env["flat"], acc[layer], sums[layer], env["tmp"])
        scatter_blocks(env["flat"], place, layer, keep_out, give_out)

    send(1)
    backward_attention(s[0], env)
    out_copy.wait()
    skewed(project_back_stages(s[0], w[0], acc[0], sums[0], put(env["out"])))
    last = pltpu.make_async_copy(env["out"].at[0:SEQ], in_grad, sems.at[5])
    last.start()
    send(0)
    last.wait()


def run_kernel(four, tokens, out_grad, own, other, count, ids, table_counts):
    names, scratch = make_scratch()
    full = jax.ShapeDtypeStruct((SEQ, D, ROWS), F32)
    blocks = pltpu.VMEM(own.shape, BF16)
    own, other = (pltpu.with_memory_space_constraint(part, pltpu.VMEM) for part in (own, other))

    def body(*refs):
        kernel(names, four, *refs)

    vmem = pl.BlockSpec(memory_space=pltpu.VMEM)
    anywhere = pl.BlockSpec(memory_space=pl.ANY)
    return pl.pallas_call(
        body,
        out_shape=(full, full, blocks, blocks),
        in_specs=[anywhere] * 2 + [vmem] * 5,
        out_specs=[anywhere] * 2 + [vmem] * 2,
        scratch_shapes=scratch,
        compiler_params=pltpu.CompilerParams(vmem_limit_bytes=VMEM_BYTES),
    )(tokens, out_grad, own, other, count, ids, table_counts)


def halves_of_pairs(flat):
    rows = jnp.pad(flat.reshape(LAYERS, FLAT, LANES), ((0, 0), (0, BLOCK), (0, 0)))

    def blocks(skip):
        parts = [rows[:, 145 * chip + skip : 145 * chip + skip + BLOCK] for chip in range(16)]
        return jnp.stack([jnp.stack(parts[at::4]) for at in range(4)])

    return blocks(0), blocks(72)


def pairs_joined(even, odd):
    joined = []
    for chip in range(16):
        first, second = even[chip % 4, chip // 4], odd[chip % 4, chip // 4]
        seam = jnp.concatenate([first[:, 72:73, 0:64], second[:, 0:1, 64:]], axis=2)
        joined += [first[:, 0:72], seam, second[:, 1:73]]
    return jnp.concatenate(joined, axis=1).reshape(LAYERS, PSIZE)


def swap_along(x, axis, bit):
    pairs = [(i, i ^ bit) for i in range(lax.axis_size(axis))]
    return lax.ppermute(x, axis, pairs)


def gather_pairs(flat_params):
    size = flat_params.shape[1]
    room = BLOCK * LANES - size
    part = jnp.where(
        lax.axis_index("core") == 0,
        jnp.pad(flat_params, ((0, 0), (0, room))),
        jnp.pad(flat_params, ((0, 0), (64, room - 64))),
    ).reshape(1, LAYERS, BLOCK, LANES)
    for bit in (2, 1):
        part = jnp.concatenate([part, swap_along(part, "z", bit)], axis=0)
    own = lax.all_gather(part, ("x", "y"), axis=0, tiled=False)
    return own, swap_along(own, "core", 1)


def reduce_pairs(keep, give, size):
    got = swap_along(give, "core", 1)
    part = (keep.astype(F32) + got.astype(F32)).astype(BF16)
    part = lax.all_to_all(part, ("x", "y"), 0, 0, tiled=True)
    part = jnp.sum(part.astype(F32), axis=0)
    z = lax.axis_index("z")
    for bit in (2, 1):
        high = (z // bit) % 2
        stay = lax.dynamic_slice_in_dim(part, high * bit, bit, 0)
        go = lax.dynamic_slice_in_dim(part, (1 - high) * bit, bit, 0).astype(BF16)
        part = stay + swap_along(go, "z", bit).astype(F32)
    total = part.reshape(LAYERS, BLOCK * LANES)
    return jnp.where(
        lax.axis_index("core") == 0, total[:, 0:size], total[:, 64 : 64 + size]
    )


def body(axes, tokens, out_grad, flat_params, feat_count, table_ids, table_counts):
    four = "core" in axes
    count, ids = feat_count[None, :], table_ids[None, :]
    if four:
        own, other = gather_pairs(flat_params)
    else:
        own, other = halves_of_pairs(lax.all_gather(flat_params, axes, axis=1, tiled=True))
        turn = jnp.array([0, 2, 1, 3])
        own, other = own[:, turn], other[:, turn]
    turned = jnp.transpose(tokens, (1, 2, 0))
    turned_grad = jnp.transpose(out_grad, (1, 2, 0))
    results = [
        run_kernel(
            four,
            turned[:, :, at : at + ROWS],
            turned_grad[:, :, at : at + ROWS],
            own,
            other,
            count[:, at : at + ROWS],
            ids[:, at : at + ROWS],
            table_counts[None, :],
        )
        for at in range(0, tokens.shape[0], ROWS)
    ]
    out, in_grad, keep, give = results[0]
    if len(results) > 1:
        out = jnp.concatenate([r[0] for r in results], axis=2)
        in_grad = jnp.concatenate([r[1] for r in results], axis=2)
        keep = sum(r[2].astype(F32) for r in results)
        give = sum(r[3].astype(F32) for r in results)
    if four:
        grads = reduce_pairs(keep, give, flat_params.shape[1])
    else:
        flat = pairs_joined(keep.astype(F32), give.astype(F32))
        grads = lax.psum_scatter(flat, axes, scatter_dimension=1, tiled=True)
    return jnp.transpose(out, (2, 0, 1)), jnp.transpose(in_grad, (2, 0, 1)), grads


def solution(mesh):
    axes = mesh.axis_names
    if tuple(mesh.devices.shape) == (8, 4):
        axes = ("z", "x", "y", "core")
        mesh = jax.sharding.Mesh(mesh.devices.reshape(4, 2, 2, 2), axes)
    rows = P(axes, None, None)
    placed = (rows, rows, P(None, axes), P(axes), P(axes), P())
    return jax.shard_map(
        functools.partial(body, axes),
        mesh=mesh,
        in_specs=placed,
        out_specs=(rows, rows, P(None, axes)),
        check_vma=False,
    )
```

```python
import functools
import math

import jax
import jax.numpy as jnp
from jax import lax
from jax.experimental import pallas as pl
from jax.experimental.pallas import tpu as pltpu
from jax.sharding import PartitionSpec as P

D = 192
FF = 256
HEADS = 8
HEAD_DIM = 24
SEQ = 17
LAYERS = 2
PSIZE = 296960
ROWS = 128
SLOTS = 18
LANES = 128
FORWARD_GROUPS = 8
BACKWARD_GROUPS = 16
DEPTH = 8
BAND = 32
GROUP = 8
GROUPS = ROWS // GROUP
GT = SLOTS * GROUP
QL = HEADS * GT
TOKENS = SLOTS * ROWS
CHUNK = 2 * ROWS
CHUNKS = TOKENS // CHUNK
HALVES = (slice(0, ROWS), slice(ROWS, CHUNK))
FLAT = PSIZE // LANES
BLOCK = 80
EPS = 1e-05
VMEM_BYTES = 60 * 1024 * 1024
SCALE = 1.0 / math.sqrt(HEAD_DIM)
F32 = jnp.float32
BF16 = jnp.bfloat16


def dot(a, b, ca, cb):
    return lax.dot_general(a, b, (((ca,), (cb,)), ((), ())), preferred_element_type=F32)


def lane_half(shape):
    return lax.broadcasted_iota(jnp.int32, shape, len(shape) - 1) < 64


def swap(x):
    return pltpu.roll(x, 64, x.ndim - 1)


def low_half(x):
    return jnp.where(lane_half(x.shape), x, 0.0)


def splice(a, b):
    return swap(jnp.where(lane_half(a.shape), b, a))


def after(a, b):
    return jnp.where(lane_half(a.shape), a, swap(b))


def wide(column):
    return jnp.concatenate([column, column], axis=1)


def gather_flat(own, other, place, layer, flat):
    z, core = place[0], place[1]
    for chip in range(FLAT // 145):
        turn = z ^ (chip // 4)
        at = (turn & 1) * 2 + turn // 2
        mine = own[chip % 4, at, layer].astype(F32)
        theirs = other[chip % 4, at, layer].astype(F32)
        first = jnp.where(core == 0, mine, theirs)
        second = jnp.where(core == 0, theirs, mine)
        base = 145 * chip
        flat[pl.ds(base, BLOCK), :] = first
        flat[pl.ds(base + 72, BLOCK), :] = second
        flat[pl.ds(base + 72, 1), :] = jnp.where(
            lane_half((1, LANES)), first[72:73], second[0:1]
        )


def unpack(flat, w, tmp):
    def rows(start, count, stride):
        return flat[pl.ds(start, count, stride=stride), :]

    def row(index):
        return flat[pl.ds(index, 1), :]

    def pair_row(a, b):
        return jnp.concatenate([a, b], axis=1)

    vectors = [
        pair_row(row(0), low_half(row(1))),
        pair_row(splice(row(1), row(2)), low_half(swap(row(2)))),
        pair_row(row(1158), low_half(row(1159))),
        pair_row(splice(row(1159), row(1160)), low_half(swap(row(1160)))),
        pair_row(row(1161), low_half(row(1162))),
        pair_row(splice(row(2318), row(2319)), low_half(swap(row(2319)))),
    ]
    index = lax.broadcasted_iota(jnp.int32, (16, 2 * LANES), 0)
    stacked = jnp.zeros((16, 2 * LANES), F32)
    for i, vector in enumerate(vectors):
        stacked = jnp.where(index == i, vector, stacked)
    stacked = stacked.astype(BF16)
    for i in range(6):
        pick = jnp.where(index[:, 0:LANES] == i, 1.0, 0.0).astype(BF16)
        w["cols"][i] = dot(stacked, pick, 0, 0)[0:D]

    e = [rows(3 + j, 96, 9) for j in range(9)]
    even = (e[0], low_half(e[1]), splice(e[1], e[2]), low_half(swap(e[2])), e[3], low_half(e[4]))
    odd = (
        splice(e[4], e[5]),
        low_half(swap(e[5])),
        e[6],
        low_half(e[7]),
        splice(e[7], e[8]),
        low_half(swap(e[8])),
    )
    zero_row = jnp.zeros((1, LANES), F32)
    bias = (
        row(867),
        low_half(row(868)),
        zero_row,
        zero_row,
        splice(row(868), row(869)),
        low_half(swap(row(869))),
    )
    first_row = lax.broadcasted_iota(jnp.int32, (16, LANES), 0) == 0
    for j in range(6):
        tmp[j % 2, pl.ds(0, 96, stride=2), :] = even[j]
        tmp[j % 2, pl.ds(1, 96, stride=2), :] = odd[j]
        w["qkv"][0:D, j * LANES : (j + 1) * LANES] = tmp[j % 2, 0:D, :].astype(BF16)
        w["qkv"][D : D + 16, j * LANES : (j + 1) * LANES] = jnp.where(
            first_row, jnp.broadcast_to(bias[j], (16, LANES)), 0.0
        ).astype(BF16)

    e = [rows(870 + j, 96, 3) for j in range(3)]
    tmp[0, pl.ds(0, 96, stride=2), :] = e[0]
    tmp[1, pl.ds(0, 96, stride=2), :] = low_half(e[1])
    tmp[0, pl.ds(1, 96, stride=2), :] = splice(e[1], e[2])
    tmp[1, pl.ds(1, 96, stride=2), :] = low_half(swap(e[2]))
    w_out = jnp.concatenate([tmp[0, 0:D, :], tmp[1, 0:D, :]], axis=1)
    w["out_t"][...] = jnp.transpose(w_out.astype(BF16))[0:D]

    g = [rows(1162 + j, 192, 4) for j in range(5)]
    tiles = [splice(g[j], g[j + 1]) for j in range(4)]
    gate_up = jnp.concatenate(tiles, axis=1)
    w["gu"][...] = gate_up.astype(BF16)
    bias_row = jnp.concatenate(
        [splice(row(1930 + j), row(1931 + j)) for j in range(4)], axis=1
    )
    bias_rows = jnp.where(
        lax.broadcasted_iota(jnp.int32, (64, 2 * FF), 0) == 0,
        jnp.broadcast_to(bias_row, (64, 2 * FF)),
        0.0,
    )
    w["gu_t"][...] = jnp.transpose(jnp.concatenate([gate_up, bias_rows], axis=0).astype(BF16))[
        :, 0 : D + 16
    ]

    e = [rows(1934 + j, 128, 3) for j in range(4)]
    tmp[0, pl.ds(0, 128, stride=2), :] = splice(e[0], e[1])
    tmp[1, pl.ds(0, 128, stride=2), :] = low_half(swap(e[1]))
    tmp[0, pl.ds(1, 128, stride=2), :] = e[2]
    tmp[1, pl.ds(1, 128, stride=2), :] = low_half(e[3])
    w_down = jnp.concatenate([tmp[0, 0:FF, :], tmp[1, 0:FF, :]], axis=1)
    w["down"][...] = w_down[:, 0:D].astype(BF16)
    w["down_t"][...] = jnp.transpose(w_down.astype(BF16))[0:D]


def row_of(columns):
    turned = jnp.sum(jnp.transpose(columns), axis=0, keepdims=True)
    return turned[:, 0:LANES], jnp.concatenate(
        [turned[:, LANES:D], jnp.zeros((1, LANES - (D - LANES)), F32)], axis=1
    )


def pack(flat, acc, sums, tmp):
    def put(start, count, stride, value):
        flat[pl.ds(start, count, stride=stride), :] = value

    def put_row(index, value):
        flat[pl.ds(index, 1), :] = value

    def down(j, start, count, stride):
        return acc["down"][j, pl.ds(start, count, stride=stride), :]

    g1 = row_of(sums[0])
    b1 = row_of(sums[1])
    g2 = row_of(sums[2])
    b2 = row_of(sums[3])
    bo = row_of(sums[4])
    put_row(0, g1[0])
    put_row(1, after(g1[1], b1[0]))
    put_row(2, splice(b1[0], b1[1]))

    even = [acc["qkv"][j, pl.ds(0, 96, stride=2), :] for j in range(6)]
    odd = [acc["qkv"][j, pl.ds(1, 96, stride=2), :] for j in range(6)]
    put(3, 96, 9, even[0])
    put(4, 96, 9, after(even[1], even[2]))
    put(5, 96, 9, splice(even[2], even[3]))
    put(6, 96, 9, even[4])
    put(7, 96, 9, after(even[5], odd[0]))
    put(8, 96, 9, splice(odd[0], odd[1]))
    put(9, 96, 9, odd[2])
    put(10, 96, 9, after(odd[3], odd[4]))
    put(11, 96, 9, splice(odd[4], odd[5]))
    bias = [acc["qkv"][j, D : D + 1, :] for j in range(6)]
    put_row(867, bias[0])
    put_row(868, after(bias[1], bias[4]))
    put_row(869, splice(bias[4], bias[5]))

    w_out = jnp.transpose(
        jnp.concatenate([acc["out_t"][...], jnp.zeros((64, D), F32)], axis=0)
    )
    tmp[0, 0:D, :] = w_out[:, 0:LANES]
    tmp[1, 0:D, :] = w_out[:, LANES:]
    even = [tmp[j, pl.ds(0, 96, stride=2), :] for j in range(2)]
    odd = [tmp[j, pl.ds(1, 96, stride=2), :] for j in range(2)]
    put(870, 96, 3, even[0])
    put(871, 96, 3, after(even[1], odd[0]))
    put(872, 96, 3, splice(odd[0], odd[1]))
    put_row(1158, bo[0])
    put_row(1159, after(bo[1], g2[0]))
    put_row(1160, splice(g2[0], g2[1]))
    put_row(1161, b2[0])

    gu = [acc["gu"][j, 0 : D + 8, :] for j in range(4)]
    put_row(1162, after(b2[1], gu[0][0:1]))
    put(1166, 192, 4, splice(gu[3][0:192], acc["gu"][0, pl.ds(1, 192), :]))
    for j in range(1, 4):
        joined = splice(gu[j - 1], gu[j])
        put(1162 + j, 192, 4, joined[0:192])
        put_row(1930 + j, joined[192:193])
    put_row(1934, splice(gu[3][192:193], acc["down"][0, 0:1, :]))

    w0e, w1e = down(0, 0, 128, 2), down(1, 0, 128, 2)
    w0o, w1o = down(0, 1, 128, 2), down(1, 1, 128, 2)
    put(1935, 128, 3, splice(w0e, w1e))
    put(1936, 128, 3, w0o)
    put(1937, 128, 3, after(w1o, down(0, 2, 128, 2)))
    put_row(2319, splice(acc["down"][0, FF : FF + 1, :], acc["down"][1, FF : FF + 1, :]))


def scatter_blocks(flat, place, layer, keep, give):
    core = place[1]
    for chip in range(FLAT // 145):
        first = flat[pl.ds(145 * chip, BLOCK), :]
        second = flat[pl.ds(145 * chip + 72, BLOCK), :]
        z = chip // 4
        at = (z & 1) * 2 + z // 2
        keep[chip % 4, at, layer] = jnp.where(core == 0, first, second).astype(BF16)
        give[chip % 4, at, layer] = jnp.where(core == 0, second, first).astype(BF16)


def norm(x, gain, bias):
    centre = x - jnp.sum(x, axis=0, keepdims=True) * (1.0 / D)
    variance = jnp.sum(centre * centre, axis=0, keepdims=True) * (1.0 / D)
    rstd = lax.rsqrt(variance + EPS)
    xhat = centre * rstd
    return xhat, rstd, (xhat * gain + bias).astype(BF16)


def norm_back(grad, xhat, rstd, gain):
    e = gain * grad
    mean_e = jnp.sum(e, axis=0, keepdims=True) * (1.0 / D)
    mean_ex = jnp.sum(e * xhat, axis=0, keepdims=True) * (1.0 / D)
    return rstd * (e - mean_e - xhat * mean_ex)


def fold(x):
    return x[:, 0:LANES] + x[:, LANES:]


def gelu_parts(gate):
    z = gate * (1.0 / math.sqrt(2.0))
    cdf = 0.5 * lax.erf(z) + 0.5
    bell = jnp.exp2(z * z * (-1.0 / math.log(2.0)))
    return cdf, cdf + (z * bell) * (1.0 / math.sqrt(math.pi))


def to_groups(x):
    n = x.shape[-1]
    x = x.reshape(2, GROUPS, GROUP, n)
    return jnp.concatenate([x[0][:, None], x[1][:, None]], axis=1).reshape(
        GROUPS, 2 * GROUP, n
    )


def from_groups(x):
    n = x.shape[-1]
    x = x.reshape(GROUPS, 2, GROUP, n)
    return jnp.concatenate([x[:, 0], x[:, 1]], axis=0).reshape(CHUNK, n)


def group_rows(c):
    return slice(2 * GROUP * c, 2 * GROUP * (c + 1))


def skewed(stages):
    held = {}
    for tick in range(CHUNKS + len(stages) - 1):
        for j, stage in enumerate(stages):
            c = tick - j
            if 0 <= c < CHUNKS:
                held[c] = stage(c, held.get(c))


def view(ref, c, rows=None):
    return ref.at[0 : ref.shape[0] if rows is None else rows, c * CHUNK : (c + 1) * CHUNK]


def project_stages(s, w):
    def project(c, _):
        lows = []
        for half in HALVES:
            xhat, rstd, low = norm(
                view(s["x"], c).at[:, half][...], w["cols"][0], w["cols"][1]
            )
            view(s["xhat1"], c).at[:, half][...] = xhat
            view(s["rstd1"], c).at[:, half][...] = rstd
            lows.append(low)
        view(s["h1"], c, D)[...] = jnp.concatenate(lows, axis=1)
        return dot(view(s["h1"], c)[...], w["qkv"][...], 0, 0)

    def keep(c, qkv):
        place = group_rows(c)
        s["q"][:, place, :] = to_groups(qkv[:, 0:D]).astype(BF16)
        for name, start in (("k", 256), ("v", 512)):
            part = qkv[:, start : start + D].reshape(2, GROUPS, GROUP, D)
            turned = jnp.concatenate(
                [
                    pltpu.roll(part[t], (2 * c + t) % GROUP, 1)[:, None]
                    for t in range(2)
                ],
                axis=1,
            )
            s[name][:, place, :] = turned.reshape(GROUPS, 2 * GROUP, D).astype(BF16)

    return project, keep


def spread(values, masks):
    n = values.shape[1]
    doubled = [
        jnp.concatenate([values[8 * a : 8 * a + 8], values[8 * a : 8 * a + 8]], axis=0).astype(BF16)
        for a in range(3)
    ]
    parts = [doubled[a] * masks[m][:, 0:n] for a in range(2) for m in range(4)]
    parts.append(doubled[2] * masks[4][:, 0:n])
    return jnp.concatenate(parts, axis=0)


def collect(scores, bits):
    n = scores.shape[1]
    bits = [bit[:, 0:n] for bit in bits]
    out = []
    for a in range(2):
        level = [scores[64 * a + 8 * j : 64 * a + 8 * j + 8] for j in range(8)]
        for bit in bits:
            level = [
                jnp.where(bit, level[2 * i + 1], level[2 * i]) for i in range(len(level) // 2)
            ]
        out.append(level[0])
    out.append(scores[128:136])
    return out


def blocks_of(turned, t, halves):
    first = turned[48 * t : 48 * t + 16]
    middle = turned[48 * t + 16 : 48 * t + 32]
    last = turned[48 * t + 32 : 48 * t + 48]
    none = jnp.zeros_like(first)
    return jnp.concatenate(
        [
            jnp.concatenate([first, none], axis=1),
            jnp.concatenate([middle * halves[0], middle * halves[1]], axis=1),
            jnp.concatenate([none, last], axis=1),
        ],
        axis=0,
    )


def padded(block, t):
    parts = [block]
    if t > 0:
        parts.insert(0, jnp.zeros((48 * t, block.shape[1]), BF16))
    if t < 3:
        parts.append(jnp.zeros((48 * (3 - t), block.shape[1]), BF16))
    return jnp.concatenate(parts, axis=0)


def tail_of(rows, heads):
    return jnp.concatenate([rows * heads[h, 0:1, :] for h in range(HEADS)], axis=0)


def heads_joined(tiles, tail, heads, scale=None):
    main = []
    for tile in tiles:
        main += [tile[0:HEAD_DIM, 0:LANES], tile[HEAD_DIM:, LANES:]]
    main = jnp.concatenate(main, axis=0)
    if scale is not None:
        main, tail = main * scale, tail * scale
    main = jnp.transpose(main.astype(BF16))
    tail = tail.astype(BF16)
    last = tail[0:16] * heads[0, 0:1, :]
    for h in range(1, HEADS):
        last += tail[16 * h : 16 * h + 16] * heads[h, 0:1, :]
    return main, last


def softmax(kept, diff, limit):
    n = kept[0].shape[1]
    own = diff[:, 0:n]
    limit = limit[:, 0:n]
    slot = own.astype(F32)
    scale = SCALE / math.log(2.0)
    low = -1e9 / math.log(2.0)
    shown = [
        jnp.where(slot <= limit, kept[0] * scale, low),
        jnp.where(slot + 8.0 <= limit, kept[1] * scale, low),
        jnp.where(own == 0, jnp.where(limit >= 16.0, kept[2] * scale, low), -3e38),
    ]
    top = jnp.max(jnp.maximum(jnp.maximum(shown[0], shown[1]), shown[2]), axis=0, keepdims=True)
    shown = [jnp.exp2(part - top) for part in shown]
    inverse = 1.0 / jnp.sum(shown[0] + shown[1] + shown[2], axis=0, keepdims=True)
    return jnp.concatenate([part * inverse for part in shown], axis=0)


def staged(items, first, second):
    waiting = []
    for item in items:
        waiting.append((item, first(item)))
        if len(waiting) > DEPTH:
            second(*waiting.pop(0))
    for entry in waiting:
        second(*entry)


def batches(size, run):
    if size == GROUPS:
        run(0)
        return

    def step(i, carry):
        run(i * size)
        return carry

    lax.fori_loop(0, GROUPS // size, step, 0)


def forward_attention(s, env):
    diff = env["diff"][...]
    bits = [(diff & (1 << i)) != 0 for i in range(3)]
    halves = [env["halves"][i] for i in range(2)]

    def run(base):
        state = {}

        def load(u):
            g = base + u
            queries, values = s["q"][g], s["v"][g]
            state[u] = {
                "g": g,
                "queries": queries,
                "keys": s["k"][g],
                "turned": jnp.transpose(queries)[:, 0:LANES],
                "values": values,
                "turned_values": jnp.transpose(values),
                "count": env["count"][pl.ds(g, 1), :],
                "tiles": [],
            }

        def scores(item):
            u, t = item
            if t == 0:
                load(u)
            at = state[u]
            if t < 4:
                return dot(at["keys"], padded(blocks_of(at["turned"], t, halves), t), 1, 0)
            return dot(at["keys"], tail_of(at["queries"][LANES:GT], env["heads"]), 1, 1)

        def mix(item, products):
            u, t = item
            at = state[u]
            attention = softmax(collect(products, bits), diff, at["count"])
            s["att"][at["g"], :, t * CHUNK : min((t + 1) * CHUNK, QL)] = attention
            low = spread(attention, env["masks"])
            if t < 4:
                at["tiles"].append(dot(at["turned_values"][48 * t : 48 * t + 48], low, 1, 0))
                return
            tail = dot(low, at["values"], 0, 0)
            main, last = heads_joined(at["tiles"], tail, env["heads"])
            s["mixed"][at["g"], 0:LANES, :] = main
            s["mixed"][at["g"], LANES:GT, :] = last

        staged([(u, t) for u in range(FORWARD_GROUPS) for t in range(5)], scores, mix)

    batches(FORWARD_GROUPS, run)


def rest_stages(s, w, done):
    def attended(c, _):
        mixed = from_groups(s["mixed"][:, group_rows(c), :].astype(F32)).astype(BF16)
        return dot(w["out_t"][...], mixed, 1, 1)

    def normed(c, product):
        lows = []
        for half in HALVES:
            middle = view(s["x"], c).at[:, half][...] + (product[:, half] + w["cols"][2])
            view(s["middle"], c).at[:, half][...] = middle
            xhat, rstd, low = norm(middle, w["cols"][3], w["cols"][4])
            view(s["xhat2"], c).at[:, half][...] = xhat
            view(s["rstd2"], c).at[:, half][...] = rstd
            lows.append(low)
        view(s["h2"], c, D)[...] = jnp.concatenate(lows, axis=1)
        return dot(w["gu_t"][...], view(s["h2"], c)[...], 1, 0)

    def gated(c, gate_up):
        acts = []
        for r in range(0, FF, BAND):
            band = pl.ds(r, BAND)
            gate, up = gate_up[r : r + BAND], gate_up[FF + r : FF + r + BAND]
            cdf, slope = gelu_parts(gate)
            gelu = gate * cdf
            view(s["gelu"], c).at[band][...] = gelu
            view(s["slope"], c).at[band][...] = slope * up
            acts.append((gelu * up).astype(BF16))
        act = jnp.concatenate(acts, axis=0)
        view(s["act"], c, FF)[...] = act
        return dot(w["down_t"][...], act, 1, 0)

    def finish(c, product):
        for i, half in enumerate(HALVES):
            value = view(s["middle"], c).at[:, half][...]
            done(c, i, value + (product[:, half] + w["cols"][5]))

    return attended, normed, gated, finish


def add_tiles(ref, value):
    for j in range(ref.shape[0]):
        ref[j] += value[:, j * LANES : (j + 1) * LANES]


def add_narrow(ref, value):
    ref[0] += value[:, 0:LANES]
    ref[1, :, 0 : D - LANES] += value[:, LANES:D]


def rest_back_stages(s, w, acc, sums):
    def down(c, _):
        branch = view(s["g"], c)[...].astype(BF16)
        return dot(view(s["act"], c)[...], branch, 1, 1), dot(w["down"][...], branch, 1, 0)

    def gate_up(c, held):
        grad_down, d_act = held
        add_narrow(acc["down"], grad_down)
        gates, ups = [], []
        for r in range(0, FF, BAND):
            band = pl.ds(r, BAND)
            part = d_act[r : r + BAND]
            gates.append((part * view(s["slope"], c).at[band][...]).astype(BF16))
            ups.append((part * view(s["gelu"], c).at[band][...]).astype(BF16))
        d_gate_up = jnp.concatenate(gates + ups, axis=0)
        return dot(view(s["h2"], c)[...], d_gate_up, 1, 1), dot(w["gu"][...], d_gate_up, 1, 0)

    def normed(c, held):
        grad_gu, d_normed = held
        add_tiles(acc["gu"], grad_gu)
        lows = []
        for half in HALVES:
            xhat = view(s["xhat2"], c).at[:, half][...]
            part = d_normed[:, half]
            sums[2] += part * xhat
            sums[3] += part
            g = view(s["g"], c).at[:, half]
            d_middle = g[...] + norm_back(
                part, xhat, view(s["rstd2"], c).at[:, half][...], w["cols"][3]
            )
            g[...] = d_middle
            low = d_middle.astype(BF16)
            sums[4] += low.astype(F32)
            lows.append(low)
        d_attended = jnp.concatenate(lows, axis=1)
        mixed = from_groups(s["mixed"][:, group_rows(c), :].astype(F32)).astype(BF16)
        return dot(d_attended, w["out_t"][...], 0, 0), dot(d_attended, mixed, 1, 0)

    def finish(c, held):
        d_mixed, grad_out = held
        s["dqkv"][:, group_rows(c), 0:D] = to_groups(d_mixed).astype(BF16)
        acc["out_t"][...] += grad_out

    return down, gate_up, normed, finish


def backward_attention(s, env):
    diff = env["diff"][...]
    bits = [(diff & (1 << i)) != 0 for i in range(3)]
    halves = [env["halves"][i] for i in range(2)]

    def run(base):
        state = {}

        def load(u):
            g = base + u
            queries, keys, grads = s["q"][g], s["k"][g], s["dqkv"][g, :, 0:D]
            state[u] = {
                "g": g,
                "queries": queries,
                "grads": grads,
                "keys": keys,
                "values": s["v"][g],
                "turned": jnp.transpose(queries)[:, 0:LANES],
                "turned_grads": jnp.transpose(grads)[:, 0:LANES],
                "turned_keys": jnp.transpose(keys),
                "dq": [],
                "dk": [],
                "dv": [],
            }

        def products(item):
            u, t = item
            if t == 0:
                load(u)
            at = state[u]
            if t < 4:
                block = blocks_of(at["turned_grads"], t, halves)
                return block, dot(at["values"], padded(block, t), 1, 0)
            block = tail_of(at["grads"][LANES:GT], env["heads"])
            return block, dot(at["values"], block, 1, 1)

        def back(item, result):
            u, t = item
            at = state[u]
            grad_block, product = result
            attention = s["att"][at["g"], :, t * CHUNK : min((t + 1) * CHUNK, QL)]
            weighted = attention * jnp.concatenate(collect(product, bits), axis=0)
            total = jnp.sum(weighted, axis=0, keepdims=True)
            d_score = spread(weighted - attention * total, env["masks"])
            low = spread(attention, env["masks"])
            if t < 4:
                at["dv"].append(dot(grad_block, low, 1, 1))
                at["dk"].append(dot(blocks_of(at["turned"], t, halves), d_score, 1, 1))
                at["dq"].append(dot(at["turned_keys"][48 * t : 48 * t + 48], d_score, 1, 0))
                return
            d_values = dot(low, grad_block, 1, 0)
            d_keys = dot(d_score, tail_of(at["queries"][LANES:GT], env["heads"]), 1, 0)
            finish(at, d_values, d_keys, dot(d_score, at["keys"], 0, 0))

        def finish(at, d_values, d_keys, tail):
            g = at["g"]
            main, last = heads_joined(at["dq"], tail, env["heads"], SCALE)
            s["dqkv"][g, 0:LANES, 0:D] = main
            s["dqkv"][g, LANES:GT, 0:D] = last
            for parts, own, start, scale in (
                (at["dk"], d_keys, 256, SCALE),
                (at["dv"], d_values, 512, 1.0),
            ):
                value = jnp.transpose(jnp.concatenate(parts, axis=0)) + own
                slots = (value * scale).reshape(SLOTS, GROUP, D)
                turned = [
                    slots[k] if k % GROUP == 0 else pltpu.roll(slots[k], GROUP - k % GROUP, 0)
                    for k in range(SLOTS)
                ]
                s["dqkv"][g, :, start : start + D] = jnp.concatenate(turned, axis=0).astype(BF16)

        staged([(u, t) for u in range(BACKWARD_GROUPS) for t in range(5)], products, back)

    batches(BACKWARD_GROUPS, run)


def project_back_stages(s, w, acc, sums, done):
    def products(c, _):
        d_qkv = from_groups(s["dqkv"][:, group_rows(c), :].astype(F32)).astype(BF16)
        return dot(view(s["h1"], c)[...], d_qkv, 1, 0), dot(w["qkv"][0:D, :], d_qkv, 1, 1)

    def finish(c, held):
        grad_qkv, d_normed = held
        add_tiles(acc["qkv"], grad_qkv)
        for i, half in enumerate(HALVES):
            xhat = view(s["xhat1"], c).at[:, half][...]
            part = d_normed[:, half]
            sums[0] += part * xhat
            sums[1] += part
            back = norm_back(part, xhat, view(s["rstd1"], c).at[:, half][...], w["cols"][0])
            done(c, i, view(s["g"], c).at[:, half][...] + back)

    return products, finish


def per_layer():
    return {
        "xhat1": ((D, TOKENS), F32),
        "rstd1": ((1, TOKENS), F32),
        "h1": ((D + 16, TOKENS), BF16),
        "q": ((GROUPS, GT, D), BF16),
        "k": ((GROUPS, GT, D), BF16),
        "v": ((GROUPS, GT, D), BF16),
        "att": ((GROUPS, 24, QL), F32),
        "mixed": ((GROUPS, GT, D), BF16),
        "xhat2": ((D, TOKENS), F32),
        "rstd2": ((1, TOKENS), F32),
        "h2": ((D + 16, TOKENS), BF16),
        "act": ((FF + 16, TOKENS), BF16),
        "gelu": ((FF, TOKENS), F32),
        "slope": ((FF, TOKENS), F32),
    }


def weights():
    return {
        "cols": ((6, D, LANES), F32),
        "qkv": ((D + 16, 6 * LANES), BF16),
        "out_t": ((D, D), BF16),
        "gu": ((D, 2 * FF), BF16),
        "gu_t": ((2 * FF, D + 16), BF16),
        "down": ((FF, D), BF16),
        "down_t": ((D, FF), BF16),
    }


def accumulators():
    return {
        "qkv": ((6, D + 16, LANES), F32),
        "out_t": ((D, D), F32),
        "gu": ((4, D + 16, LANES), F32),
        "down": ((2, FF + 16, LANES), F32),
        "sums": ((5, D, LANES), F32),
    }


def common():
    full = (SEQ, D, ROWS)
    return {
        "halves": ((2, 16, LANES), BF16),
        "heads": ((HEADS, 16, D), BF16),
        "masks": ((5, 16, CHUNK), BF16),
        "diff": ((GROUP, CHUNK), jnp.int32),
        "count": ((GROUPS, CHUNK), F32),
        "dqkv": ((GROUPS, GT, 6 * LANES), BF16),
        "x": ((D, TOKENS), F32),
        "middle": ((D, TOKENS), F32),
        "g": ((D, TOKENS), F32),
        "flat": ((FLAT + 8, LANES), F32),
        "tmp": ((2, FF, LANES), F32),
        "tokens": (full, BF16),
        "out_grad": (full, BF16),
        "out": ((SLOTS, D, ROWS), F32),
    }


def make_scratch():
    shapes, names = [], []
    for prefix, table in (
        ("common", common()),
        ("acc0", accumulators()),
        ("acc1", accumulators()),
        ("s0", per_layer()),
        ("s1", per_layer()),
        ("w0", weights()),
        ("w1", weights()),
    ):
        for name, (shape, kind) in table.items():
            names.append((prefix, name))
            shapes.append(pltpu.VMEM(shape, kind))
    return names, shapes + [pltpu.SemaphoreType.DMA((6,))]


def init_env(env, count):
    lane = lax.broadcasted_iota(jnp.int32, (GROUP, CHUNK), 1)
    sub = lax.broadcasted_iota(jnp.int32, (GROUP, CHUNK), 0)
    diff = (sub - lane) & (GROUP - 1)
    env["diff"][...] = diff
    for m in range(5):
        first = jnp.where(diff == (2 * m) % 8, 1.0, 0.0)
        second = jnp.where(diff == 2 * m + 1, 1.0, 0.0)
        env["masks"][m] = jnp.concatenate([first, second], axis=0).astype(BF16)
    sub = lax.broadcasted_iota(jnp.int32, (16, LANES), 0)
    env["halves"][0] = jnp.where(sub < 8, 1.0, 0.0).astype(BF16)
    env["halves"][1] = jnp.where(sub < 8, 0.0, 1.0).astype(BF16)
    feature = lax.broadcasted_iota(jnp.int32, (16, D), 1) // HEAD_DIM
    for h in range(HEADS):
        env["heads"][h] = jnp.where(feature == h, 1.0, 0.0).astype(BF16)
    row = lax.broadcasted_iota(jnp.int32, (GROUPS, LANES), 1)
    group = lax.broadcasted_iota(jnp.int32, (GROUPS, LANES), 0)
    mine = jnp.where(row // GROUP == group, jnp.broadcast_to(count, (GROUPS, LANES)), 0.0)
    here = lax.broadcasted_iota(jnp.int32, (LANES, CHUNK), 0)
    there = lax.broadcasted_iota(jnp.int32, (LANES, CHUNK), 1)
    pick = jnp.where(here % GROUP == there % GROUP, 1.0, 0.0).astype(BF16)
    env["count"][...] = dot(mine.astype(BF16), pick, 1, 0)


def ones_below(ref, rows):
    tail = ref.shape[0] - rows
    mark = lax.broadcasted_iota(jnp.int32, (tail, ref.shape[1]), 0) == 0
    ref[rows:, :] = jnp.where(mark, 1.0, 0.0).astype(BF16)


def scales(ids, table_counts):
    counts = table_counts.astype(F32)
    tables = counts.shape[1]
    high = jnp.floor(counts * (1.0 / 32.0))
    table = lax.broadcasted_iota(jnp.int32, (tables, ROWS), 0)
    match = jnp.where(table == ids, 1.0, 0.0).astype(BF16)

    def pick(values):
        return dot(jnp.broadcast_to(values, (8, tables)).astype(BF16), match, 1, 0)[0:1]

    mine = 32.0 * pick(high) + pick(counts - 32.0 * high)
    return jnp.sqrt(jnp.sum(counts, axis=1, keepdims=True) * (1.0 / tables) / mine)


def kernel(names, four, *refs):
    inputs, outputs, scratch, sems = refs[0:7], refs[7:11], refs[11:-1], refs[-1]
    tokens, out_grad, own, other, feat_count, table_ids, table_counts = inputs
    out, in_grad, keep_out, give_out = outputs
    table = {}
    for (prefix, name), ref in zip(names, scratch):
        table.setdefault(prefix, {})[name] = ref
    env = table["common"]
    acc = [table["acc0"], table["acc1"]]
    s, w = [table["s0"], table["s1"]], [table["w0"], table["w1"]]
    sums = [part["sums"] for part in acc]
    place = (lax.axis_index("z"), lax.axis_index("core")) if four else (0, 0)

    copies = [
        pltpu.make_async_copy(source, env[name], sems.at[i])
        for i, (source, name) in enumerate(
            ((tokens, "tokens"), (out_grad, "out_grad"))
        )
    ]
    for copy in copies:
        copy.start()

    count = feat_count[...].astype(F32)
    init_env(env, count)
    pad = jnp.zeros((GROUPS, GT, 2 * LANES - D), BF16)
    for part in range(3):
        env["dqkv"][:, :, 2 * LANES * part + D : 2 * LANES * (part + 1)] = pad
    for layer in range(LAYERS):
        ones_below(s[layer]["h1"], D)
        ones_below(s[layer]["h2"], D)
        ones_below(s[layer]["act"], FF)
        for ref in acc[layer].values():
            ref[...] = jnp.zeros_like(ref)
    env["x"][:, SEQ * ROWS :] = jnp.zeros((D, ROWS), F32)
    env["g"][:, SEQ * ROWS :] = jnp.zeros((D, ROWS), F32)
    row_scale = scales(table_ids[...], table_counts[...])
    for layer in range(LAYERS):
        gather_flat(own, other, place, layer, env["flat"])
        unpack(env["flat"], w[layer], env["tmp"])
    copies[0].wait()
    copies[1].wait()
    for slot in range(SEQ):
        lanes = slice(slot * ROWS, (slot + 1) * ROWS)
        env["x"][:, lanes] = env["tokens"][slot].astype(F32)
        keep = jnp.where(count >= float(slot), row_scale, 0.0)
        env["g"][:, lanes] = env["out_grad"][slot].astype(F32) * keep

    def put(target):
        def done(c, i, value):
            target[2 * c + i] = value

        return done

    def set_to(target):
        def done(c, i, value):
            view(target, c).at[:, HALVES[i]][...] = value

        return done

    shared = {name: env[name] for name in ("x", "middle", "g", "dqkv")}
    s = [dict(part, **shared) for part in s]

    skewed(project_stages(s[0], w[0]))
    forward_attention(s[0], env)
    attended, normed, gated, finish = rest_stages(s[0], w[0], set_to(env["x"]))
    project, hold = project_stages(s[1], w[1])

    def finish_project(c, held):
        finish(c, held)
        return project(c, None)

    skewed((attended, normed, gated, finish_project, hold))
    forward_attention(s[1], env)
    attended, normed, gated, finish_out = rest_stages(s[1], w[1], put(env["out"]))
    down, gate_up, normed_back, finish_back = rest_back_stages(s[1], w[1], acc[1], sums[1])

    def gated_down(c, held):
        return gated(c, held), down(c, None)

    def finish_gate_up(c, held):
        finish_out(c, held[0])
        return gate_up(c, held[1])

    skewed((attended, normed, gated_down, finish_gate_up, normed_back, finish_back))
    out_copy = pltpu.make_async_copy(env["out"].at[0:SEQ], out, sems.at[4])
    out_copy.start()
    backward_attention(s[1], env)
    products, finish_project_back = project_back_stages(
        s[1], w[1], acc[1], sums[1], set_to(env["g"])
    )
    down, gate_up, normed_back, finish_back = rest_back_stages(s[0], w[0], acc[0], sums[0])

    def finish_down(c, held):
        finish_project_back(c, held)
        return down(c, None)

    skewed((products, finish_down, gate_up, normed_back, finish_back))

    def send(layer):
        pack(env["flat"], acc[layer], sums[layer], env["tmp"])
        scatter_blocks(env["flat"], place, layer, keep_out, give_out)

    send(1)
    backward_attention(s[0], env)
    out_copy.wait()
    skewed(project_back_stages(s[0], w[0], acc[0], sums[0], put(env["out"])))
    last = pltpu.make_async_copy(env["out"].at[0:SEQ], in_grad, sems.at[5])
    last.start()
    send(0)
    last.wait()


def run_kernel(four, tokens, out_grad, own, other, count, ids, table_counts):
    names, scratch = make_scratch()
    full = jax.ShapeDtypeStruct((SEQ, D, ROWS), F32)
    blocks = pltpu.VMEM(own.shape, BF16)
    own, other = (pltpu.with_memory_space_constraint(part, pltpu.VMEM) for part in (own, other))

    def body(*refs):
        kernel(names, four, *refs)

    vmem = pl.BlockSpec(memory_space=pltpu.VMEM)
    anywhere = pl.BlockSpec(memory_space=pl.ANY)
    return pl.pallas_call(
        body,
        out_shape=(full, full, blocks, blocks),
        in_specs=[anywhere] * 2 + [vmem] * 5,
        out_specs=[anywhere] * 2 + [vmem] * 2,
        scratch_shapes=scratch,
        compiler_params=pltpu.CompilerParams(vmem_limit_bytes=VMEM_BYTES),
    )(tokens, out_grad, own, other, count, ids, table_counts)


def halves_of_pairs(flat):
    rows = jnp.pad(flat.reshape(LAYERS, FLAT, LANES), ((0, 0), (0, BLOCK), (0, 0)))

    def blocks(skip):
        parts = [rows[:, 145 * chip + skip : 145 * chip + skip + BLOCK] for chip in range(16)]
        return jnp.stack([jnp.stack(parts[at::4]) for at in range(4)])

    return blocks(0), blocks(72)


def pairs_joined(even, odd):
    joined = []
    for chip in range(16):
        at = (chip // 4 % 2) * 2 + chip // 8
        first, second = even[chip % 4, at], odd[chip % 4, at]
        seam = jnp.concatenate([first[:, 72:73, 0:64], second[:, 0:1, 64:]], axis=2)
        joined += [first[:, 0:72], seam, second[:, 1:73]]
    return jnp.concatenate(joined, axis=1).reshape(LAYERS, PSIZE)


def swap_along(x, axis, bit):
    pairs = [(i, i ^ bit) for i in range(lax.axis_size(axis))]
    return lax.ppermute(x, axis, pairs)


def gather_pairs(flat_params):
    size = flat_params.shape[1]
    room = BLOCK * LANES - size
    part = jnp.where(
        lax.axis_index("core") == 0,
        jnp.pad(flat_params, ((0, 0), (0, room))),
        jnp.pad(flat_params, ((0, 0), (64, room - 64))),
    ).reshape(1, LAYERS, BLOCK, LANES)
    for bit in (2, 1):
        part = jnp.concatenate([part, swap_along(part, "z", bit)], axis=0)
    own = lax.all_gather(part, ("x", "y"), axis=0, tiled=False)
    return own, swap_along(own, "core", 1)


def reduce_pairs(keep, give, size):
    got = swap_along(give, "core", 1)
    part = (keep.astype(F32) + got.astype(F32)).astype(BF16)
    me = 2 * lax.axis_index("x") + lax.axis_index("y")
    total = lax.dynamic_index_in_dim(part, me, 0, False).astype(F32)
    for away in (3, 2, 1):
        pairs = [(i, i ^ away) for i in range(4)]
        theirs = lax.dynamic_index_in_dim(part, me ^ away, 0, False)
        total += lax.ppermute(theirs, ("x", "y"), pairs).astype(F32)
    part = total
    z = lax.axis_index("z")
    for bit, count in ((1, 2), (2, 1)):
        high = (z // bit) % 2
        stay = lax.dynamic_slice_in_dim(part, high * count, count, 0)
        go = lax.dynamic_slice_in_dim(part, (1 - high) * count, count, 0).astype(BF16)
        part = stay + swap_along(go, "z", bit).astype(F32)
    total = part.reshape(LAYERS, BLOCK * LANES)
    return jnp.where(
        lax.axis_index("core") == 0, total[:, 0:size], total[:, 64 : 64 + size]
    )


def body(axes, tokens, out_grad, flat_params, feat_count, table_ids, table_counts):
    four = "core" in axes
    count, ids = feat_count[None, :], table_ids[None, :]
    if four:
        own, other = gather_pairs(flat_params)
    else:
        own, other = halves_of_pairs(lax.all_gather(flat_params, axes, axis=1, tiled=True))
        turn = jnp.array([0, 2, 1, 3])
        own, other = own[:, turn], other[:, turn]
    turned = jnp.transpose(tokens, (1, 2, 0))
    turned_grad = jnp.transpose(out_grad, (1, 2, 0))
    results = [
        run_kernel(
            four,
            turned[:, :, at : at + ROWS],
            turned_grad[:, :, at : at + ROWS],
            own,
            other,
            count[:, at : at + ROWS],
            ids[:, at : at + ROWS],
            table_counts[None, :],
        )
        for at in range(0, tokens.shape[0], ROWS)
    ]
    out, in_grad, keep, give = results[0]
    if len(results) > 1:
        out = jnp.concatenate([r[0] for r in results], axis=2)
        in_grad = jnp.concatenate([r[1] for r in results], axis=2)
        keep = sum(r[2].astype(F32) for r in results)
        give = sum(r[3].astype(F32) for r in results)
    if four:
        grads = reduce_pairs(keep, give, flat_params.shape[1])
    else:
        flat = pairs_joined(keep.astype(F32), give.astype(F32))
        grads = lax.psum_scatter(flat, axes, scatter_dimension=1, tiled=True)
    return jnp.transpose(out, (2, 0, 1)), jnp.transpose(in_grad, (2, 0, 1)), grads


def solution(mesh):
    axes = mesh.axis_names
    if tuple(mesh.devices.shape) == (8, 4):
        axes = ("z", "x", "y", "core")
        mesh = jax.sharding.Mesh(mesh.devices.reshape(4, 2, 2, 2), axes)
    rows = P(axes, None, None)
    placed = (rows, rows, P(None, axes), P(axes), P(axes), P())
    return jax.shard_map(
        functools.partial(body, axes),
        mesh=mesh,
        in_specs=placed,
        out_specs=(rows, rows, P(None, axes)),
        check_vma=False,
    )
```

```python
import functools
import math

import jax
import jax.numpy as jnp
from jax import lax
from jax.experimental import pallas as pl
from jax.experimental.pallas import tpu as pltpu
from jax.sharding import PartitionSpec as P

D = 192
FF = 256
HEADS = 8
HEAD_DIM = 24
SEQ = 17
LAYERS = 2
PSIZE = 296960
ROWS = 128
SLOTS = 18
LANES = 128
FORWARD_GROUPS = 8
BACKWARD_GROUPS = 16
DEPTH = 8
BAND = 32
GROUP = 8
GROUPS = ROWS // GROUP
GT = SLOTS * GROUP
QL = HEADS * GT
TOKENS = SLOTS * ROWS
CHUNK = 2 * ROWS
CHUNKS = TOKENS // CHUNK
HALVES = (slice(0, ROWS), slice(ROWS, CHUNK))
FLAT = PSIZE // LANES
BLOCK = 80
EPS = 1e-05
VMEM_BYTES = 60 * 1024 * 1024
SCALE = 1.0 / math.sqrt(HEAD_DIM)
F32 = jnp.float32
BF16 = jnp.bfloat16


def dot(a, b, ca, cb):
    return lax.dot_general(a, b, (((ca,), (cb,)), ((), ())), preferred_element_type=F32)


def lane_half(shape):
    return lax.broadcasted_iota(jnp.int32, shape, len(shape) - 1) < 64


def swap(x):
    return pltpu.roll(x, 64, x.ndim - 1)


def low_half(x):
    return jnp.where(lane_half(x.shape), x, 0.0)


def splice(a, b):
    return swap(jnp.where(lane_half(a.shape), b, a))


def after(a, b):
    return jnp.where(lane_half(a.shape), a, swap(b))


def wide(column):
    return jnp.concatenate([column, column], axis=1)


def gather_flat(own, other, place, layer, flat):
    z, core, xy = place
    for chip in range(FLAT // 145):
        turn = z ^ (chip // 4)
        at = (turn & 1) * 2 + turn // 2
        mine = own[xy ^ (chip % 4), at, layer].astype(F32)
        theirs = other[xy ^ (chip % 4), at, layer].astype(F32)
        first = jnp.where(core == 0, mine, theirs)
        second = jnp.where(core == 0, theirs, mine)
        base = 145 * chip
        flat[pl.ds(base, BLOCK), :] = first
        flat[pl.ds(base + 72, BLOCK), :] = second
        flat[pl.ds(base + 72, 1), :] = jnp.where(
            lane_half((1, LANES)), first[72:73], second[0:1]
        )


def unpack(flat, w, tmp):
    def rows(start, count, stride):
        return flat[pl.ds(start, count, stride=stride), :]

    def row(index):
        return flat[pl.ds(index, 1), :]

    def pair_row(a, b):
        return jnp.concatenate([a, b], axis=1)

    vectors = [
        pair_row(row(0), low_half(row(1))),
        pair_row(splice(row(1), row(2)), low_half(swap(row(2)))),
        pair_row(row(1158), low_half(row(1159))),
        pair_row(splice(row(1159), row(1160)), low_half(swap(row(1160)))),
        pair_row(row(1161), low_half(row(1162))),
        pair_row(splice(row(2318), row(2319)), low_half(swap(row(2319)))),
    ]
    index = lax.broadcasted_iota(jnp.int32, (16, 2 * LANES), 0)
    stacked = jnp.zeros((16, 2 * LANES), F32)
    for i, vector in enumerate(vectors):
        stacked = jnp.where(index == i, vector, stacked)
    stacked = stacked.astype(BF16)
    for i in range(6):
        pick = jnp.where(index[:, 0:LANES] == i, 1.0, 0.0).astype(BF16)
        w["cols"][i] = dot(stacked, pick, 0, 0)[0:D]

    e = [rows(3 + j, 96, 9) for j in range(9)]
    even = (e[0], low_half(e[1]), splice(e[1], e[2]), low_half(swap(e[2])), e[3], low_half(e[4]))
    odd = (
        splice(e[4], e[5]),
        low_half(swap(e[5])),
        e[6],
        low_half(e[7]),
        splice(e[7], e[8]),
        low_half(swap(e[8])),
    )
    zero_row = jnp.zeros((1, LANES), F32)
    bias = (
        row(867),
        low_half(row(868)),
        zero_row,
        zero_row,
        splice(row(868), row(869)),
        low_half(swap(row(869))),
    )
    first_row = lax.broadcasted_iota(jnp.int32, (16, LANES), 0) == 0
    for j in range(6):
        tmp[j % 2, pl.ds(0, 96, stride=2), :] = even[j]
        tmp[j % 2, pl.ds(1, 96, stride=2), :] = odd[j]
        w["qkv"][0:D, j * LANES : (j + 1) * LANES] = tmp[j % 2, 0:D, :].astype(BF16)
        w["qkv"][D : D + 16, j * LANES : (j + 1) * LANES] = jnp.where(
            first_row, jnp.broadcast_to(bias[j], (16, LANES)), 0.0
        ).astype(BF16)

    e = [rows(870 + j, 96, 3) for j in range(3)]
    tmp[0, pl.ds(0, 96, stride=2), :] = e[0]
    tmp[1, pl.ds(0, 96, stride=2), :] = low_half(e[1])
    tmp[0, pl.ds(1, 96, stride=2), :] = splice(e[1], e[2])
    tmp[1, pl.ds(1, 96, stride=2), :] = low_half(swap(e[2]))
    w_out = jnp.concatenate([tmp[0, 0:D, :], tmp[1, 0:D, :]], axis=1)
    bias_rows = jnp.where(
        lax.broadcasted_iota(jnp.int32, (64, 2 * LANES), 0) == 0,
        jnp.broadcast_to(vectors[2], (64, 2 * LANES)),
        0.0,
    )
    w_out = jnp.concatenate([w_out, bias_rows], axis=0).astype(BF16)
    w["out_t"][...] = jnp.transpose(w_out)[0:D]

    g = [rows(1162 + j, 192, 4) for j in range(5)]
    tiles = [splice(g[j], g[j + 1]) for j in range(4)]
    gate_up = jnp.concatenate(tiles, axis=1)
    w["gu"][...] = gate_up.astype(BF16)
    bias_row = jnp.concatenate(
        [splice(row(1930 + j), row(1931 + j)) for j in range(4)], axis=1
    )
    bias_rows = jnp.where(
        lax.broadcasted_iota(jnp.int32, (64, 2 * FF), 0) == 0,
        jnp.broadcast_to(bias_row, (64, 2 * FF)),
        0.0,
    )
    w["gu_t"][...] = jnp.transpose(jnp.concatenate([gate_up, bias_rows], axis=0).astype(BF16))[
        :, 0 : D + 16
    ]

    e = [rows(1934 + j, 128, 3) for j in range(4)]
    tmp[0, pl.ds(0, 128, stride=2), :] = splice(e[0], e[1])
    tmp[1, pl.ds(0, 128, stride=2), :] = low_half(swap(e[1]))
    tmp[0, pl.ds(1, 128, stride=2), :] = e[2]
    tmp[1, pl.ds(1, 128, stride=2), :] = low_half(e[3])
    w_down = jnp.concatenate([tmp[0, 0:FF, :], tmp[1, 0:FF, :]], axis=1)
    w["down"][...] = w_down[:, 0:D].astype(BF16)
    w["down_t"][...] = jnp.transpose(w_down.astype(BF16))[0:D]


def row_of(columns):
    turned = jnp.sum(jnp.transpose(columns), axis=0, keepdims=True)
    return turned[:, 0:LANES], jnp.concatenate(
        [turned[:, LANES:D], jnp.zeros((1, LANES - (D - LANES)), F32)], axis=1
    )


def pack(flat, w, acc, sums, tmp):
    def put(start, count, stride, value):
        flat[pl.ds(start, count, stride=stride), :] = value

    def put_row(index, value):
        flat[pl.ds(index, 1), :] = value

    def down(j, start, count, stride):
        return acc["down"][j, pl.ds(start, count, stride=stride), :]

    def through(weight, name):
        total = jnp.zeros((D, LANES), F32)
        for j in range(acc[name].shape[0]):
            part = weight[0:D, j * LANES : (j + 1) * LANES].astype(F32)
            total += part * acc[name][j, D : D + 1, :]
        return row_of(total)

    g1 = row_of(sums[0])
    b1 = through(w["qkv"], "qkv")
    g2 = row_of(sums[1])
    b2 = through(w["gu"], "gu")
    w_out = jnp.transpose(acc["out_t"][...])
    bo = (
        w_out[D : D + 1, 0:LANES],
        jnp.concatenate([w_out[D : D + 1, LANES:], jnp.zeros((1, 64), F32)], axis=1),
    )
    put_row(0, g1[0])
    put_row(1, after(g1[1], b1[0]))
    put_row(2, splice(b1[0], b1[1]))

    even = [acc["qkv"][j, pl.ds(0, 96, stride=2), :] for j in range(6)]
    odd = [acc["qkv"][j, pl.ds(1, 96, stride=2), :] for j in range(6)]
    put(3, 96, 9, even[0])
    put(4, 96, 9, after(even[1], even[2]))
    put(5, 96, 9, splice(even[2], even[3]))
    put(6, 96, 9, even[4])
    put(7, 96, 9, after(even[5], odd[0]))
    put(8, 96, 9, splice(odd[0], odd[1]))
    put(9, 96, 9, odd[2])
    put(10, 96, 9, after(odd[3], odd[4]))
    put(11, 96, 9, splice(odd[4], odd[5]))
    bias = [acc["qkv"][j, D : D + 1, :] for j in range(6)]
    put_row(867, bias[0])
    put_row(868, after(bias[1], bias[4]))
    put_row(869, splice(bias[4], bias[5]))

    tmp[0, 0:D, :] = w_out[0:D, 0:LANES]
    tmp[1, 0:D, 0 : D - LANES] = w_out[0:D, LANES:]
    even = [tmp[j, pl.ds(0, 96, stride=2), :] for j in range(2)]
    odd = [tmp[j, pl.ds(1, 96, stride=2), :] for j in range(2)]
    put(870, 96, 3, even[0])
    put(871, 96, 3, after(even[1], odd[0]))
    put(872, 96, 3, splice(odd[0], odd[1]))
    put_row(1158, bo[0])
    put_row(1159, after(bo[1], g2[0]))
    put_row(1160, splice(g2[0], g2[1]))
    put_row(1161, b2[0])

    gu = [acc["gu"][j, 0 : D + 8, :] for j in range(4)]
    put_row(1162, after(b2[1], gu[0][0:1]))
    put(1166, 192, 4, splice(gu[3][0:192], acc["gu"][0, pl.ds(1, 192), :]))
    for j in range(1, 4):
        joined = splice(gu[j - 1], gu[j])
        put(1162 + j, 192, 4, joined[0:192])
        put_row(1930 + j, joined[192:193])
    put_row(1934, splice(gu[3][192:193], acc["down"][0, 0:1, :]))

    w0e, w1e = down(0, 0, 128, 2), down(1, 0, 128, 2)
    w0o, w1o = down(0, 1, 128, 2), down(1, 1, 128, 2)
    put(1935, 128, 3, splice(w0e, w1e))
    put(1936, 128, 3, w0o)
    put(1937, 128, 3, after(w1o, down(0, 2, 128, 2)))
    put_row(2319, splice(acc["down"][0, FF : FF + 1, :], acc["down"][1, FF : FF + 1, :]))


def scatter_blocks(flat, place, layer, keep, give):
    core = place[1]
    for chip in range(FLAT // 145):
        first = flat[pl.ds(145 * chip, BLOCK), :]
        second = flat[pl.ds(145 * chip + 72, BLOCK), :]
        z = chip // 4
        at = (z & 1) * 2 + z // 2
        keep[chip % 4, at, layer] = jnp.where(core == 0, first, second).astype(BF16)
        give[chip % 4, at, layer] = jnp.where(core == 0, second, first).astype(BF16)


def norm(x, gain, bias):
    centre = x - jnp.sum(x, axis=0, keepdims=True) * (1.0 / D)
    variance = jnp.sum(centre * centre, axis=0, keepdims=True) * (1.0 / D)
    rstd = lax.rsqrt(variance + EPS)
    xhat = centre * rstd
    return xhat, rstd, (xhat * gain + bias).astype(BF16)


def norm_back(grad, xhat, rstd, gain):
    e = gain * grad
    mean_e = jnp.sum(e, axis=0, keepdims=True) * (1.0 / D)
    mean_ex = jnp.sum(e * xhat, axis=0, keepdims=True) * (1.0 / D)
    return rstd * (e - mean_e - xhat * mean_ex)


def fold(x):
    return x[:, 0:LANES] + x[:, LANES:]


def gelu_parts(gate):
    z = gate * (1.0 / math.sqrt(2.0))
    cdf = 0.5 * lax.erf(z) + 0.5
    bell = jnp.exp2(z * z * (-1.0 / math.log(2.0)))
    return cdf, cdf + (z * bell) * (1.0 / math.sqrt(math.pi))


def to_groups(x):
    n = x.shape[-1]
    x = x.reshape(2, GROUPS, GROUP, n)
    return jnp.concatenate([x[0][:, None], x[1][:, None]], axis=1).reshape(
        GROUPS, 2 * GROUP, n
    )


def from_groups(x):
    n = x.shape[-1]
    x = x.reshape(GROUPS, 2, GROUP, n)
    return jnp.concatenate([x[:, 0], x[:, 1]], axis=0).reshape(CHUNK, n)


def group_rows(c):
    return slice(2 * GROUP * c, 2 * GROUP * (c + 1))


def skewed(stages):
    held = {}
    for tick in range(CHUNKS + len(stages) - 1):
        for j, stage in enumerate(stages):
            c = tick - j
            if 0 <= c < CHUNKS:
                held[c] = stage(c, held.get(c))


def view(ref, c, rows=None):
    return ref.at[0 : ref.shape[0] if rows is None else rows, c * CHUNK : (c + 1) * CHUNK]


def project_stages(s, w):
    def project(c, _):
        lows = []
        for half in HALVES:
            xhat, rstd, low = norm(
                view(s["x"], c).at[:, half][...], w["cols"][0], w["cols"][1]
            )
            view(s["xhat1"], c).at[:, half][...] = xhat
            view(s["rstd1"], c).at[:, half][...] = rstd
            lows.append(low)
        view(s["h1"], c, D)[...] = jnp.concatenate(lows, axis=1)
        return dot(view(s["h1"], c)[...], w["qkv"][...], 0, 0)

    def keep(c, qkv):
        place = group_rows(c)
        s["q"][:, place, :] = to_groups(qkv[:, 0:D]).astype(BF16)
        for name, start in (("k", 256), ("v", 512)):
            part = qkv[:, start : start + D].reshape(2, GROUPS, GROUP, D)
            turned = jnp.concatenate(
                [
                    pltpu.roll(part[t], (2 * c + t) % GROUP, 1)[:, None]
                    for t in range(2)
                ],
                axis=1,
            )
            s[name][:, place, :] = turned.reshape(GROUPS, 2 * GROUP, D).astype(BF16)

    return project, keep


def spread(values, masks):
    n = values.shape[1]
    doubled = [
        jnp.concatenate([values[8 * a : 8 * a + 8], values[8 * a : 8 * a + 8]], axis=0).astype(BF16)
        for a in range(3)
    ]
    parts = [doubled[a] * masks[m][:, 0:n] for a in range(2) for m in range(4)]
    parts.append(doubled[2] * masks[4][:, 0:n])
    return jnp.concatenate(parts, axis=0)


def collect(scores, bits):
    n = scores.shape[1]
    bits = [bit[:, 0:n] for bit in bits]
    out = []
    for a in range(2):
        level = [scores[64 * a + 8 * j : 64 * a + 8 * j + 8] for j in range(8)]
        for bit in bits:
            level = [
                jnp.where(bit, level[2 * i + 1], level[2 * i]) for i in range(len(level) // 2)
            ]
        out.append(level[0])
    out.append(scores[128:136])
    return out


def blocks_of(turned, t, halves):
    first = turned[48 * t : 48 * t + 16]
    middle = turned[48 * t + 16 : 48 * t + 32]
    last = turned[48 * t + 32 : 48 * t + 48]
    none = jnp.zeros_like(first)
    return jnp.concatenate(
        [
            jnp.concatenate([first, none], axis=1),
            jnp.concatenate([middle * halves[0], middle * halves[1]], axis=1),
            jnp.concatenate([none, last], axis=1),
        ],
        axis=0,
    )


def padded(block, t):
    parts = [block]
    if t > 0:
        parts.insert(0, jnp.zeros((48 * t, block.shape[1]), BF16))
    if t < 3:
        parts.append(jnp.zeros((48 * (3 - t), block.shape[1]), BF16))
    return jnp.concatenate(parts, axis=0)


def tail_of(rows, heads):
    return jnp.concatenate([rows * heads[h, 0:1, :] for h in range(HEADS)], axis=0)


def heads_joined(tiles, tail, heads, scale=None):
    main = []
    for tile in tiles:
        main += [tile[0:HEAD_DIM, 0:LANES], tile[HEAD_DIM:, LANES:]]
    main = jnp.concatenate(main, axis=0)
    if scale is not None:
        main, tail = main * scale, tail * scale
    main = jnp.transpose(main.astype(BF16))
    tail = tail.astype(BF16)
    last = tail[0:16] * heads[0, 0:1, :]
    for h in range(1, HEADS):
        last += tail[16 * h : 16 * h + 16] * heads[h, 0:1, :]
    return main, last


def softmax(kept, diff, limit):
    n = kept[0].shape[1]
    own = diff[:, 0:n]
    limit = limit[:, 0:n]
    slot = own.astype(F32)
    scale = SCALE / math.log(2.0)
    low = -1e9 / math.log(2.0)
    shown = [
        jnp.where(slot <= limit, kept[0] * scale, low),
        jnp.where(slot + 8.0 <= limit, kept[1] * scale, low),
        jnp.where(own == 0, jnp.where(limit >= 16.0, kept[2] * scale, low), -3e38),
    ]
    top = jnp.max(jnp.maximum(jnp.maximum(shown[0], shown[1]), shown[2]), axis=0, keepdims=True)
    shown = [jnp.exp2(part - top) for part in shown]
    inverse = 1.0 / jnp.sum(shown[0] + shown[1] + shown[2], axis=0, keepdims=True)
    return jnp.concatenate([part * inverse for part in shown], axis=0)


def staged(items, first, second):
    waiting = []
    for item in items:
        waiting.append((item, first(item)))
        if len(waiting) > DEPTH:
            second(*waiting.pop(0))
    for entry in waiting:
        second(*entry)


def batches(size, run):
    if size == GROUPS:
        run(0)
        return

    def step(i, carry):
        run(i * size)
        return carry

    lax.fori_loop(0, GROUPS // size, step, 0)


def forward_attention(s, env):
    diff = env["diff"][...]
    bits = [(diff & (1 << i)) != 0 for i in range(3)]
    halves = [env["halves"][i] for i in range(2)]

    def run(base):
        state = {}

        def load(u):
            g = base + u
            queries, values = s["q"][g], s["v"][g]
            state[u] = {
                "g": g,
                "queries": queries,
                "keys": s["k"][g],
                "turned": jnp.transpose(queries)[:, 0:LANES],
                "values": values,
                "turned_values": jnp.transpose(values),
                "count": env["count"][pl.ds(g, 1), :],
                "tiles": [],
            }

        def scores(item):
            u, t = item
            if t == 0:
                load(u)
            at = state[u]
            if t < 4:
                return dot(at["keys"], padded(blocks_of(at["turned"], t, halves), t), 1, 0)
            return dot(at["keys"], tail_of(at["queries"][LANES:GT], env["heads"]), 1, 1)

        def mix(item, products):
            u, t = item
            at = state[u]
            attention = softmax(collect(products, bits), diff, at["count"])
            s["att"][at["g"], :, t * CHUNK : min((t + 1) * CHUNK, QL)] = attention
            low = spread(attention, env["masks"])
            if t < 4:
                at["tiles"].append(dot(at["turned_values"][48 * t : 48 * t + 48], low, 1, 0))
                return
            tail = dot(low, at["values"], 0, 0)
            main, last = heads_joined(at["tiles"], tail, env["heads"])
            s["mixed"][at["g"], 0:LANES, 0:D] = main
            s["mixed"][at["g"], LANES:GT, 0:D] = last

        staged([(u, t) for u in range(FORWARD_GROUPS) for t in range(5)], scores, mix)

    batches(FORWARD_GROUPS, run)


def rest_stages(s, w, done):
    def attended(c, _):
        mixed = from_groups(s["mixed"][:, group_rows(c), :].astype(F32)).astype(BF16)
        return dot(w["out_t"][...], mixed, 1, 1)

    def normed(c, product):
        lows = []
        for half in HALVES:
            middle = view(s["x"], c).at[:, half][...] + product[:, half]
            view(s["middle"], c).at[:, half][...] = middle
            xhat, rstd, low = norm(middle, w["cols"][3], w["cols"][4])
            view(s["xhat2"], c).at[:, half][...] = xhat
            view(s["rstd2"], c).at[:, half][...] = rstd
            lows.append(low)
        view(s["h2"], c, D)[...] = jnp.concatenate(lows, axis=1)
        return dot(w["gu_t"][...], view(s["h2"], c)[...], 1, 0)

    def gated(c, gate_up):
        acts = []
        for r in range(0, FF, BAND):
            band = pl.ds(r, BAND)
            gate, up = gate_up[r : r + BAND], gate_up[FF + r : FF + r + BAND]
            cdf, slope = gelu_parts(gate)
            gelu = gate * cdf
            view(s["gelu"], c).at[band][...] = gelu
            view(s["slope"], c).at[band][...] = slope * up
            acts.append((gelu * up).astype(BF16))
        act = jnp.concatenate(acts, axis=0)
        view(s["act"], c, FF)[...] = act
        return dot(w["down_t"][...], act, 1, 0)

    def finish(c, product):
        for i, half in enumerate(HALVES):
            value = view(s["middle"], c).at[:, half][...]
            done(c, i, value + (product[:, half] + w["cols"][5]))

    return attended, normed, gated, finish


def add_tiles(ref, value):
    for j in range(ref.shape[0]):
        ref[j] += value[:, j * LANES : (j + 1) * LANES]


def add_narrow(ref, value):
    ref[0] += value[:, 0:LANES]
    ref[1, :, 0 : D - LANES] += value[:, LANES:D]


def rest_back_stages(s, w, acc, sums):
    def down(c, _):
        branch = view(s["g"], c)[...].astype(BF16)
        return dot(view(s["act"], c)[...], branch, 1, 1), dot(w["down"][...], branch, 1, 0)

    def gate_up(c, held):
        grad_down, d_act = held
        add_narrow(acc["down"], grad_down)
        gates, ups = [], []
        for r in range(0, FF, BAND):
            band = pl.ds(r, BAND)
            part = d_act[r : r + BAND]
            gates.append((part * view(s["slope"], c).at[band][...]).astype(BF16))
            ups.append((part * view(s["gelu"], c).at[band][...]).astype(BF16))
        d_gate_up = jnp.concatenate(gates + ups, axis=0)
        return dot(view(s["h2"], c)[...], d_gate_up, 1, 1), dot(w["gu"][...], d_gate_up, 1, 0)

    def normed(c, held):
        grad_gu, d_normed = held
        add_tiles(acc["gu"], grad_gu)
        lows = []
        for half in HALVES:
            xhat = view(s["xhat2"], c).at[:, half][...]
            part = d_normed[:, half]
            sums[1] += part * xhat
            g = view(s["g"], c).at[:, half]
            d_middle = g[...] + norm_back(
                part, xhat, view(s["rstd2"], c).at[:, half][...], w["cols"][3]
            )
            g[...] = d_middle
            lows.append(d_middle.astype(BF16))
        d_attended = jnp.concatenate(lows, axis=1)
        mixed = from_groups(s["mixed"][:, group_rows(c), :].astype(F32)).astype(BF16)
        return dot(d_attended, w["out_t"][:, 0:D], 0, 0), dot(d_attended, mixed, 1, 0)

    def finish(c, held):
        d_mixed, grad_out = held
        s["dqkv"][:, group_rows(c), 0:D] = to_groups(d_mixed).astype(BF16)
        acc["out_t"][...] += grad_out

    return down, gate_up, normed, finish


def backward_attention(s, env):
    diff = env["diff"][...]
    bits = [(diff & (1 << i)) != 0 for i in range(3)]
    halves = [env["halves"][i] for i in range(2)]

    def run(base):
        state = {}

        def load(u):
            g = base + u
            queries, keys, grads = s["q"][g], s["k"][g], s["dqkv"][g, :, 0:D]
            state[u] = {
                "g": g,
                "queries": queries,
                "grads": grads,
                "keys": keys,
                "values": s["v"][g],
                "turned": jnp.transpose(queries)[:, 0:LANES],
                "turned_grads": jnp.transpose(grads)[:, 0:LANES],
                "turned_keys": jnp.transpose(keys),
                "dq": [],
                "dk": [],
                "dv": [],
            }

        def products(item):
            u, t = item
            if t == 0:
                load(u)
            at = state[u]
            if t < 4:
                block = blocks_of(at["turned_grads"], t, halves)
                return block, dot(at["values"], padded(block, t), 1, 0)
            block = tail_of(at["grads"][LANES:GT], env["heads"])
            return block, dot(at["values"], block, 1, 1)

        def back(item, result):
            u, t = item
            at = state[u]
            grad_block, product = result
            attention = s["att"][at["g"], :, t * CHUNK : min((t + 1) * CHUNK, QL)]
            weighted = attention * jnp.concatenate(collect(product, bits), axis=0)
            total = jnp.sum(weighted, axis=0, keepdims=True)
            d_score = spread(weighted - attention * total, env["masks"])
            low = spread(attention, env["masks"])
            if t < 4:
                at["dv"].append(dot(grad_block, low, 1, 1))
                at["dk"].append(dot(blocks_of(at["turned"], t, halves), d_score, 1, 1))
                at["dq"].append(dot(at["turned_keys"][48 * t : 48 * t + 48], d_score, 1, 0))
                return
            d_values = dot(low, grad_block, 1, 0)
            d_keys = dot(d_score, tail_of(at["queries"][LANES:GT], env["heads"]), 1, 0)
            finish(at, d_values, d_keys, dot(d_score, at["keys"], 0, 0))

        def finish(at, d_values, d_keys, tail):
            g = at["g"]
            main, last = heads_joined(at["dq"], tail, env["heads"], SCALE)
            s["dqkv"][g, 0:LANES, 0:D] = main
            s["dqkv"][g, LANES:GT, 0:D] = last
            for parts, own, start, scale in (
                (at["dk"], d_keys, 256, SCALE),
                (at["dv"], d_values, 512, 1.0),
            ):
                value = jnp.transpose(jnp.concatenate(parts, axis=0)) + own
                slots = (value * scale).reshape(SLOTS, GROUP, D)
                turned = [
                    slots[k] if k % GROUP == 0 else pltpu.roll(slots[k], GROUP - k % GROUP, 0)
                    for k in range(SLOTS)
                ]
                s["dqkv"][g, :, start : start + D] = jnp.concatenate(turned, axis=0).astype(BF16)

        staged([(u, t) for u in range(BACKWARD_GROUPS) for t in range(5)], products, back)

    batches(BACKWARD_GROUPS, run)


def project_back_stages(s, w, acc, sums, done):
    def products(c, _):
        d_qkv = from_groups(s["dqkv"][:, group_rows(c), :].astype(F32)).astype(BF16)
        return dot(view(s["h1"], c)[...], d_qkv, 1, 0), dot(w["qkv"][0:D, :], d_qkv, 1, 1)

    def finish(c, held):
        grad_qkv, d_normed = held
        add_tiles(acc["qkv"], grad_qkv)
        for i, half in enumerate(HALVES):
            xhat = view(s["xhat1"], c).at[:, half][...]
            part = d_normed[:, half]
            sums[0] += part * xhat
            back = norm_back(part, xhat, view(s["rstd1"], c).at[:, half][...], w["cols"][0])
            done(c, i, view(s["g"], c).at[:, half][...] + back)

    return products, finish


def per_layer():
    return {
        "xhat1": ((D, TOKENS), F32),
        "rstd1": ((1, TOKENS), F32),
        "h1": ((D + 16, TOKENS), BF16),
        "q": ((GROUPS, GT, D), BF16),
        "k": ((GROUPS, GT, D), BF16),
        "v": ((GROUPS, GT, D), BF16),
        "att": ((GROUPS, 24, QL), F32),
        "mixed": ((GROUPS, GT, 2 * LANES), BF16),
        "xhat2": ((D, TOKENS), F32),
        "rstd2": ((1, TOKENS), F32),
        "h2": ((D + 16, TOKENS), BF16),
        "act": ((FF + 16, TOKENS), BF16),
        "gelu": ((FF, TOKENS), F32),
        "slope": ((FF, TOKENS), F32),
    }


def weights():
    return {
        "cols": ((6, D, LANES), F32),
        "qkv": ((D + 16, 6 * LANES), BF16),
        "out_t": ((D, 2 * LANES), BF16),
        "gu": ((D, 2 * FF), BF16),
        "gu_t": ((2 * FF, D + 16), BF16),
        "down": ((FF, D), BF16),
        "down_t": ((D, FF), BF16),
    }


def accumulators():
    return {
        "qkv": ((6, D + 16, LANES), F32),
        "out_t": ((D, 2 * LANES), F32),
        "gu": ((4, D + 16, LANES), F32),
        "down": ((2, FF + 16, LANES), F32),
        "sums": ((2, D, LANES), F32),
    }


def common():
    full = (SEQ, D, ROWS)
    return {
        "halves": ((2, 16, LANES), BF16),
        "heads": ((HEADS, 16, D), BF16),
        "masks": ((5, 16, CHUNK), BF16),
        "diff": ((GROUP, CHUNK), jnp.int32),
        "count": ((GROUPS, CHUNK), F32),
        "dqkv": ((GROUPS, GT, 6 * LANES), BF16),
        "x": ((D, TOKENS), F32),
        "middle": ((D, TOKENS), F32),
        "g": ((D, TOKENS), F32),
        "flat": ((FLAT + 8, LANES), F32),
        "tmp": ((2, FF, LANES), F32),
        "tokens": (full, BF16),
        "out_grad": (full, BF16),
        "out": ((SLOTS, D, ROWS), F32),
    }


def make_scratch():
    shapes, names = [], []
    for prefix, table in (
        ("common", common()),
        ("acc0", accumulators()),
        ("acc1", accumulators()),
        ("s0", per_layer()),
        ("s1", per_layer()),
        ("w0", weights()),
        ("w1", weights()),
    ):
        for name, (shape, kind) in table.items():
            names.append((prefix, name))
            shapes.append(pltpu.VMEM(shape, kind))
    return names, shapes + [pltpu.SemaphoreType.DMA((6,))]


def init_env(env, count):
    lane = lax.broadcasted_iota(jnp.int32, (GROUP, CHUNK), 1)
    sub = lax.broadcasted_iota(jnp.int32, (GROUP, CHUNK), 0)
    diff = (sub - lane) & (GROUP - 1)
    env["diff"][...] = diff
    for m in range(5):
        first = jnp.where(diff == (2 * m) % 8, 1.0, 0.0)
        second = jnp.where(diff == 2 * m + 1, 1.0, 0.0)
        env["masks"][m] = jnp.concatenate([first, second], axis=0).astype(BF16)
    sub = lax.broadcasted_iota(jnp.int32, (16, LANES), 0)
    env["halves"][0] = jnp.where(sub < 8, 1.0, 0.0).astype(BF16)
    env["halves"][1] = jnp.where(sub < 8, 0.0, 1.0).astype(BF16)
    feature = lax.broadcasted_iota(jnp.int32, (16, D), 1) // HEAD_DIM
    for h in range(HEADS):
        env["heads"][h] = jnp.where(feature == h, 1.0, 0.0).astype(BF16)
    row = lax.broadcasted_iota(jnp.int32, (GROUPS, LANES), 1)
    group = lax.broadcasted_iota(jnp.int32, (GROUPS, LANES), 0)
    mine = jnp.where(row // GROUP == group, jnp.broadcast_to(count, (GROUPS, LANES)), 0.0)
    here = lax.broadcasted_iota(jnp.int32, (LANES, CHUNK), 0)
    there = lax.broadcasted_iota(jnp.int32, (LANES, CHUNK), 1)
    pick = jnp.where(here % GROUP == there % GROUP, 1.0, 0.0).astype(BF16)
    env["count"][...] = dot(mine.astype(BF16), pick, 1, 0)


def ones_below(ref, rows):
    tail = ref.shape[0] - rows
    mark = lax.broadcasted_iota(jnp.int32, (tail, ref.shape[1]), 0) == 0
    ref[rows:, :] = jnp.where(mark, 1.0, 0.0).astype(BF16)


def scales(ids, table_counts):
    counts = table_counts.astype(F32)
    tables = counts.shape[1]
    high = jnp.floor(counts * (1.0 / 32.0))
    table = lax.broadcasted_iota(jnp.int32, (tables, ROWS), 0)
    match = jnp.where(table == ids, 1.0, 0.0).astype(BF16)

    def pick(values):
        return dot(jnp.broadcast_to(values, (8, tables)).astype(BF16), match, 1, 0)[0:1]

    mine = 32.0 * pick(high) + pick(counts - 32.0 * high)
    return jnp.sqrt(jnp.sum(counts, axis=1, keepdims=True) * (1.0 / tables) / mine)


def kernel(names, four, *refs):
    inputs, outputs, scratch, sems = refs[0:7], refs[7:11], refs[11:-1], refs[-1]
    tokens, out_grad, own, other, feat_count, table_ids, table_counts = inputs
    out, in_grad, keep_out, give_out = outputs
    table = {}
    for (prefix, name), ref in zip(names, scratch):
        table.setdefault(prefix, {})[name] = ref
    env = table["common"]
    acc = [table["acc0"], table["acc1"]]
    s, w = [table["s0"], table["s1"]], [table["w0"], table["w1"]]
    sums = [part["sums"] for part in acc]
    place = (0, 0, 0)
    if four:
        xy = 2 * lax.axis_index("x") + lax.axis_index("y")
        place = (lax.axis_index("z"), lax.axis_index("core"), xy)

    copies = [
        pltpu.make_async_copy(source, env[name], sems.at[i])
        for i, (source, name) in enumerate(
            ((tokens, "tokens"), (out_grad, "out_grad"))
        )
    ]
    for copy in copies:
        copy.start()

    count = feat_count[...].astype(F32)
    init_env(env, count)
    pad = jnp.zeros((GROUPS, GT, 2 * LANES - D), BF16)
    for part in range(3):
        env["dqkv"][:, :, 2 * LANES * part + D : 2 * LANES * (part + 1)] = pad
    for layer in range(LAYERS):
        mark = lax.broadcasted_iota(jnp.int32, (GROUPS, GT, 2 * LANES - D), 2) == 0
        s[layer]["mixed"][:, :, D:] = jnp.where(mark, 1.0, 0.0).astype(BF16)
        ones_below(s[layer]["h1"], D)
        ones_below(s[layer]["h2"], D)
        ones_below(s[layer]["act"], FF)
        for ref in acc[layer].values():
            ref[...] = jnp.zeros_like(ref)
    env["x"][:, SEQ * ROWS :] = jnp.zeros((D, ROWS), F32)
    env["g"][:, SEQ * ROWS :] = jnp.zeros((D, ROWS), F32)
    row_scale = scales(table_ids[...], table_counts[...])
    for layer in range(LAYERS):
        gather_flat(own, other, place, layer, env["flat"])
        unpack(env["flat"], w[layer], env["tmp"])
    copies[0].wait()
    copies[1].wait()
    for slot in range(SEQ):
        lanes = slice(slot * ROWS, (slot + 1) * ROWS)
        env["x"][:, lanes] = env["tokens"][slot].astype(F32)
        keep = jnp.where(count >= float(slot), row_scale, 0.0)
        env["g"][:, lanes] = env["out_grad"][slot].astype(F32) * keep

    def put(target):
        def done(c, i, value):
            target[2 * c + i] = value

        return done

    def set_to(target):
        def done(c, i, value):
            view(target, c).at[:, HALVES[i]][...] = value

        return done

    shared = {name: env[name] for name in ("x", "middle", "g", "dqkv")}
    s = [dict(part, **shared) for part in s]

    skewed(project_stages(s[0], w[0]))
    forward_attention(s[0], env)
    attended, normed, gated, finish = rest_stages(s[0], w[0], set_to(env["x"]))
    project, hold = project_stages(s[1], w[1])

    def finish_project(c, held):
        finish(c, held)
        return project(c, None)

    skewed((attended, normed, gated, finish_project, hold))
    forward_attention(s[1], env)
    attended, normed, gated, finish_out = rest_stages(s[1], w[1], put(env["out"]))
    down, gate_up, normed_back, finish_back = rest_back_stages(s[1], w[1], acc[1], sums[1])

    def gated_down(c, held):
        return gated(c, held), down(c, None)

    def finish_gate_up(c, held):
        finish_out(c, held[0])
        return gate_up(c, held[1])

    skewed((attended, normed, gated_down, finish_gate_up, normed_back, finish_back))
    out_copy = pltpu.make_async_copy(env["out"].at[0:SEQ], out, sems.at[4])
    out_copy.start()
    backward_attention(s[1], env)
    products, finish_project_back = project_back_stages(
        s[1], w[1], acc[1], sums[1], set_to(env["g"])
    )
    down, gate_up, normed_back, finish_back = rest_back_stages(s[0], w[0], acc[0], sums[0])

    def finish_down(c, held):
        finish_project_back(c, held)
        return down(c, None)

    skewed((products, finish_down, gate_up, normed_back, finish_back))

    def send(layer):
        pack(env["flat"], w[layer], acc[layer], sums[layer], env["tmp"])
        scatter_blocks(env["flat"], place, layer, keep_out, give_out)

    send(1)
    backward_attention(s[0], env)
    out_copy.wait()
    skewed(project_back_stages(s[0], w[0], acc[0], sums[0], put(env["out"])))
    last = pltpu.make_async_copy(env["out"].at[0:SEQ], in_grad, sems.at[5])
    last.start()
    send(0)
    last.wait()


def run_kernel(four, tokens, out_grad, own, other, count, ids, table_counts):
    names, scratch = make_scratch()
    full = jax.ShapeDtypeStruct((SEQ, D, ROWS), F32)
    blocks = pltpu.VMEM(own.shape, BF16)
    own, other = (pltpu.with_memory_space_constraint(part, pltpu.VMEM) for part in (own, other))

    def body(*refs):
        kernel(names, four, *refs)

    vmem = pl.BlockSpec(memory_space=pltpu.VMEM)
    anywhere = pl.BlockSpec(memory_space=pl.ANY)
    return pl.pallas_call(
        body,
        out_shape=(full, full, blocks, blocks),
        in_specs=[anywhere] * 2 + [vmem] * 5,
        out_specs=[anywhere] * 2 + [vmem] * 2,
        scratch_shapes=scratch,
        compiler_params=pltpu.CompilerParams(vmem_limit_bytes=VMEM_BYTES),
    )(tokens, out_grad, own, other, count, ids, table_counts)


def halves_of_pairs(flat):
    rows = jnp.pad(flat.reshape(LAYERS, FLAT, LANES), ((0, 0), (0, BLOCK), (0, 0)))

    def blocks(skip):
        parts = [rows[:, 145 * chip + skip : 145 * chip + skip + BLOCK] for chip in range(16)]
        return jnp.stack([jnp.stack(parts[at::4]) for at in range(4)])

    return blocks(0), blocks(72)


def pairs_joined(even, odd):
    joined = []
    for chip in range(16):
        at = (chip // 4 % 2) * 2 + chip // 8
        first, second = even[chip % 4, at], odd[chip % 4, at]
        seam = jnp.concatenate([first[:, 72:73, 0:64], second[:, 0:1, 64:]], axis=2)
        joined += [first[:, 0:72], seam, second[:, 1:73]]
    return jnp.concatenate(joined, axis=1).reshape(LAYERS, PSIZE)


def swap_along(x, axis, bit):
    pairs = [(i, i ^ bit) for i in range(lax.axis_size(axis))]
    return lax.ppermute(x, axis, pairs)


def gather_pairs(flat_params):
    size = flat_params.shape[1]
    room = BLOCK * LANES - size
    part = jnp.where(
        lax.axis_index("core") == 0,
        jnp.pad(flat_params, ((0, 0), (0, room))),
        jnp.pad(flat_params, ((0, 0), (64, room - 64))),
    ).reshape(1, LAYERS, BLOCK, LANES)
    for bit in (2, 1):
        part = jnp.concatenate([part, swap_along(part, "z", bit)], axis=0)
    parts = [part]
    for away in (1, 2, 3):
        pairs = [(i, i ^ away) for i in range(4)]
        parts.append(lax.ppermute(part, ("x", "y"), pairs))
    own = jnp.stack(parts)
    return own, swap_along(own, "core", 1)


def reduce_pairs(keep, give, size):
    got = swap_along(give, "core", 1)
    part = (keep.astype(F32) + got.astype(F32)).astype(BF16)
    me = 2 * lax.axis_index("x") + lax.axis_index("y")
    total = lax.dynamic_index_in_dim(part, me, 0, False).astype(F32)
    for away in (3, 2, 1):
        pairs = [(i, i ^ away) for i in range(4)]
        theirs = lax.dynamic_index_in_dim(part, me ^ away, 0, False)
        total += lax.ppermute(theirs, ("x", "y"), pairs).astype(F32)
    part = total
    z = lax.axis_index("z")
    for bit, count in ((1, 2), (2, 1)):
        high = (z // bit) % 2
        stay = lax.dynamic_slice_in_dim(part, high * count, count, 0)
        go = lax.dynamic_slice_in_dim(part, (1 - high) * count, count, 0).astype(BF16)
        part = stay + swap_along(go, "z", bit).astype(F32)
    total = part.reshape(LAYERS, BLOCK * LANES)
    return jnp.where(
        lax.axis_index("core") == 0, total[:, 0:size], total[:, 64 : 64 + size]
    )


def body(axes, tokens, out_grad, flat_params, feat_count, table_ids, table_counts):
    four = "core" in axes
    count, ids = feat_count[None, :], table_ids[None, :]
    if four:
        own, other = gather_pairs(flat_params)
    else:
        own, other = halves_of_pairs(lax.all_gather(flat_params, axes, axis=1, tiled=True))
        turn = jnp.array([0, 2, 1, 3])
        own, other = own[:, turn], other[:, turn]
    turned = jnp.transpose(tokens, (1, 2, 0))
    turned_grad = jnp.transpose(out_grad, (1, 2, 0))
    results = [
        run_kernel(
            four,
            turned[:, :, at : at + ROWS],
            turned_grad[:, :, at : at + ROWS],
            own,
            other,
            count[:, at : at + ROWS],
            ids[:, at : at + ROWS],
            table_counts[None, :],
        )
        for at in range(0, tokens.shape[0], ROWS)
    ]
    out, in_grad, keep, give = results[0]
    if len(results) > 1:
        out = jnp.concatenate([r[0] for r in results], axis=2)
        in_grad = jnp.concatenate([r[1] for r in results], axis=2)
        keep = sum(r[2].astype(F32) for r in results)
        give = sum(r[3].astype(F32) for r in results)
    if four:
        grads = reduce_pairs(keep, give, flat_params.shape[1])
    else:
        flat = pairs_joined(keep.astype(F32), give.astype(F32))
        grads = lax.psum_scatter(flat, axes, scatter_dimension=1, tiled=True)
    return jnp.transpose(out, (2, 0, 1)), jnp.transpose(in_grad, (2, 0, 1)), grads


def solution(mesh):
    axes = mesh.axis_names
    if tuple(mesh.devices.shape) == (8, 4):
        axes = ("z", "x", "y", "core")
        mesh = jax.sharding.Mesh(mesh.devices.reshape(4, 2, 2, 2), axes)
    rows = P(axes, None, None)
    placed = (rows, rows, P(None, axes), P(axes), P(axes), P())
    return jax.shard_map(
        functools.partial(body, axes),
        mesh=mesh,
        in_specs=placed,
        out_specs=(rows, rows, P(None, axes)),
        check_vma=False,
    )
```

```python
import functools
import math

import jax
import jax.numpy as jnp
from jax import lax
from jax.experimental import pallas as pl
from jax.experimental.pallas import tpu as pltpu
from jax.sharding import PartitionSpec as P

D = 192
FF = 256
HEADS = 8
HEAD_DIM = 24
SEQ = 17
LAYERS = 2
PSIZE = 296960
ROWS = 128
SLOTS = 18
LANES = 128
FORWARD_GROUPS = 8
BACKWARD_GROUPS = 16
DEPTH = 8
BAND = 32
GROUP = 8
GROUPS = ROWS // GROUP
GT = SLOTS * GROUP
QL = HEADS * GT
TOKENS = SLOTS * ROWS
CHUNK = 2 * ROWS
CHUNKS = TOKENS // CHUNK
HALVES = (slice(0, ROWS), slice(ROWS, CHUNK))
FLAT = PSIZE // LANES
BLOCK = 80
EPS = 1e-05
VMEM_BYTES = 60 * 1024 * 1024
SCALE = 1.0 / math.sqrt(HEAD_DIM)
F32 = jnp.float32
BF16 = jnp.bfloat16


def dot(a, b, ca, cb):
    return lax.dot_general(a, b, (((ca,), (cb,)), ((), ())), preferred_element_type=F32)


def lane_half(shape):
    return lax.broadcasted_iota(jnp.int32, shape, len(shape) - 1) < 64


def swap(x):
    return pltpu.roll(x, 64, x.ndim - 1)


def low_half(x):
    return jnp.where(lane_half(x.shape), x, 0.0)


def splice(a, b):
    return swap(jnp.where(lane_half(a.shape), b, a))


def after(a, b):
    return jnp.where(lane_half(a.shape), a, swap(b))


def wide(column):
    return jnp.concatenate([column, column], axis=1)


def gather_flat(own, other, place, layer, flat):
    z, core, xy = place
    for chip in range(FLAT // 145):
        turn = z ^ (chip // 4)
        at = (turn & 1) * 2 + turn // 2
        mine = own[xy ^ (chip % 4), at, layer].astype(F32)
        theirs = other[xy ^ (chip % 4), at, layer].astype(F32)
        first = jnp.where(core == 0, mine, theirs)
        second = jnp.where(core == 0, theirs, mine)
        base = 145 * chip
        flat[pl.ds(base, BLOCK), :] = first
        flat[pl.ds(base + 72, BLOCK), :] = second
        flat[pl.ds(base + 72, 1), :] = jnp.where(
            lane_half((1, LANES)), first[72:73], second[0:1]
        )


def unpack(flat, w, tmp):
    def rows(start, count, stride):
        return flat[pl.ds(start, count, stride=stride), :]

    def row(index):
        return flat[pl.ds(index, 1), :]

    def pair_row(a, b):
        return jnp.concatenate([a, b], axis=1)

    vectors = [
        pair_row(row(0), low_half(row(1))),
        pair_row(splice(row(1), row(2)), low_half(swap(row(2)))),
        pair_row(row(1158), low_half(row(1159))),
        pair_row(splice(row(1159), row(1160)), low_half(swap(row(1160)))),
        pair_row(row(1161), low_half(row(1162))),
        pair_row(splice(row(2318), row(2319)), low_half(swap(row(2319)))),
    ]
    index = lax.broadcasted_iota(jnp.int32, (16, 2 * LANES), 0)
    stacked = jnp.zeros((16, 2 * LANES), F32)
    for i, vector in enumerate(vectors):
        stacked = jnp.where(index == i, vector, stacked)
    stacked = stacked.astype(BF16)
    for i in range(6):
        pick = jnp.where(index[:, 0:LANES] == i, 1.0, 0.0).astype(BF16)
        w["cols"][i] = dot(stacked, pick, 0, 0)[0:D]

    e = [rows(3 + j, 96, 9) for j in range(9)]
    even = (e[0], low_half(e[1]), splice(e[1], e[2]), low_half(swap(e[2])), e[3], low_half(e[4]))
    odd = (
        splice(e[4], e[5]),
        low_half(swap(e[5])),
        e[6],
        low_half(e[7]),
        splice(e[7], e[8]),
        low_half(swap(e[8])),
    )
    zero_row = jnp.zeros((1, LANES), F32)
    bias = (
        row(867),
        low_half(row(868)),
        zero_row,
        zero_row,
        splice(row(868), row(869)),
        low_half(swap(row(869))),
    )
    first_row = lax.broadcasted_iota(jnp.int32, (16, LANES), 0) == 0
    for j in range(6):
        tmp[j % 2, pl.ds(0, 96, stride=2), :] = even[j]
        tmp[j % 2, pl.ds(1, 96, stride=2), :] = odd[j]
        w["qkv"][0:D, j * LANES : (j + 1) * LANES] = tmp[j % 2, 0:D, :].astype(BF16)
        w["qkv"][D : D + 16, j * LANES : (j + 1) * LANES] = jnp.where(
            first_row, jnp.broadcast_to(bias[j], (16, LANES)), 0.0
        ).astype(BF16)

    e = [rows(870 + j, 96, 3) for j in range(3)]
    tmp[0, pl.ds(0, 96, stride=2), :] = e[0]
    tmp[1, pl.ds(0, 96, stride=2), :] = low_half(e[1])
    tmp[0, pl.ds(1, 96, stride=2), :] = splice(e[1], e[2])
    tmp[1, pl.ds(1, 96, stride=2), :] = low_half(swap(e[2]))
    w_out = jnp.concatenate([tmp[0, 0:D, :], tmp[1, 0:D, :]], axis=1)
    bias_rows = jnp.where(
        lax.broadcasted_iota(jnp.int32, (64, 2 * LANES), 0) == 0,
        jnp.broadcast_to(vectors[2], (64, 2 * LANES)),
        0.0,
    )
    w_out = jnp.concatenate([w_out, bias_rows], axis=0).astype(BF16)
    w["out_t"][...] = jnp.transpose(w_out)[0:D]

    g = [rows(1162 + j, 192, 4) for j in range(5)]
    tiles = [splice(g[j], g[j + 1]) for j in range(4)]
    gate_up = jnp.concatenate(tiles, axis=1)
    w["gu"][...] = gate_up.astype(BF16)
    bias_row = jnp.concatenate(
        [splice(row(1930 + j), row(1931 + j)) for j in range(4)], axis=1
    )
    bias_rows = jnp.where(
        lax.broadcasted_iota(jnp.int32, (64, 2 * FF), 0) == 0,
        jnp.broadcast_to(bias_row, (64, 2 * FF)),
        0.0,
    )
    w["gu_t"][...] = jnp.transpose(jnp.concatenate([gate_up, bias_rows], axis=0).astype(BF16))[
        :, 0 : D + 16
    ]

    e = [rows(1934 + j, 128, 3) for j in range(4)]
    tmp[0, pl.ds(0, 128, stride=2), :] = splice(e[0], e[1])
    tmp[1, pl.ds(0, 128, stride=2), :] = low_half(swap(e[1]))
    tmp[0, pl.ds(1, 128, stride=2), :] = e[2]
    tmp[1, pl.ds(1, 128, stride=2), :] = low_half(e[3])
    w_down = jnp.concatenate([tmp[0, 0:FF, :], tmp[1, 0:FF, :]], axis=1)
    w["down"][...] = w_down[:, 0:D].astype(BF16)
    w["down_t"][...] = jnp.transpose(w_down.astype(BF16))[0:D]


def row_of(columns):
    turned = jnp.sum(jnp.transpose(columns), axis=0, keepdims=True)
    return turned[:, 0:LANES], jnp.concatenate(
        [turned[:, LANES:D], jnp.zeros((1, LANES - (D - LANES)), F32)], axis=1
    )


def pack(flat, w, acc, sums, tmp):
    def put(start, count, stride, value):
        flat[pl.ds(start, count, stride=stride), :] = value

    def put_row(index, value):
        flat[pl.ds(index, 1), :] = value

    def down(j, start, count, stride):
        return acc["down"][j, pl.ds(start, count, stride=stride), :]

    def through(weight, name):
        total = jnp.zeros((D, LANES), F32)
        for j in range(acc[name].shape[0]):
            part = weight[0:D, j * LANES : (j + 1) * LANES].astype(F32)
            total += part * acc[name][j, D : D + 1, :]
        return row_of(total)

    g1 = row_of(sums[0])
    b1 = through(w["qkv"], "qkv")
    g2 = row_of(sums[1])
    b2 = through(w["gu"], "gu")
    w_out = jnp.transpose(acc["out_t"][...])
    bo = (
        w_out[D : D + 1, 0:LANES],
        jnp.concatenate([w_out[D : D + 1, LANES:], jnp.zeros((1, 64), F32)], axis=1),
    )
    put_row(0, g1[0])
    put_row(1, after(g1[1], b1[0]))
    put_row(2, splice(b1[0], b1[1]))

    even = [acc["qkv"][j, pl.ds(0, 96, stride=2), :] for j in range(6)]
    odd = [acc["qkv"][j, pl.ds(1, 96, stride=2), :] for j in range(6)]
    put(3, 96, 9, even[0])
    put(4, 96, 9, after(even[1], even[2]))
    put(5, 96, 9, splice(even[2], even[3]))
    put(6, 96, 9, even[4])
    put(7, 96, 9, after(even[5], odd[0]))
    put(8, 96, 9, splice(odd[0], odd[1]))
    put(9, 96, 9, odd[2])
    put(10, 96, 9, after(odd[3], odd[4]))
    put(11, 96, 9, splice(odd[4], odd[5]))
    bias = [acc["qkv"][j, D : D + 1, :] for j in range(6)]
    put_row(867, bias[0])
    put_row(868, after(bias[1], bias[4]))
    put_row(869, splice(bias[4], bias[5]))

    tmp[0, 0:D, :] = w_out[0:D, 0:LANES]
    tmp[1, 0:D, 0 : D - LANES] = w_out[0:D, LANES:]
    even = [tmp[j, pl.ds(0, 96, stride=2), :] for j in range(2)]
    odd = [tmp[j, pl.ds(1, 96, stride=2), :] for j in range(2)]
    put(870, 96, 3, even[0])
    put(871, 96, 3, after(even[1], odd[0]))
    put(872, 96, 3, splice(odd[0], odd[1]))
    put_row(1158, bo[0])
    put_row(1159, after(bo[1], g2[0]))
    put_row(1160, splice(g2[0], g2[1]))
    put_row(1161, b2[0])

    gu = [acc["gu"][j, 0 : D + 8, :] for j in range(4)]
    put_row(1162, after(b2[1], gu[0][0:1]))
    put(1166, 192, 4, splice(gu[3][0:192], acc["gu"][0, pl.ds(1, 192), :]))
    for j in range(1, 4):
        joined = splice(gu[j - 1], gu[j])
        put(1162 + j, 192, 4, joined[0:192])
        put_row(1930 + j, joined[192:193])
    put_row(1934, splice(gu[3][192:193], acc["down"][0, 0:1, :]))

    w0e, w1e = down(0, 0, 128, 2), down(1, 0, 128, 2)
    w0o, w1o = down(0, 1, 128, 2), down(1, 1, 128, 2)
    put(1935, 128, 3, splice(w0e, w1e))
    put(1936, 128, 3, w0o)
    put(1937, 128, 3, after(w1o, down(0, 2, 128, 2)))
    put_row(2319, splice(acc["down"][0, FF : FF + 1, :], acc["down"][1, FF : FF + 1, :]))


def scatter_blocks(flat, place, layer, keep, give):
    core = place[1]
    for chip in range(FLAT // 145):
        first = flat[pl.ds(145 * chip, BLOCK), :]
        second = flat[pl.ds(145 * chip + 72, BLOCK), :]
        z = chip // 4
        at = (z & 1) * 2 + z // 2
        keep[chip % 4, at, layer] = jnp.where(core == 0, first, second).astype(BF16)
        give[chip % 4, at, layer] = jnp.where(core == 0, second, first).astype(BF16)


def norm(x, gain, bias):
    centre = x - jnp.sum(x, axis=0, keepdims=True) * (1.0 / D)
    variance = jnp.sum(centre * centre, axis=0, keepdims=True) * (1.0 / D)
    rstd = lax.rsqrt(variance + EPS)
    xhat = centre * rstd
    return xhat, rstd, (xhat * gain + bias).astype(BF16)


def norm_back(grad, xhat, rstd, gain):
    e = gain * grad
    mean_e = jnp.sum(e, axis=0, keepdims=True) * (1.0 / D)
    mean_ex = jnp.sum(e * xhat, axis=0, keepdims=True) * (1.0 / D)
    return rstd * (e - mean_e - xhat * mean_ex)


def fold(x):
    return x[:, 0:LANES] + x[:, LANES:]


def gelu_parts(gate):
    z = gate * (1.0 / math.sqrt(2.0))
    cdf = 0.5 * lax.erf(z) + 0.5
    bell = jnp.exp2(z * z * (-1.0 / math.log(2.0)))
    return cdf, cdf + (z * bell) * (1.0 / math.sqrt(math.pi))


def to_groups(x):
    n = x.shape[-1]
    x = x.reshape(2, GROUPS, GROUP, n)
    return jnp.concatenate([x[0][:, None], x[1][:, None]], axis=1).reshape(
        GROUPS, 2 * GROUP, n
    )


def from_groups(x):
    n = x.shape[-1]
    x = x.reshape(GROUPS, 2, GROUP, n)
    return jnp.concatenate([x[:, 0], x[:, 1]], axis=0).reshape(CHUNK, n)


def group_rows(c):
    return slice(2 * GROUP * c, 2 * GROUP * (c + 1))


def skewed(stages):
    held = {}
    for tick in range(CHUNKS + len(stages) - 1):
        for j, stage in enumerate(stages):
            c = tick - j
            if 0 <= c < CHUNKS:
                held[c] = stage(c, held.get(c))


def view(ref, c, rows=None):
    return ref.at[0 : ref.shape[0] if rows is None else rows, c * CHUNK : (c + 1) * CHUNK]


def project_stages(s, w):
    def project(c, _):
        lows = []
        for half in HALVES:
            xhat, rstd, low = norm(
                view(s["x"], c).at[:, half][...], w["cols"][0], w["cols"][1]
            )
            view(s["xhat1"], c).at[:, half][...] = xhat
            view(s["rstd1"], c).at[:, half][...] = rstd
            lows.append(low)
        view(s["h1"], c, D)[...] = jnp.concatenate(lows, axis=1)
        return dot(view(s["h1"], c)[...], w["qkv"][...], 0, 0)

    def keep(c, qkv):
        place = group_rows(c)
        s["q"][:, place, :] = to_groups(qkv[:, 0:D]).astype(BF16)
        for name, start in (("k", 256), ("v", 512)):
            part = qkv[:, start : start + D].reshape(2, GROUPS, GROUP, D)
            turned = jnp.concatenate(
                [
                    pltpu.roll(part[t], (2 * c + t) % GROUP, 1)[:, None]
                    for t in range(2)
                ],
                axis=1,
            )
            s[name][:, place, :] = turned.reshape(GROUPS, 2 * GROUP, D).astype(BF16)

    return project, keep


def spread(values, masks):
    n = values.shape[1]
    doubled = [
        jnp.concatenate([values[8 * a : 8 * a + 8], values[8 * a : 8 * a + 8]], axis=0).astype(BF16)
        for a in range(3)
    ]
    parts = [doubled[a] * masks[m][:, 0:n] for a in range(2) for m in range(4)]
    parts.append(doubled[2] * masks[4][:, 0:n])
    return jnp.concatenate(parts, axis=0)


def collect(scores, bits):
    n = scores.shape[1]
    bits = [bit[:, 0:n] for bit in bits]
    out = []
    for a in range(2):
        level = [scores[64 * a + 8 * j : 64 * a + 8 * j + 8] for j in range(8)]
        for bit in bits:
            level = [
                jnp.where(bit, level[2 * i + 1], level[2 * i]) for i in range(len(level) // 2)
            ]
        out.append(level[0])
    out.append(scores[128:136])
    return out


def blocks_of(turned, t, halves):
    first = turned[48 * t : 48 * t + 16]
    middle = turned[48 * t + 16 : 48 * t + 32]
    last = turned[48 * t + 32 : 48 * t + 48]
    none = jnp.zeros_like(first)
    return jnp.concatenate(
        [
            jnp.concatenate([first, none], axis=1),
            jnp.concatenate([middle * halves[0], middle * halves[1]], axis=1),
            jnp.concatenate([none, last], axis=1),
        ],
        axis=0,
    )


def padded(block, t):
    parts = [block]
    if t > 0:
        parts.insert(0, jnp.zeros((48 * t, block.shape[1]), BF16))
    if t < 3:
        parts.append(jnp.zeros((48 * (3 - t), block.shape[1]), BF16))
    return jnp.concatenate(parts, axis=0)


def tail_of(rows, heads):
    return jnp.concatenate([rows * heads[h, 0:1, :] for h in range(HEADS)], axis=0)


def heads_joined(tiles, tail, heads, scale=None):
    main = []
    for tile in tiles:
        main += [tile[0:HEAD_DIM, 0:LANES], tile[HEAD_DIM:, LANES:]]
    main = jnp.concatenate(main, axis=0)
    if scale is not None:
        main, tail = main * scale, tail * scale
    main = jnp.transpose(main.astype(BF16))
    tail = tail.astype(BF16)
    last = tail[0:16] * heads[0, 0:1, :]
    for h in range(1, HEADS):
        last += tail[16 * h : 16 * h + 16] * heads[h, 0:1, :]
    return main, last


def softmax(kept, diff, limit):
    n = kept[0].shape[1]
    own = diff[:, 0:n]
    limit = limit[:, 0:n]
    slot = own.astype(F32)
    scale = SCALE / math.log(2.0)
    low = -1e9 / math.log(2.0)
    shown = [
        jnp.where(slot <= limit, kept[0] * scale, low),
        jnp.where(slot + 8.0 <= limit, kept[1] * scale, low),
        jnp.where(own == 0, jnp.where(limit >= 16.0, kept[2] * scale, low), -3e38),
    ]
    top = jnp.max(jnp.maximum(jnp.maximum(shown[0], shown[1]), shown[2]), axis=0, keepdims=True)
    shown = [jnp.exp2(part - top) for part in shown]
    inverse = 1.0 / jnp.sum(shown[0] + shown[1] + shown[2], axis=0, keepdims=True)
    return jnp.concatenate([part * inverse for part in shown], axis=0)


def staged(items, first, second):
    waiting = []
    for item in items:
        waiting.append((item, first(item)))
        if len(waiting) > DEPTH:
            second(*waiting.pop(0))
    for entry in waiting:
        second(*entry)


def batches(size, run):
    if size == GROUPS:
        run(0)
        return

    def step(i, carry):
        run(i * size)
        return carry

    lax.fori_loop(0, GROUPS // size, step, 0)


def forward_attention(s, env):
    diff = env["diff"][...]
    bits = [(diff & (1 << i)) != 0 for i in range(3)]
    halves = [env["halves"][i] for i in range(2)]

    def run(base):
        state = {}

        def load(u):
            g = base + u
            queries, values = s["q"][g], s["v"][g]
            state[u] = {
                "g": g,
                "queries": queries,
                "keys": s["k"][g],
                "turned": jnp.transpose(queries)[:, 0:LANES],
                "values": values,
                "turned_values": jnp.transpose(values),
                "count": env["count"][pl.ds(g, 1), :],
                "tiles": [],
            }

        def scores(item):
            u, t = item
            if t == 0:
                load(u)
            at = state[u]
            if t < 4:
                return dot(at["keys"], padded(blocks_of(at["turned"], t, halves), t), 1, 0)
            return dot(at["keys"], tail_of(at["queries"][LANES:GT], env["heads"]), 1, 1)

        def mix(item, products):
            u, t = item
            at = state[u]
            attention = softmax(collect(products, bits), diff, at["count"])
            s["att"][at["g"], :, t * CHUNK : min((t + 1) * CHUNK, QL)] = attention
            low = spread(attention, env["masks"])
            if t < 4:
                at["tiles"].append(dot(at["turned_values"][48 * t : 48 * t + 48], low, 1, 0))
                return
            tail = dot(low, at["values"], 0, 0)
            main, last = heads_joined(at["tiles"], tail, env["heads"])
            s["mixed"][at["g"], 0:LANES, 0:D] = main
            s["mixed"][at["g"], LANES:GT, 0:D] = last

        staged([(u, t) for u in range(FORWARD_GROUPS) for t in range(5)], scores, mix)

    batches(FORWARD_GROUPS, run)


def rest_stages(s, w, done):
    def attended(c, _):
        mixed = from_groups(s["mixed"][:, group_rows(c), :].astype(F32)).astype(BF16)
        return dot(w["out_t"][...], mixed, 1, 1)

    def normed(c, product):
        lows = []
        for half in HALVES:
            middle = view(s["x"], c).at[:, half][...] + product[:, half]
            view(s["middle"], c).at[:, half][...] = middle
            xhat, rstd, low = norm(middle, w["cols"][3], w["cols"][4])
            view(s["xhat2"], c).at[:, half][...] = xhat
            view(s["rstd2"], c).at[:, half][...] = rstd
            lows.append(low)
        view(s["h2"], c, D)[...] = jnp.concatenate(lows, axis=1)
        return dot(w["gu_t"][...], view(s["h2"], c)[...], 1, 0)

    def gated(c, gate_up):
        acts = []
        for r in range(0, FF, BAND):
            band = pl.ds(r, BAND)
            gate, up = gate_up[r : r + BAND], gate_up[FF + r : FF + r + BAND]
            cdf, slope = gelu_parts(gate)
            gelu = gate * cdf
            view(s["gelu"], c).at[band][...] = gelu
            view(s["slope"], c).at[band][...] = slope * up
            acts.append((gelu * up).astype(BF16))
        act = jnp.concatenate(acts, axis=0)
        view(s["act"], c, FF)[...] = act
        return dot(w["down_t"][...], act, 1, 0)

    def finish(c, product):
        for i, half in enumerate(HALVES):
            value = view(s["middle"], c).at[:, half][...]
            done(c, i, value + (product[:, half] + w["cols"][5]))

    return attended, normed, gated, finish


def add_tiles(ref, value):
    for j in range(ref.shape[0]):
        ref[j] += value[:, j * LANES : (j + 1) * LANES]


def add_narrow(ref, value):
    ref[0] += value[:, 0:LANES]
    ref[1, :, 0 : D - LANES] += value[:, LANES:D]


def rest_back_stages(s, w, acc, sums):
    def down(c, _):
        branch = view(s["g"], c)[...].astype(BF16)
        return dot(view(s["act"], c)[...], branch, 1, 1), dot(w["down"][...], branch, 1, 0)

    def gate_up(c, held):
        grad_down, d_act = held
        add_narrow(acc["down"], grad_down)
        gates, ups = [], []
        for r in range(0, FF, BAND):
            band = pl.ds(r, BAND)
            part = d_act[r : r + BAND]
            gates.append((part * view(s["slope"], c).at[band][...]).astype(BF16))
            ups.append((part * view(s["gelu"], c).at[band][...]).astype(BF16))
        d_gate_up = jnp.concatenate(gates + ups, axis=0)
        return dot(view(s["h2"], c)[...], d_gate_up, 1, 1), dot(w["gu"][...], d_gate_up, 1, 0)

    def normed(c, held):
        grad_gu, d_normed = held
        add_tiles(acc["gu"], grad_gu)
        lows = []
        for half in HALVES:
            xhat = view(s["xhat2"], c).at[:, half][...]
            part = d_normed[:, half]
            sums[1] += part * xhat
            g = view(s["g"], c).at[:, half]
            d_middle = g[...] + norm_back(
                part, xhat, view(s["rstd2"], c).at[:, half][...], w["cols"][3]
            )
            g[...] = d_middle
            lows.append(d_middle.astype(BF16))
        d_attended = jnp.concatenate(lows, axis=1)
        mixed = from_groups(s["mixed"][:, group_rows(c), :].astype(F32)).astype(BF16)
        return dot(d_attended, w["out_t"][:, 0:D], 0, 0), dot(d_attended, mixed, 1, 0)

    def finish(c, held):
        d_mixed, grad_out = held
        s["dqkv"][:, group_rows(c), 0:D] = to_groups(d_mixed).astype(BF16)
        acc["out_t"][...] += grad_out

    return down, gate_up, normed, finish


def backward_attention(s, env):
    diff = env["diff"][...]
    bits = [(diff & (1 << i)) != 0 for i in range(3)]
    halves = [env["halves"][i] for i in range(2)]

    def run(base):
        state = {}

        def load(u):
            g = base + u
            queries, keys, grads = s["q"][g], s["k"][g], s["dqkv"][g, :, 0:D]
            state[u] = {
                "g": g,
                "queries": queries,
                "grads": grads,
                "keys": keys,
                "values": s["v"][g],
                "turned": jnp.transpose(queries)[:, 0:LANES],
                "turned_grads": jnp.transpose(grads)[:, 0:LANES],
                "turned_keys": jnp.transpose(keys),
                "dq": [],
                "dk": [],
                "dv": [],
            }

        def products(item):
            u, t = item
            if t == 0:
                load(u)
            at = state[u]
            if t < 4:
                block = blocks_of(at["turned_grads"], t, halves)
                return block, dot(at["values"], padded(block, t), 1, 0)
            block = tail_of(at["grads"][LANES:GT], env["heads"])
            return block, dot(at["values"], block, 1, 1)

        def back(item, result):
            u, t = item
            at = state[u]
            grad_block, product = result
            attention = s["att"][at["g"], :, t * CHUNK : min((t + 1) * CHUNK, QL)]
            weighted = attention * jnp.concatenate(collect(product, bits), axis=0)
            total = jnp.sum(weighted, axis=0, keepdims=True)
            d_score = spread(weighted - attention * total, env["masks"])
            low = spread(attention, env["masks"])
            if t < 4:
                at["dv"].append(dot(grad_block, low, 1, 1))
                at["dk"].append(dot(blocks_of(at["turned"], t, halves), d_score, 1, 1))
                at["dq"].append(dot(at["turned_keys"][48 * t : 48 * t + 48], d_score, 1, 0))
                return
            d_values = dot(low, grad_block, 1, 0)
            d_keys = dot(d_score, tail_of(at["queries"][LANES:GT], env["heads"]), 1, 0)
            finish(at, d_values, d_keys, dot(d_score, at["keys"], 0, 0))

        def finish(at, d_values, d_keys, tail):
            g = at["g"]
            main, last = heads_joined(at["dq"], tail, env["heads"], SCALE)
            s["dqkv"][g, 0:LANES, 0:D] = main
            s["dqkv"][g, LANES:GT, 0:D] = last
            for parts, own, start, scale in (
                (at["dk"], d_keys, 256, SCALE),
                (at["dv"], d_values, 512, 1.0),
            ):
                value = jnp.transpose(jnp.concatenate(parts, axis=0)) + own
                slots = (value * scale).reshape(SLOTS, GROUP, D)
                turned = [
                    slots[k] if k % GROUP == 0 else pltpu.roll(slots[k], GROUP - k % GROUP, 0)
                    for k in range(SLOTS)
                ]
                s["dqkv"][g, :, start : start + D] = jnp.concatenate(turned, axis=0).astype(BF16)

        staged([(u, t) for u in range(BACKWARD_GROUPS) for t in range(5)], products, back)

    batches(BACKWARD_GROUPS, run)


def project_back_stages(s, w, acc, sums, done):
    def products(c, _):
        d_qkv = from_groups(s["dqkv"][:, group_rows(c), :].astype(F32)).astype(BF16)
        return dot(view(s["h1"], c)[...], d_qkv, 1, 0), dot(w["qkv"][0:D, :], d_qkv, 1, 1)

    def finish(c, held):
        grad_qkv, d_normed = held
        add_tiles(acc["qkv"], grad_qkv)
        for i, half in enumerate(HALVES):
            xhat = view(s["xhat1"], c).at[:, half][...]
            part = d_normed[:, half]
            sums[0] += part * xhat
            back = norm_back(part, xhat, view(s["rstd1"], c).at[:, half][...], w["cols"][0])
            done(c, i, view(s["g"], c).at[:, half][...] + back)

    return products, finish


def per_layer():
    return {
        "xhat1": ((D, TOKENS), F32),
        "rstd1": ((1, TOKENS), F32),
        "h1": ((D + 16, TOKENS), BF16),
        "q": ((GROUPS, GT, D), BF16),
        "k": ((GROUPS, GT, D), BF16),
        "v": ((GROUPS, GT, D), BF16),
        "att": ((GROUPS, 24, QL), F32),
        "mixed": ((GROUPS, GT, 2 * LANES), BF16),
        "xhat2": ((D, TOKENS), F32),
        "rstd2": ((1, TOKENS), F32),
        "h2": ((D + 16, TOKENS), BF16),
        "act": ((FF + 16, TOKENS), BF16),
        "gelu": ((FF, TOKENS), F32),
        "slope": ((FF, TOKENS), F32),
    }


def weights():
    return {
        "cols": ((6, D, LANES), F32),
        "qkv": ((D + 16, 6 * LANES), BF16),
        "out_t": ((D, 2 * LANES), BF16),
        "gu": ((D, 2 * FF), BF16),
        "gu_t": ((2 * FF, D + 16), BF16),
        "down": ((FF, D), BF16),
        "down_t": ((D, FF), BF16),
    }


def accumulators():
    return {
        "qkv": ((6, D + 16, LANES), F32),
        "out_t": ((D, 2 * LANES), F32),
        "gu": ((4, D + 16, LANES), F32),
        "down": ((2, FF + 16, LANES), F32),
        "sums": ((2, D, LANES), F32),
    }


def common():
    full = (SEQ, D, ROWS)
    return {
        "halves": ((2, 16, LANES), BF16),
        "heads": ((HEADS, 16, D), BF16),
        "masks": ((5, 16, CHUNK), BF16),
        "diff": ((GROUP, CHUNK), jnp.int32),
        "count": ((GROUPS, CHUNK), F32),
        "dqkv": ((GROUPS, GT, 6 * LANES), BF16),
        "x": ((D, TOKENS), F32),
        "middle": ((D, TOKENS), F32),
        "g": ((D, TOKENS), F32),
        "flat": ((FLAT + 8, LANES), F32),
        "tmp": ((2, FF, LANES), F32),
        "tokens": (full, BF16),
        "out_grad": (full, BF16),
        "out": ((SLOTS, D, ROWS), F32),
    }


def make_scratch():
    shapes, names = [], []
    for prefix, table in (
        ("common", common()),
        ("acc0", accumulators()),
        ("acc1", accumulators()),
        ("s0", per_layer()),
        ("s1", per_layer()),
        ("w0", weights()),
        ("w1", weights()),
    ):
        for name, (shape, kind) in table.items():
            names.append((prefix, name))
            shapes.append(pltpu.VMEM(shape, kind))
    return names, shapes + [pltpu.SemaphoreType.DMA((6,))]


def init_env(env, count):
    lane = lax.broadcasted_iota(jnp.int32, (GROUP, CHUNK), 1)
    sub = lax.broadcasted_iota(jnp.int32, (GROUP, CHUNK), 0)
    diff = (sub - lane) & (GROUP - 1)
    env["diff"][...] = diff
    for m in range(5):
        first = jnp.where(diff == (2 * m) % 8, 1.0, 0.0)
        second = jnp.where(diff == 2 * m + 1, 1.0, 0.0)
        env["masks"][m] = jnp.concatenate([first, second], axis=0).astype(BF16)
    sub = lax.broadcasted_iota(jnp.int32, (16, LANES), 0)
    env["halves"][0] = jnp.where(sub < 8, 1.0, 0.0).astype(BF16)
    env["halves"][1] = jnp.where(sub < 8, 0.0, 1.0).astype(BF16)
    feature = lax.broadcasted_iota(jnp.int32, (16, D), 1) // HEAD_DIM
    for h in range(HEADS):
        env["heads"][h] = jnp.where(feature == h, 1.0, 0.0).astype(BF16)
    row = lax.broadcasted_iota(jnp.int32, (GROUPS, LANES), 1)
    group = lax.broadcasted_iota(jnp.int32, (GROUPS, LANES), 0)
    mine = jnp.where(row // GROUP == group, jnp.broadcast_to(count, (GROUPS, LANES)), 0.0)
    here = lax.broadcasted_iota(jnp.int32, (LANES, CHUNK), 0)
    there = lax.broadcasted_iota(jnp.int32, (LANES, CHUNK), 1)
    pick = jnp.where(here % GROUP == there % GROUP, 1.0, 0.0).astype(BF16)
    env["count"][...] = dot(mine.astype(BF16), pick, 1, 0)


def ones_below(ref, rows):
    tail = ref.shape[0] - rows
    mark = lax.broadcasted_iota(jnp.int32, (tail, ref.shape[1]), 0) == 0
    ref[rows:, :] = jnp.where(mark, 1.0, 0.0).astype(BF16)


def scales(ids, table_counts):
    counts = table_counts.astype(F32)
    tables = counts.shape[1]
    high = jnp.floor(counts * (1.0 / 32.0))
    table = lax.broadcasted_iota(jnp.int32, (tables, ROWS), 0)
    match = jnp.where(table == ids, 1.0, 0.0).astype(BF16)

    def pick(values):
        return dot(jnp.broadcast_to(values, (8, tables)).astype(BF16), match, 1, 0)[0:1]

    mine = 32.0 * pick(high) + pick(counts - 32.0 * high)
    return jnp.sqrt(jnp.sum(counts, axis=1, keepdims=True) * (1.0 / tables) / mine)


def kernel(names, four, *refs):
    inputs, outputs, scratch, sems = refs[0:7], refs[7:11], refs[11:-1], refs[-1]
    tokens, out_grad, own, other, feat_count, table_ids, table_counts = inputs
    out, in_grad, keep_out, give_out = outputs
    table = {}
    for (prefix, name), ref in zip(names, scratch):
        table.setdefault(prefix, {})[name] = ref
    env = table["common"]
    acc = [table["acc0"], table["acc1"]]
    s, w = [table["s0"], table["s1"]], [table["w0"], table["w1"]]
    sums = [part["sums"] for part in acc]
    place = (0, 0, 0)
    if four:
        xy = 2 * lax.axis_index("x") + lax.axis_index("y")
        place = (lax.axis_index("z"), lax.axis_index("core"), xy)

    copies = [
        pltpu.make_async_copy(source, env[name], sems.at[i])
        for i, (source, name) in enumerate(
            ((tokens, "tokens"), (out_grad, "out_grad"))
        )
    ]
    for copy in copies:
        copy.start()

    count = feat_count[...].astype(F32)
    init_env(env, count)
    pad = jnp.zeros((GROUPS, GT, 2 * LANES - D), BF16)
    for part in range(3):
        env["dqkv"][:, :, 2 * LANES * part + D : 2 * LANES * (part + 1)] = pad
    for layer in range(LAYERS):
        mark = lax.broadcasted_iota(jnp.int32, (GROUPS, GT, 2 * LANES - D), 2) == 0
        s[layer]["mixed"][:, :, D:] = jnp.where(mark, 1.0, 0.0).astype(BF16)
        ones_below(s[layer]["h1"], D)
        ones_below(s[layer]["h2"], D)
        ones_below(s[layer]["act"], FF)
        for ref in acc[layer].values():
            ref[...] = jnp.zeros_like(ref)
    env["x"][:, SEQ * ROWS :] = jnp.zeros((D, ROWS), F32)
    env["g"][:, SEQ * ROWS :] = jnp.zeros((D, ROWS), F32)
    row_scale = scales(table_ids[...], table_counts[...])
    for layer in range(LAYERS):
        gather_flat(own, other, place, layer, env["flat"])
        unpack(env["flat"], w[layer], env["tmp"])
    copies[0].wait()
    copies[1].wait()
    for slot in range(SEQ):
        lanes = slice(slot * ROWS, (slot + 1) * ROWS)
        env["x"][:, lanes] = env["tokens"][slot].astype(F32)
        keep = jnp.where(count >= float(slot), row_scale, 0.0)
        env["g"][:, lanes] = env["out_grad"][slot].astype(F32) * keep

    def put(target):
        def done(c, i, value):
            target[2 * c + i] = value

        return done

    def set_to(target):
        def done(c, i, value):
            view(target, c).at[:, HALVES[i]][...] = value

        return done

    shared = {name: env[name] for name in ("x", "middle", "g", "dqkv")}
    s = [dict(part, **shared) for part in s]

    skewed(project_stages(s[0], w[0]))
    forward_attention(s[0], env)
    attended, normed, gated, finish = rest_stages(s[0], w[0], set_to(env["x"]))
    project, hold = project_stages(s[1], w[1])

    def finish_project(c, held):
        finish(c, held)
        return project(c, None)

    skewed((attended, normed, gated, finish_project, hold))
    forward_attention(s[1], env)
    attended, normed, gated, finish_out = rest_stages(s[1], w[1], put(env["out"]))
    down, gate_up, normed_back, finish_back = rest_back_stages(s[1], w[1], acc[1], sums[1])

    def gated_down(c, held):
        return gated(c, held), down(c, None)

    def finish_gate_up(c, held):
        finish_out(c, held[0])
        return gate_up(c, held[1])

    skewed((attended, normed, gated_down, finish_gate_up, normed_back, finish_back))
    out_copy = pltpu.make_async_copy(env["out"].at[0:SEQ], out, sems.at[4])
    out_copy.start()
    backward_attention(s[1], env)
    products, finish_project_back = project_back_stages(
        s[1], w[1], acc[1], sums[1], set_to(env["g"])
    )
    down, gate_up, normed_back, finish_back = rest_back_stages(s[0], w[0], acc[0], sums[0])

    def finish_down(c, held):
        finish_project_back(c, held)
        return down(c, None)

    skewed((products, finish_down, gate_up, normed_back, finish_back))

    def send(layer):
        pack(env["flat"], w[layer], acc[layer], sums[layer], env["tmp"])
        scatter_blocks(env["flat"], place, layer, keep_out, give_out)

    send(1)
    backward_attention(s[0], env)
    out_copy.wait()
    skewed(project_back_stages(s[0], w[0], acc[0], sums[0], put(env["out"])))
    last = pltpu.make_async_copy(env["out"].at[0:SEQ], in_grad, sems.at[5])
    last.start()
    send(0)
    last.wait()


def run_kernel(four, tokens, out_grad, own, other, count, ids, table_counts):
    names, scratch = make_scratch()
    full = jax.ShapeDtypeStruct((SEQ, D, ROWS), F32)
    blocks = pltpu.VMEM(own.shape, BF16)
    own, other = (pltpu.with_memory_space_constraint(part, pltpu.VMEM) for part in (own, other))

    def body(*refs):
        kernel(names, four, *refs)

    vmem = pl.BlockSpec(memory_space=pltpu.VMEM)
    anywhere = pl.BlockSpec(memory_space=pl.ANY)
    return pl.pallas_call(
        body,
        out_shape=(full, full, blocks, blocks),
        in_specs=[anywhere] * 2 + [vmem] * 5,
        out_specs=[anywhere] * 2 + [vmem] * 2,
        scratch_shapes=scratch,
        compiler_params=pltpu.CompilerParams(vmem_limit_bytes=VMEM_BYTES),
    )(tokens, out_grad, own, other, count, ids, table_counts)


def halves_of_pairs(flat):
    rows = jnp.pad(flat.reshape(LAYERS, FLAT, LANES), ((0, 0), (0, BLOCK), (0, 0)))

    def blocks(skip):
        parts = [rows[:, 145 * chip + skip : 145 * chip + skip + BLOCK] for chip in range(16)]
        return jnp.stack([jnp.stack(parts[at::4]) for at in range(4)])

    return blocks(0), blocks(72)


def pairs_joined(even, odd):
    joined = []
    for chip in range(16):
        at = (chip // 4 % 2) * 2 + chip // 8
        first, second = even[chip % 4, at], odd[chip % 4, at]
        seam = jnp.concatenate([first[:, 72:73, 0:64], second[:, 0:1, 64:]], axis=2)
        joined += [first[:, 0:72], seam, second[:, 1:73]]
    return jnp.concatenate(joined, axis=1).reshape(LAYERS, PSIZE)


def swap_along(x, axis, bit):
    pairs = [(i, i ^ bit) for i in range(lax.axis_size(axis))]
    return lax.ppermute(x, axis, pairs)


def gather_pairs(flat_params):
    size = flat_params.shape[1]
    room = BLOCK * LANES - size
    part = jnp.where(
        lax.axis_index("core") == 0,
        jnp.pad(flat_params, ((0, 0), (0, room))),
        jnp.pad(flat_params, ((0, 0), (64, room - 64))),
    ).reshape(1, LAYERS, BLOCK, LANES)
    for bit in (2, 1):
        part = jnp.concatenate([part, swap_along(part, "z", bit)], axis=0)
    parts = [part]
    for away in (1, 2, 3):
        pairs = [(i, i ^ away) for i in range(4)]
        parts.append(lax.ppermute(part, ("x", "y"), pairs))
    others = [swap_along(part, "core", 1) for part in parts]
    return jnp.stack(parts), jnp.stack(others)


def reduce_pairs(keep, give, size):
    me = 2 * lax.axis_index("x") + lax.axis_index("y")
    part = 0.0
    for away in (3, 2, 1, 0):
        theirs = lax.dynamic_index_in_dim(give, me ^ away, 0, False)
        mine = lax.dynamic_index_in_dim(keep, me ^ away, 0, False)
        both = mine.astype(F32) + swap_along(theirs, "core", 1).astype(F32)
        if away:
            pairs = [(i, i ^ away) for i in range(4)]
            both = lax.ppermute(both.astype(BF16), ("x", "y"), pairs).astype(F32)
        part += both
    z = lax.axis_index("z")
    for bit, count in ((1, 2), (2, 1)):
        high = (z // bit) % 2
        stay = lax.dynamic_slice_in_dim(part, high * count, count, 0)
        go = lax.dynamic_slice_in_dim(part, (1 - high) * count, count, 0).astype(BF16)
        part = stay + swap_along(go, "z", bit).astype(F32)
    total = part.reshape(LAYERS, BLOCK * LANES)
    return jnp.where(
        lax.axis_index("core") == 0, total[:, 0:size], total[:, 64 : 64 + size]
    )


def body(axes, tokens, out_grad, flat_params, feat_count, table_ids, table_counts):
    four = "core" in axes
    count, ids = feat_count[None, :], table_ids[None, :]
    if four:
        own, other = gather_pairs(flat_params)
    else:
        own, other = halves_of_pairs(lax.all_gather(flat_params, axes, axis=1, tiled=True))
        turn = jnp.array([0, 2, 1, 3])
        own, other = own[:, turn], other[:, turn]
    turned = jnp.transpose(tokens, (1, 2, 0))
    turned_grad = jnp.transpose(out_grad, (1, 2, 0))
    results = [
        run_kernel(
            four,
            turned[:, :, at : at + ROWS],
            turned_grad[:, :, at : at + ROWS],
            own,
            other,
            count[:, at : at + ROWS],
            ids[:, at : at + ROWS],
            table_counts[None, :],
        )
        for at in range(0, tokens.shape[0], ROWS)
    ]
    out, in_grad, keep, give = results[0]
    if len(results) > 1:
        out = jnp.concatenate([r[0] for r in results], axis=2)
        in_grad = jnp.concatenate([r[1] for r in results], axis=2)
        keep = sum(r[2].astype(F32) for r in results)
        give = sum(r[3].astype(F32) for r in results)
    if four:
        grads = reduce_pairs(keep, give, flat_params.shape[1])
    else:
        flat = pairs_joined(keep.astype(F32), give.astype(F32))
        grads = lax.psum_scatter(flat, axes, scatter_dimension=1, tiled=True)
    return jnp.transpose(out, (2, 0, 1)), jnp.transpose(in_grad, (2, 0, 1)), grads


def solution(mesh):
    axes = mesh.axis_names
    if tuple(mesh.devices.shape) == (8, 4):
        axes = ("z", "x", "y", "core")
        mesh = jax.sharding.Mesh(mesh.devices.reshape(4, 2, 2, 2), axes)
    rows = P(axes, None, None)
    placed = (rows, rows, P(None, axes), P(axes), P(axes), P())
    return jax.shard_map(
        functools.partial(body, axes),
        mesh=mesh,
        in_specs=placed,
        out_specs=(rows, rows, P(None, axes)),
        check_vma=False,
    )
```
